32 devices in a mesh: groups: 2 (over x), expert: 8 (over z, y), dp: 2 (over core).
Axes of the slice: x: 2, y: 2, z: 4, core: 2. Of those that a mesh axis runs over, the one named last changes fastest.
Arguments:
- tokens: bfloat16 [4096, 768], P(('groups', 'expert', 'dp')), parts along dimension 0, may hold values from -6 to 6
- teacher: bfloat16 [4096, 768], P(('groups', 'expert', 'dp')), parts along dimension 0, may hold values from -6 to 6
- routes: int32 [4096, 2], P(('groups', 'expert', 'dp')), parts along dimension 0, may hold values from 0 to 7, all different within a row; in each aligned block of 128 rows (0 to 127, 128 to 255, ...) at most 64 rows name the same one
- gate_weights: float32 [4096, 2], P(('groups', 'expert', 'dp')), parts along dimension 0, may hold values from 0.2 to 1
- weights: bfloat16 [8, 2048, 3, 768], P('expert', 'dp'), may hold values from -0.21875 to 0.21875
Outputs:
- student: bfloat16 [4096, 768], P(('groups', 'expert', 'dp')), parts along dimension 0
- d_tokens: bfloat16 [4096, 768], P(('groups', 'expert', 'dp')), parts along dimension 0
- d_gates: float32 [4096, 2], P(('groups', 'expert', 'dp')), parts along dimension 0
- weight_grads: bfloat16 [16, 2048, 3, 768], P(('groups', 'expert'), 'dp'), parts along dimension 0
The draws below stay inside these ranges and needn't reach their ends.
There are 2 independent parts, one for each index of `groups`. The reference program is written for one: setup_inputs(seed, part) draws one part's arguments, and reference() takes and returns one part's arrays. A program takes and returns all parts, laid end to end along the dimension named above; an argument that names none is the same for every part. Nothing has to cross between parts.
Inputs may be any that keep to these rules, and one draw needn't show every extreme that they name: `routes`: the two experts of a token differ. In the 128 rows of one device no expert is named more than 64 times, and in every draw some device's rows name some expert exactly 64 times.
All inputs are finite; a program needn't handle non-finite values.
Results may differ from the reference program's by a relative error of at most 0.0063.
Values may be sent and summed in bfloat16 or wider, within the bound.
No kernel may reach another device: no remote copies, remote signals or barrier semaphores. Data moves between devices by JAX's collectives and lax.ppermute only.
A program may use at most 128 MiB of HBM per device.

```python
import math
import jax
import jax.numpy as jnp
import numpy as np
from jax import lax

D = 768
FF = 2048
TOK_DEV = 128
EXPERTS = 8
CAP = 64
TOKENS = 2048
N_EXPERT = 8
N_DP = 2


def levels(rng, extent, shards, smallest, top_value):
    factor_of = 1.0
    for position, blocks in shards:
        draws = jax.random.uniform(jax.random.fold_in(jax.random.fold_in(rng, 6), position), (blocks,), jnp.float32, smallest / len(shards), top_value / len(shards))
        factor_of = factor_of * jnp.repeat(jnp.exp(draws), extent[position] // blocks).reshape((-1,) + (1,) * (len(extent) - 1 - position))
    return factor_of


def assign_block(own_key, own, number, rows, number_of, top, most, lean):
    order = jax.random.permutation(own_key, number_of)
    crowded, common = load_shares(number_of, rows * top, most, lean, True), load_shares(number_of, rows * top, most, lean, False)
    places = jnp.arange(number_of)

    def named(sizes, turn):
        used = int((sizes > 0).sum())
        fixed = max(1, used // 4)
        moved = fixed + (places - fixed + turn * (used - fixed)) % max(1, number_of - fixed)
        return jnp.zeros((number_of,), jnp.int32).at[order[jnp.where(places < fixed, places, moved)]].set(jnp.asarray(sizes, jnp.int32))

    sizes = jnp.where(number % 4 == 0, named(crowded, number // 4), named(common, number - number // 4 - 1))
    mixed = jax.random.permutation(jax.random.fold_in(own, 3), number_of)
    giver, receiver = mixed[0:number_of // 2 * 2:2], mixed[1:number_of // 2 * 2:2]
    room = jnp.minimum(sizes[giver] - 1, most - sizes[receiver]) // 2
    room = jnp.where((giver == order[0]) | (receiver == order[0]) | (sizes[receiver] == 0), 0, jnp.maximum(room, 0))
    moved = jax.random.randint(jax.random.fold_in(own, 4), (number_of // 2,), 0, 1 << 20) % (room + 1)
    sizes = sizes.at[giver].add(-moved).at[receiver].add(moved)
    items = jnp.searchsorted(jnp.cumsum(sizes), jnp.arange(rows * top), side="right").astype(jnp.int32)
    grid = items.reshape(top, rows).T
    grid = grid[jax.random.permutation(jax.random.fold_in(own, 1), rows)]
    turn = jax.random.randint(jax.random.fold_in(own, 2), (rows, 1), 0, top)
    return jnp.take_along_axis(grid, (jnp.arange(top)[None, :] + turn) % top, axis=1)


def load_shares(number_of, total, limit, lean, full):
    portions = [(1 << 20) // math.isqrt(grade ** lean) + 1 for grade in range(1, number_of + 1)]
    largest = limit if full else min(limit, max(-(-total // number_of), total * portions[0] // sum(portions)))
    least = 1 if total - largest >= number_of - 1 else 0
    holding, rest = [largest] + [least] * (number_of - 1), total - largest - least * (number_of - 1)
    while rest > 0:
        movable = [i for i in range(1, number_of) if holding[i] < largest] or [i for i in range(1, number_of) if holding[i] < limit]
        whole, budget = sum([portions[i] for i in movable]), rest
        for i in movable:
            addition = min(limit - holding[i], max(1, budget * portions[i] // whole), rest)
            holding[i] = holding[i] + addition
            rest = rest - addition
    return np.array(holding)


def scatter_about(own_key, dims, deviation, most, cuts=(), held_as=jnp.bfloat16):
    drawn = deviation * jax.random.normal(own_key, dims, jnp.float32)
    if cuts:
        drawn = drawn * levels(own_key, dims, cuts, -0.22, 0.18)
    return jnp.clip(drawn, -most, most).astype(held_as)


def setup_inputs(seed: int = 0, part: int = 0) -> dict:
    streams_of = jax.random.split(jax.random.key(seed), 6)
    own_keys = jax.random.split(jax.random.fold_in(streams_of[5], part), 6)
    tokens = scatter_about(own_keys[0], (TOKENS, D), 1.0, 6.0, ((0, 16),))
    teacher = scatter_about(own_keys[1], (TOKENS, D), 1.0, 6.0, ((0, 16),))
    routes_keys = jax.random.split(jax.random.fold_in(own_keys[2], 1), TOKENS // TOK_DEV)
    routes_turns = jax.random.permutation(jax.random.fold_in(own_keys[2], 3), TOKENS // TOK_DEV)
    routes = jax.vmap(lambda own, number: assign_block(jax.random.fold_in(own_keys[2], 2), own, number, TOK_DEV, EXPERTS, 2, CAP, 2))(routes_keys, routes_turns).reshape((TOKENS, 2))
    gate_weights = jnp.clip(0.2 + 0.8 * jax.random.uniform(own_keys[3], (TOKENS, 2), jnp.float32) ** levels(own_keys[3], (TOKENS, 2), ((0, 16),), -0.2, 0.2), 0.2, 1.0)
    weights = scatter_about(streams_of[4], (EXPERTS, FF, 3, D), D ** -0.5, 0.21875, ((0, 8), (1, 2)))
    return {"tokens": tokens, "teacher": teacher, "routes": routes, "gate_weights": gate_weights, "weights": weights}


CONTRACT_LAST = (((1,), (1,)), ((), ()))
CONTRACT_FIRST = (((0,), (0,)), ((), ()))


def gate_terms(pre_gate, pre_up, d_hidden):
    logistic = jax.nn.sigmoid(pre_gate)
    d_gate = (d_hidden * pre_up * logistic * (1.0 + pre_gate * (1.0 - logistic))).astype(jnp.bfloat16)
    d_up = (d_hidden * pre_gate * logistic).astype(jnp.bfloat16)
    return d_gate, d_up


def reference(tokens, teacher, routes, gate_weights, weights):
    width_d = tokens.shape[1]
    flat_routes = routes.reshape(-1).astype(jnp.int32)
    routed_total = flat_routes.shape[0]
    max_rows = N_EXPERT * N_DP * CAP
    expert_ids = jnp.arange(EXPERTS, dtype=jnp.int32)
    sorted_ids = jnp.argsort(flat_routes, stable=True).astype(jnp.int32)
    padded_ids = jnp.concatenate([sorted_ids, jnp.zeros((max_rows,), jnp.int32)])
    totals = jnp.sum((flat_routes[:, None] == expert_ids[None, :]).astype(jnp.int32), axis=0).astype(jnp.int32)
    starts = (jnp.cumsum(totals) - totals).astype(jnp.int32)
    route_inputs = jnp.repeat(tokens, 2, axis=0)

    def select(expert_id):
        picked = lax.dynamic_slice_in_dim(padded_ids, starts[expert_id], max_rows)
        filled = jnp.arange(max_rows, dtype=jnp.int32) < totals[expert_id]
        return picked, filled

    def forward(expert_id):
        picked, filled = select(expert_id)
        inputs = jnp.where(filled[:, None], route_inputs[picked], jnp.zeros_like(route_inputs[:1]))
        matrices = weights[expert_id]
        pre_gate = lax.dot_general(inputs, matrices[:, 0, :], CONTRACT_LAST, preferred_element_type=jnp.float32)
        pre_up = lax.dot_general(inputs, matrices[:, 1, :], CONTRACT_LAST, preferred_element_type=jnp.float32)
        hidden = (pre_gate * jax.nn.sigmoid(pre_gate) * pre_up).astype(jnp.bfloat16)
        expert_out = jnp.dot(hidden, matrices[:, 2, :], preferred_element_type=jnp.float32).astype(jnp.bfloat16)
        return expert_out, pre_gate, pre_up

    expert_outs, pre_gates, pre_ups = lax.map(forward, expert_ids)

    def placement(expert_id):
        picked, filled = select(expert_id)
        return jnp.where(filled, picked, routed_total).astype(jnp.int32)

    targets = jax.vmap(placement)(expert_ids).reshape(-1)
    route_out = jnp.zeros((routed_total, width_d), jnp.bfloat16).at[targets].set(expert_outs.reshape(-1, width_d), mode="drop")
    routed = route_out.reshape(-1, 2, width_d).astype(jnp.float32)
    student_sum = jnp.sum(gate_weights[:, :, None] * routed, axis=1)
    difference = student_sum - teacher.astype(jnp.float32)
    d_gates = jnp.sum(difference[:, None, :] * routed, axis=2)
    route_grad = (gate_weights[:, :, None] * difference[:, None, :]).astype(jnp.bfloat16).reshape(routed_total, width_d)

    def backward(inputs_tuple):
        expert_id, pre_gate, pre_up = inputs_tuple
        picked, filled = select(expert_id)
        inputs = jnp.where(filled[:, None], route_inputs[picked], jnp.zeros_like(route_inputs[:1]))
        grad_rows = jnp.where(filled[:, None], route_grad[picked], jnp.zeros_like(route_grad[:1]))
        matrices = weights[expert_id]
        hidden = (pre_gate * jax.nn.sigmoid(pre_gate) * pre_up).astype(jnp.bfloat16)
        d_hidden = lax.dot_general(grad_rows, matrices[:, 2, :], CONTRACT_LAST, preferred_element_type=jnp.float32)
        d_gate, d_up = gate_terms(pre_gate, pre_up, d_hidden)
        row_grads = (jnp.dot(d_gate, matrices[:, 0, :], preferred_element_type=jnp.float32)
                     + jnp.dot(d_up, matrices[:, 1, :], preferred_element_type=jnp.float32)).astype(jnp.bfloat16)
        grad_gate = lax.dot_general(d_gate, inputs, CONTRACT_FIRST, preferred_element_type=jnp.float32)
        grad_up = lax.dot_general(d_up, inputs, CONTRACT_FIRST, preferred_element_type=jnp.float32)
        grad_down = lax.dot_general(hidden, grad_rows, CONTRACT_FIRST, preferred_element_type=jnp.float32)
        return row_grads, jnp.stack([grad_gate, grad_up, grad_down], axis=1).astype(jnp.bfloat16)

    row_grads, weight_grads = lax.map(backward, (expert_ids, pre_gates, pre_ups))
    route_rows = jnp.zeros((routed_total, width_d), jnp.bfloat16).at[targets].set(row_grads.reshape(-1, width_d), mode="drop")
    d_tokens = jnp.sum(route_rows.reshape(-1, 2, width_d).astype(jnp.float32), axis=1).astype(jnp.bfloat16)
    return (student_sum.astype(jnp.bfloat16), d_tokens, d_gates, weight_grads)
```

```python
import functools

import jax
import jax.numpy as jnp
from jax import lax
from jax.experimental import pallas as pl
from jax.experimental.pallas import tpu as pltpu
from jax.sharding import PartitionSpec as P

LAST = (((1,), (1,)), ((), ()))
FIRST = (((0,), (0,)), ((), ()))
MIB = 1024 * 1024
F32 = jnp.float32
BF16 = jnp.bfloat16


def dot(a, b, dims=(((1,), (0,)), ((), ()))):
    return lax.dot_general(a, b, dims, preferred_element_type=F32)


def vmem(n):
    return [pl.BlockSpec(memory_space=pltpu.VMEM)] * n


def smem():
    return pl.BlockSpec(memory_space=pltpu.SMEM)


def slot_masks(me, routes, experts, capacity):
    tok = routes.shape[1]
    expert_of = lax.broadcasted_iota(jnp.int32, (experts, tok), 0) ^ me
    first, second = routes[0:1, :] == expert_of, routes[1:2, :] == expert_of
    chosen = jnp.where(first | second, 1.0, 0.0).astype(BF16)
    before = lax.broadcasted_iota(jnp.int32, (tok, tok), 0) < lax.broadcasted_iota(
        jnp.int32, (tok, tok), 1
    )
    rank = dot(chosen, jnp.where(before, 1.0, 0.0).astype(BF16))
    rank0 = jnp.where(first, rank, -1.0)
    rank1 = jnp.where(second, rank, -1.0)
    place = lax.broadcasted_iota(jnp.int32, (capacity, tok), 0).astype(F32)

    def expand(ranks):
        return jnp.concatenate(
            [
                jnp.where(ranks[s : s + 1, :] == place, 1.0, 0.0).astype(BF16)
                for s in range(experts)
            ],
            axis=0,
        )

    return expand(rank0), expand(rank1)


def pack_kernel(experts, capacity, me_ref, routes_ref, tokens_ref, *out_refs):
    m0, m1 = slot_masks(me_ref[0], routes_ref[...], experts, capacity)
    rows = dot(m0 + m1, tokens_ref[...]).astype(BF16)
    for s in range(experts):
        out_refs[s][...] = rows[s * capacity : (s + 1) * capacity]


def forward_kernel(experts, capacity, *refs):
    ins, refs = refs[:experts], refs[experts:]
    own_ref, other_ref = refs[:2]
    outs, refs = refs[2 : 2 + experts], refs[2 + experts :]
    x_ref, hid_ref, fa_ref, fb_ref, acc_ref = refs
    step = pl.program_id(0)

    @pl.when(step == 0)
    def _():
        for s in range(experts):
            x_ref[s * capacity : (s + 1) * capacity, :] = ins[s][...]
        acc_ref[...] = jnp.zeros_like(acc_ref)

    x = x_ref[...]
    for half, w_ref in enumerate((own_ref, other_ref)):
        gate = dot(x, w_ref[0], LAST)
        up = dot(x, w_ref[1], LAST)
        sig = jax.nn.sigmoid(gate)
        silu = gate * sig
        hid = (silu * up).astype(BF16)
        hid_ref[half] = hid
        fa_ref[half] = (up * sig * (1.0 + gate * (1.0 - sig))).astype(BF16)
        fb_ref[half] = silu.astype(BF16)
        acc_ref[...] += dot(hid, w_ref[2])

    @pl.when(step == pl.num_programs(0) - 1)
    def _():
        for s in range(experts):
            outs[s][...] = acc_ref[s * capacity : (s + 1) * capacity, :].astype(BF16)


def combine_kernel(experts, capacity, me_ref, routes_ref, gates_ref, teacher_ref, *refs):
    ins, refs = refs[:experts], refs[experts:]
    student_ref, d_gates_ref = refs[:2]
    outs = refs[2:]
    m0, m1 = slot_masks(me_ref[0], routes_ref[...], experts, capacity)
    got = jnp.concatenate([r[...] for r in ins], axis=0)
    o0, o1 = dot(m0, got, FIRST), dot(m1, got, FIRST)
    g0, g1 = gates_ref[:, 0:1], gates_ref[:, 1:2]
    total = g0 * o0 + g1 * o1
    student_ref[...] = total.astype(BF16)
    diff = total - teacher_ref[...].astype(F32)
    d_gates_ref[...] = jnp.concatenate(
        [
            jnp.sum(diff * o0, axis=1, keepdims=True),
            jnp.sum(diff * o1, axis=1, keepdims=True),
        ],
        axis=1,
    )
    grads = jnp.concatenate([(g0 * diff).astype(BF16), (g1 * diff).astype(BF16)], axis=0)
    rows = dot(jnp.concatenate([m0, m1], axis=1), grads).astype(BF16)
    for s in range(experts):
        outs[s][...] = rows[s * capacity : (s + 1) * capacity]


def backward_kernel(experts, capacity, *refs):
    ins, refs = refs[:experts], refs[experts:]
    own_ref, other_ref, fa_ref, fb_ref = refs[:4]
    outs, refs = refs[4 : 4 + experts], refs[4 + experts :]
    rg_ref, dg_ref, du_ref, acc_ref = refs
    step = pl.program_id(0)

    @pl.when(step == 0)
    def _():
        for s in range(experts):
            rg_ref[s * capacity : (s + 1) * capacity, :] = ins[s][...]
        acc_ref[...] = jnp.zeros_like(acc_ref)

    rg = rg_ref[...]
    for half, w_ref in enumerate((own_ref, other_ref)):
        dh = dot(rg, w_ref[2], LAST)
        dg = (dh * fa_ref[half].astype(F32)).astype(BF16)
        du = (dh * fb_ref[half].astype(F32)).astype(BF16)
        dg_ref[half] = dg
        du_ref[half] = du
        acc_ref[...] += dot(dg, w_ref[0]) + dot(du, w_ref[1])

    @pl.when(step == pl.num_programs(0) - 1)
    def _():
        for s in range(experts):
            outs[s][...] = acc_ref[s * capacity : (s + 1) * capacity, :].astype(BF16)


def weight_kernel(x_ref, rg_ref, dg_ref, du_ref, hid_ref, *refs):
    out_ref = refs[-1]
    x, rg = x_ref[...], rg_ref[...]
    terms = (dot(dg_ref[0], x, FIRST), dot(du_ref[0], x, FIRST), dot(hid_ref[0], rg, FIRST))
    for m, term in enumerate(terms):
        if len(refs) == 2:
            term = term + refs[0][m].astype(F32)
        out_ref[m] = term.astype(BF16)


def final_kernel(experts, capacity, me_ref, routes_ref, *refs):
    ins, out_ref = refs[:experts], refs[experts]
    m0, m1 = slot_masks(me_ref[0], routes_ref[...], experts, capacity)
    got = jnp.concatenate([r[...] for r in ins], axis=0)
    out_ref[...] = dot(m0 + m1, got, FIRST).astype(BF16)


def exchange(rows):
    experts = len(rows)
    got = [rows[0]] + [None] * (experts - 1)
    for s in range(experts - 1, 0, -1):
        got[s] = lax.ppermute(rows[s], "expert", [(i, i ^ s) for i in range(experts)])
    return got


def local(tokens, teacher, routes, gate_weights, weights):
    tok, width = tokens.shape
    experts = lax.axis_size("expert")
    capacity = 4 * tok // experts
    slots = experts * capacity
    units = weights.shape[1]
    chunk = min(256, units)
    steps = units // chunk
    me = lax.axis_index("expert").reshape(1)
    routes_t = routes.T
    rows_type = [jax.ShapeDtypeStruct((capacity, width), BF16)] * experts
    whole = lambda shape: pl.BlockSpec(shape, lambda i: (0,) * len(shape))
    rows_specs = [whole((capacity, width))] * experts
    w_spec = pl.BlockSpec((3, chunk, width), lambda i: (0, i, 0))
    act_spec = pl.BlockSpec((2, slots, chunk), lambda i: (0, 0, i))
    act_type = jax.ShapeDtypeStruct((2, slots, units), BF16)
    flat_type = jax.ShapeDtypeStruct((slots, width), BF16)
    matmul = 2 * slots * width * units

    own = weights[0].transpose(1, 0, 2)
    other = lax.ppermute(own, "dp", [(0, 1), (1, 0)])

    small = dict(compiler_params=pltpu.CompilerParams(vmem_limit_bytes=24 * MIB))
    big = dict(
        compiler_params=pltpu.CompilerParams(
            vmem_limit_bytes=32 * MIB, dimension_semantics=("arbitrary",)
        )
    )

    packed = pl.pallas_call(
        functools.partial(pack_kernel, experts, capacity),
        in_specs=[smem()] + vmem(2),
        out_specs=vmem(experts),
        out_shape=rows_type,
        name="pack_tokens",
        **small,
    )(me, routes_t, tokens)

    arrived = exchange(packed)

    res = pl.pallas_call(
        functools.partial(forward_kernel, experts, capacity),
        grid=(steps,),
        in_specs=rows_specs + [w_spec] * 2,
        out_specs=rows_specs + [whole((slots, width))] + [act_spec] * 3,
        out_shape=rows_type + [flat_type] + [act_type] * 3,
        scratch_shapes=[pltpu.VMEM((slots, width), F32)],
        cost_estimate=pl.CostEstimate(
            flops=6 * matmul, bytes_accessed=20 * MIB, transcendentals=2 * slots * units
        ),
        name="expert_forward",
        **big,
    )(*arrived, own, other)
    expert_out, (x, hid, fa, fb) = res[:experts], res[experts:]

    returned = exchange(expert_out)

    res = pl.pallas_call(
        functools.partial(combine_kernel, experts, capacity),
        in_specs=[smem()] + vmem(3 + experts),
        out_specs=vmem(2 + experts),
        out_shape=[
            jax.ShapeDtypeStruct((tok, width), BF16),
            jax.ShapeDtypeStruct((tok, 2), F32),
        ]
        + rows_type,
        name="combine_routes",
        **small,
    )(me, routes_t, gate_weights, teacher, *returned)
    student, d_gates, grad_rows = res[0], res[1], res[2:]

    grad_arrived = exchange(grad_rows)

    res = pl.pallas_call(
        functools.partial(backward_kernel, experts, capacity),
        grid=(steps,),
        in_specs=rows_specs + [w_spec] * 2 + [act_spec] * 2,
        out_specs=rows_specs + [whole((slots, width))] + [act_spec] * 2,
        out_shape=rows_type + [flat_type] + [act_type] * 2,
        scratch_shapes=[pltpu.VMEM((slots, width), F32)],
        cost_estimate=pl.CostEstimate(
            flops=6 * matmul, bytes_accessed=20 * MIB, transcendentals=0
        ),
        name="expert_backward",
        **big,
    )(*grad_arrived, own, other, fa, fb)
    row_grads, (rg, dg, du) = res[:experts], res[experts:]

    back = exchange(row_grads)

    def weight_terms(half, *received):
        half_spec = pl.BlockSpec((1, slots, chunk), lambda i: (half, 0, i))
        return pl.pallas_call(
            weight_kernel,
            grid=(steps,),
            in_specs=[whole((slots, width))] * 2 + [half_spec] * 3 + [w_spec] * len(received),
            out_specs=w_spec,
            out_shape=jax.ShapeDtypeStruct((3, units, width), BF16),
            cost_estimate=pl.CostEstimate(
                flops=3 * matmul, bytes_accessed=10 * MIB, transcendentals=0
            ),
            name="weight_terms",
            **big,
        )(x, rg, dg, du, hid, *received)

    sent = weight_terms(1)
    received = lax.ppermute(sent, "dp", [(0, 1), (1, 0)])
    weight_grads = weight_terms(0, received)

    d_tokens = pl.pallas_call(
        functools.partial(final_kernel, experts, capacity),
        in_specs=[smem()] + vmem(1 + experts),
        out_specs=vmem(1)[0],
        out_shape=jax.ShapeDtypeStruct((tok, width), BF16),
        name="combine_gradients",
        **small,
    )(me, routes_t, *back)

    return (student, d_tokens, d_gates, weight_grads.transpose(1, 0, 2)[None])


def solution(mesh):
    rows = P(("groups", "expert", "dp"), None)
    return jax.shard_map(
        local,
        mesh=mesh,
        in_specs=(rows, rows, rows, rows, P("expert", "dp", None, None)),
        out_specs=(rows, rows, rows, P(("groups", "expert"), "dp", None, None)),
        check_vma=False,
    )
```

```python
import functools

import jax
import jax.numpy as jnp
from jax import lax
from jax.experimental import pallas as pl
from jax.experimental.pallas import tpu as pltpu
from jax.sharding import PartitionSpec as P

PLAIN = (((1,), (0,)), ((), ()))
LAST = (((1,), (1,)), ((), ()))
FIRST = (((0,), (0,)), ((), ()))
MIB = 1024 * 1024
F32 = jnp.float32
BF16 = jnp.bfloat16


def dot(a, b, dims=PLAIN):
    return lax.dot_general(a, b, dims, preferred_element_type=F32)


def slot_masks(base, routes, experts, capacity):
    tok = routes.shape[1]
    expert_of = (lax.broadcasted_iota(jnp.int32, (experts, tok), 0) + base).astype(F32)
    first, second = routes[0:1, :] == expert_of, routes[1:2, :] == expert_of
    chosen = jnp.where(first | second, 1.0, 0.0).astype(BF16)
    before = lax.broadcasted_iota(jnp.int32, (tok, tok), 0) < lax.broadcasted_iota(
        jnp.int32, (tok, tok), 1
    )
    rank = dot(chosen, jnp.where(before, 1.0, 0.0).astype(BF16))
    rank0 = jnp.where(first, rank, -1.0)
    rank1 = jnp.where(second, rank, -1.0)
    place = lax.broadcasted_iota(jnp.int32, (capacity, tok), 0).astype(F32)

    def expand(ranks):
        return jnp.concatenate(
            [
                jnp.where(ranks[s : s + 1, :] == place, 1.0, 0.0).astype(BF16)
                for s in range(experts)
            ],
            axis=0,
        )

    return expand(rank0), expand(rank1)


def put_blocks(ref, rows):
    experts, capacity = ref.shape[:2]
    for s in range(experts):
        ref[s] = rows[s * capacity : (s + 1) * capacity].astype(ref.dtype)


def get_blocks(ref):
    return jnp.concatenate([ref[s] for s in range(ref.shape[0])], axis=0)


def gate_columns(meta):
    columns = meta.T
    return columns[:, 2:3], columns[:, 3:4]


def pack_kernel(base_ref, meta_ref, tokens_ref, rows_ref):
    m0, m1 = slot_masks(base_ref[0], meta_ref[0:2, :], *rows_ref.shape[:2])
    put_blocks(rows_ref, dot(m0 + m1, tokens_ref[...]))


def forward_kernel(chunk, w_ref, xa_ref, xb_ref, pa_ref, pb_ref, hid_ref, fa_ref, fb_ref):
    x = jnp.concatenate([get_blocks(xa_ref), get_blocks(xb_ref)], axis=0)
    units = w_ref.shape[1]
    for j in range(0, units, chunk):
        sl = slice(j, j + chunk)
        gate = dot(x, w_ref[0, sl, :], LAST)
        up = dot(x, w_ref[1, sl, :], LAST)
        sig = 0.5 * jnp.tanh(0.5 * gate) + 0.5
        silu = gate * sig
        hid_ref[:, sl] = (silu * up).astype(BF16)
        fa_ref[:, sl] = (up * (sig + silu * (1.0 - sig))).astype(BF16)
        fb_ref[:, sl] = silu.astype(BF16)
    out = dot(hid_ref[...], w_ref[2])
    rows = out.shape[0] // 2
    put_blocks(pa_ref, out[:rows])
    put_blocks(pb_ref, out[rows:])


def backward_kernel(chunk, w_ref, ra_ref, rb_ref, fa_ref, fb_ref, pa_ref, pb_ref, dgu_ref):
    rg = jnp.concatenate([get_blocks(ra_ref), get_blocks(rb_ref)], axis=0)
    units, width = w_ref.shape[1:]
    for j in range(0, units, chunk):
        sl = slice(j, j + chunk)
        dh = dot(rg, w_ref[2, sl, :], LAST)
        dgu_ref[:, sl] = (dh * fa_ref[:, sl].astype(F32)).astype(BF16)
        dgu_ref[:, units + j : units + j + chunk] = (dh * fb_ref[:, sl].astype(F32)).astype(BF16)
    out = dot(dgu_ref[...], w_ref[0:2].reshape(2 * units, width))
    rows = out.shape[0] // 2
    put_blocks(pa_ref, out[:rows])
    put_blocks(pb_ref, out[rows:])


def add_kernel(a_ref, b_ref, out_ref):
    out_ref[...] = (a_ref[...] + b_ref[...].astype(F32)).astype(BF16)


def relay_forward_kernel(base_ref, meta_ref, got_ref, part_ref):
    meta = meta_ref[...]
    m0, m1 = slot_masks(base_ref[0], meta[0:2, :], *got_ref.shape[:2])
    got = get_blocks(got_ref)
    g0, g1 = gate_columns(meta)
    part_ref[...] = (g0 * dot(m0, got, FIRST) + g1 * dot(m1, got, FIRST)).astype(BF16)


def combine_kernel(
    base_ref, meta_ref, teacher_ref, got_ref, part_ref, student_ref, d_gates_ref, diff_ref, rows_ref
):
    meta = meta_ref[...]
    m0, m1 = slot_masks(base_ref[0], meta[0:2, :], *got_ref.shape[:2])
    got = get_blocks(got_ref)
    g0, g1 = gate_columns(meta)
    o0, o1 = dot(m0, got, FIRST), dot(m1, got, FIRST)
    total = g0 * o0 + g1 * o1 + part_ref[...].astype(F32)
    student_ref[...] = total.astype(BF16)
    diff = total - teacher_ref[...].astype(F32)
    diff_ref[...] = diff.astype(BF16)
    put_d_gates(d_gates_ref, diff, o0, o1)
    put_route_grads(rows_ref, m0, m1, g0, g1, diff)


def put_d_gates(ref, diff, o0, o1):
    ref[...] = jnp.concatenate(
        [
            jnp.sum(diff * o0, axis=1, keepdims=True),
            jnp.sum(diff * o1, axis=1, keepdims=True),
        ],
        axis=1,
    )


def put_route_grads(ref, m0, m1, g0, g1, diff):
    grads = jnp.concatenate([(g0 * diff).astype(BF16), (g1 * diff).astype(BF16)], axis=0)
    put_blocks(ref, dot(jnp.concatenate([m0, m1], axis=1), grads))


def relay_backward_kernel(base_ref, meta_ref, got_ref, diff_ref, d_gates_ref, rows_ref):
    meta = meta_ref[...]
    m0, m1 = slot_masks(base_ref[0], meta[0:2, :], *got_ref.shape[:2])
    got = get_blocks(got_ref)
    g0, g1 = gate_columns(meta)
    diff = diff_ref[...].astype(F32)
    put_route_grads(rows_ref, m0, m1, g0, g1, diff)
    put_d_gates(d_gates_ref, diff, dot(m0, got, FIRST), dot(m1, got, FIRST))


def relay_sum_kernel(base_ref, meta_ref, got_ref, part_ref):
    m0, m1 = slot_masks(base_ref[0], meta_ref[0:2, :], *got_ref.shape[:2])
    part_ref[...] = dot(m0 + m1, get_blocks(got_ref), FIRST).astype(BF16)


def final_kernel(base_ref, meta_ref, got_ref, part_ref, out_ref):
    m0, m1 = slot_masks(base_ref[0], meta_ref[0:2, :], *got_ref.shape[:2])
    total = dot(m0 + m1, get_blocks(got_ref), FIRST) + part_ref[...].astype(F32)
    out_ref[...] = total.astype(BF16)


def weight_kernel(*refs):
    xs, rgs, acts, out_ref = refs[0:4], refs[4:8], refs[8:14], refs[14]
    x_near = jnp.concatenate([get_blocks(r) for r in xs[:2]], axis=0)
    x_far = jnp.concatenate([get_blocks(r) for r in xs[2:]], axis=0)
    rg_near = jnp.concatenate([get_blocks(r) for r in rgs[:2]], axis=0)
    rg_far = jnp.concatenate([get_blocks(r) for r in rgs[2:]], axis=0)
    for m, (near, far) in enumerate(((x_near, x_far), (x_near, x_far), (rg_near, rg_far))):
        term = dot(acts[m][...], near, FIRST) + dot(acts[3 + m][...], far, FIRST)
        out_ref[m] = term.astype(BF16)


def local(tokens, teacher, routes, gate_weights, weights):
    tok, width = tokens.shape
    experts = lax.axis_size("expert")
    half = experts // 2
    capacity = 4 * tok // experts
    rows = 2 * half * capacity
    units = weights.shape[1]
    chunk = min(256, units)
    base = (lax.axis_index("expert") // half * half).reshape(1)
    groups = [list(range(half)), list(range(half, experts))]
    mirror = [(i, i ^ half) for i in range(experts)]

    blocks = jax.ShapeDtypeStruct((half, capacity, width), BF16)
    blocks_f32 = jax.ShapeDtypeStruct((half, capacity, width), F32)
    dense = jax.ShapeDtypeStruct((tok, width), BF16)
    pair = jax.ShapeDtypeStruct((tok, 2), F32)
    acts = jax.ShapeDtypeStruct((rows, units), BF16)
    acts2 = jax.ShapeDtypeStruct((rows, 2 * units), BF16)
    vspec = pl.BlockSpec(memory_space=pltpu.VMEM)
    sspec = pl.BlockSpec(memory_space=pltpu.SMEM)
    matmul = 2 * rows * width * units

    def call(kernel, name, out_shape, scalars, *args, flops=0, limit=16):
        many = isinstance(out_shape, list)
        return pl.pallas_call(
            kernel,
            in_specs=[sspec] * scalars + [vspec] * (len(args) - scalars),
            out_specs=[vspec] * len(out_shape) if many else vspec,
            out_shape=out_shape,
            cost_estimate=pl.CostEstimate(
                flops=flops or 10**8, bytes_accessed=4 * MIB, transcendentals=0
            ),
            compiler_params=pltpu.CompilerParams(vmem_limit_bytes=limit * MIB),
            name=name,
        )(*args)

    def within_half(x):
        return lax.all_to_all(
            x, "expert", split_axis=0, concat_axis=0, axis_index_groups=groups, tiled=True
        )

    def to_mirror(x):
        return lax.ppermute(x, "expert", mirror)

    def to_sibling(x):
        return lax.ppermute(x, "dp", [(0, 1), (1, 0)])

    own = weights[0].transpose(1, 0, 2)
    meta = jnp.concatenate(
        [routes.T.astype(F32), gate_weights.T, jnp.zeros((4, tok), F32)], axis=0
    )

    def forward(x, name):
        x_sib = to_sibling(x)
        pa, pb, hid, fa, fb = call(
            functools.partial(forward_kernel, chunk),
            name,
            [blocks_f32, blocks, acts, acts, acts],
            0,
            own,
            x,
            x_sib,
            flops=3 * matmul,
            limit=24,
        )
        out = call(add_kernel, "add_halves", blocks, 0, pa, to_sibling(pb))
        return out, (x, x_sib, hid, fa, fb)

    def backward(rg, saved, name):
        fa, fb = saved[3:]
        rg_sib = to_sibling(rg)
        pa, pb, dgu = call(
            functools.partial(backward_kernel, chunk),
            name,
            [blocks_f32, blocks, acts2],
            0,
            own,
            rg,
            rg_sib,
            fa,
            fb,
            flops=3 * matmul,
            limit=24,
        )
        out = call(add_kernel, "add_halves", blocks, 0, pa, to_sibling(pb))
        return out, (rg, rg_sib, dgu)

    far_tokens = to_mirror(tokens)
    far_meta = to_mirror(meta)
    x_near = within_half(call(pack_kernel, "pack_near", blocks, 1, base, meta, tokens))
    x_far = within_half(call(pack_kernel, "pack_far", blocks, 1, base, far_meta, far_tokens))

    out_near, saved_near = forward(x_near, "forward_near")
    out_far, saved_far = forward(x_far, "forward_far")

    got_far = within_half(out_far)
    part = to_mirror(
        call(relay_forward_kernel, "relay_forward", dense, 1, base, far_meta, got_far)
    )
    got_near = within_half(out_near)
    student, d_gates, diff, rows_near = call(
        combine_kernel,
        "combine_routes",
        [dense, pair, dense, blocks],
        1,
        base,
        meta,
        teacher,
        got_near,
        part,
    )

    far_diff = to_mirror(diff)
    rg_near = within_half(rows_near)
    far_d_gates, rows_far = call(
        relay_backward_kernel,
        "relay_backward",
        [pair, blocks],
        1,
        base,
        far_meta,
        got_far,
        far_diff,
    )
    rg_far = within_half(rows_far)
    d_gates = d_gates + to_mirror(far_d_gates)

    grad_near, more_near = backward(rg_near, saved_near, "backward_near")
    grad_far, more_far = backward(rg_far, saved_far, "backward_far")

    back_far = within_half(grad_far)
    part = to_mirror(call(relay_sum_kernel, "relay_sum", dense, 1, base, far_meta, back_far))
    back_near = within_half(grad_near)

    whole = pl.BlockSpec((half, capacity, width), lambda i: (0, 0, 0))
    steps = units // chunk
    column = lambda first: pl.BlockSpec((rows, chunk), lambda i: (0, first + i))
    weight_grads = pl.pallas_call(
        weight_kernel,
        grid=(steps,),
        in_specs=[whole] * 8 + [column(0), column(steps), column(0)] * 2,
        out_specs=pl.BlockSpec((3, chunk, width), lambda i: (0, i, 0)),
        out_shape=jax.ShapeDtypeStruct((3, units, width), BF16),
        cost_estimate=pl.CostEstimate(
            flops=6 * matmul, bytes_accessed=20 * MIB, transcendentals=0
        ),
        compiler_params=pltpu.CompilerParams(vmem_limit_bytes=24 * MIB),
        name="weight_gradients",
    )(
        *saved_near[:2],
        *saved_far[:2],
        *more_near[:2],
        *more_far[:2],
        more_near[2],
        more_near[2],
        saved_near[2],
        more_far[2],
        more_far[2],
        saved_far[2],
    )

    d_tokens = call(
        final_kernel, "combine_gradients", dense, 1, base, meta, back_near, part
    )
    return (student, d_tokens, d_gates, weight_grads.transpose(1, 0, 2)[None])


def solution(mesh):
    rows = P(("groups", "expert", "dp"), None)
    return jax.shard_map(
        local,
        mesh=mesh,
        in_specs=(rows, rows, rows, rows, P("expert", "dp", None, None)),
        out_specs=(rows, rows, rows, P(("groups", "expert"), "dp", None, None)),
        check_vma=False,
    )
```

```python
import functools

import jax
import jax.numpy as jnp
from jax import lax
from jax.experimental import pallas as pl
from jax.experimental.pallas import tpu as pltpu
from jax.sharding import PartitionSpec as P

PLAIN = (((1,), (0,)), ((), ()))
LAST = (((1,), (1,)), ((), ()))
FIRST = (((0,), (0,)), ((), ()))
MIB = 1024 * 1024
F32 = jnp.float32
BF16 = jnp.bfloat16


def dot(a, b, dims=PLAIN):
    return lax.dot_general(a, b, dims, preferred_element_type=F32)


def slot_masks(me, meta, pieces, capacity):
    tok = meta.shape[1]
    expert_of = (lax.broadcasted_iota(jnp.int32, (pieces, tok), 0) ^ me).astype(F32)
    first, second = meta[0:1, :] == expert_of, meta[1:2, :] == expert_of
    chosen = jnp.where(first | second, 1.0, 0.0).astype(BF16)
    before = lax.broadcasted_iota(jnp.int32, (tok, tok), 0) < lax.broadcasted_iota(
        jnp.int32, (tok, tok), 1
    )
    rank = dot(chosen, jnp.where(before, 1.0, 0.0).astype(BF16))
    rank0 = jnp.where(first, rank, -1.0)
    rank1 = jnp.where(second, rank, -1.0)
    place = lax.broadcasted_iota(jnp.int32, (capacity, tok), 0).astype(F32)

    def expand(ranks):
        return jnp.concatenate(
            [
                jnp.where(ranks[s : s + 1, :] == place, 1.0, 0.0).astype(BF16)
                for s in range(pieces)
            ],
            axis=0,
        )

    return expand(rank0), expand(rank1)


def put(refs, rows):
    capacity = refs[0].shape[0]
    for s, ref in enumerate(refs):
        ref[...] = rows[s * capacity : (s + 1) * capacity].astype(ref.dtype)


def get(refs):
    return jnp.concatenate([ref[...] for ref in refs], axis=0)


def masks_of(me_ref, meta, refs):
    return slot_masks(me_ref[0], meta, len(refs), refs[0].shape[0])


def gate_columns(meta):
    columns = meta.T
    return columns[:, 2:3], columns[:, 3:4]


def route_sums(me_ref, meta, refs):
    m0, m1 = masks_of(me_ref, meta, refs)
    got = get(refs)
    g0, g1 = gate_columns(meta)
    o0, o1 = dot(m0, got, FIRST), dot(m1, got, FIRST)
    return m0, m1, g0, g1, o0, o1, g0 * o0 + g1 * o1


def put_d_gates(ref, diff, o0, o1):
    tok = diff.shape[0]
    lane = lax.broadcasted_iota(jnp.int32, (tok, 128), 1)
    d0 = jnp.sum(diff * o0, axis=1, keepdims=True)
    d1 = jnp.sum(diff * o1, axis=1, keepdims=True)
    ref[...] = jnp.where(lane == 0, d0, jnp.where(lane == 1, d1, 0.0)).T[0:2, :]


def put_route_grads(refs, m0, m1, g0, g1, diff):
    grads = jnp.concatenate([(g0 * diff).astype(BF16), (g1 * diff).astype(BF16)], axis=0)
    put(refs, dot(jnp.concatenate([m0, m1], axis=1), grads))


def pack_near_kernel(me_ref, routes_ref, gates_ref, tokens_ref, meta_ref, *rows_refs):
    meta = jnp.concatenate(
        [
            routes_ref[...].astype(F32),
            gates_ref[...],
            jnp.zeros((4, routes_ref.shape[1]), F32),
        ],
        axis=0,
    )
    meta_ref[...] = meta
    m0, m1 = masks_of(me_ref, meta, rows_refs)
    put(rows_refs, dot(m0 + m1, tokens_ref[...]))


def pack_far_kernel(me_ref, meta_ref, tokens_ref, *rows_refs):
    m0, m1 = masks_of(me_ref, meta_ref[...], rows_refs)
    put(rows_refs, dot(m0 + m1, tokens_ref[...]))


def forward_kernel(pieces, chunk, own_ref, other_ref, *refs):
    ins, outs, refs = refs[:pieces], refs[pieces : 2 * pieces], refs[2 * pieces :]
    x_ref, hid_own_ref, hid_other_ref, fa_ref, fb_ref = refs
    x = get(ins)
    x_ref[...] = x
    units = own_ref.shape[1]
    for w_ref, hid_ref, first in ((own_ref, hid_own_ref, 0), (other_ref, hid_other_ref, units)):
        for j in range(0, units, chunk):
            sl = slice(j, j + chunk)
            to = slice(first + j, first + j + chunk)
            gate = dot(x, w_ref[0, sl, :], LAST)
            up = dot(x, w_ref[1, sl, :], LAST)
            sig = 0.5 * jnp.tanh(0.5 * gate) + 0.5
            silu = gate * sig
            hid_ref[:, sl] = (silu * up).astype(BF16)
            fa_ref[:, to] = (up * (sig + silu * (1.0 - sig))).astype(BF16)
            fb_ref[:, to] = silu.astype(BF16)
    put(outs, dot(hid_own_ref[...], own_ref[2]) + dot(hid_other_ref[...], other_ref[2]))


def backward_kernel(pieces, chunk, own_ref, other_ref, fa_ref, fb_ref, *refs):
    ins, outs, refs = refs[:pieces], refs[pieces : 2 * pieces], refs[2 * pieces :]
    rg_ref, dgu_own_ref, dgu_other_ref = refs
    rg = get(ins)
    rg_ref[...] = rg
    units, width = own_ref.shape[1:]
    for w_ref, dgu_ref, first in ((own_ref, dgu_own_ref, 0), (other_ref, dgu_other_ref, units)):
        for j in range(0, units, chunk):
            sl = slice(j, j + chunk)
            at = slice(first + j, first + j + chunk)
            dh = dot(rg, w_ref[2, sl, :], LAST)
            dgu_ref[:, sl] = (dh * fa_ref[:, at].astype(F32)).astype(BF16)
            dgu_ref[:, units + j : units + j + chunk] = (dh * fb_ref[:, at].astype(F32)).astype(BF16)
    put(
        outs,
        dot(dgu_own_ref[...], own_ref[0:2].reshape(2 * units, width))
        + dot(dgu_other_ref[...], other_ref[0:2].reshape(2 * units, width)),
    )


def near_sum_kernel(me_ref, meta_ref, teacher_ref, *refs):
    ins, out_ref = refs[:-1], refs[-1]
    total = route_sums(me_ref, meta_ref[...], ins)[-1]
    out_ref[...] = (total - teacher_ref[...].astype(F32)).astype(BF16)


def far_sum_kernel(me_ref, meta_ref, *refs):
    ins, out_ref = refs[:-1], refs[-1]
    out_ref[...] = route_sums(me_ref, meta_ref[...], ins)[-1].astype(BF16)


def far_grad_kernel(pieces, me_ref, meta_ref, rest_ref, *refs):
    ins, d_gates_ref, outs = refs[:pieces], refs[pieces], refs[pieces + 1 :]
    m0, m1, g0, g1, o0, o1, total = route_sums(me_ref, meta_ref[...], ins)
    diff = total + rest_ref[...].astype(F32)
    put_route_grads(outs, m0, m1, g0, g1, diff)
    put_d_gates(d_gates_ref, diff, o0, o1)


def near_grad_kernel(pieces, me_ref, meta_ref, teacher_ref, part_ref, *refs):
    ins, student_ref, d_gates_ref, outs = (
        refs[:pieces],
        refs[pieces],
        refs[pieces + 1],
        refs[pieces + 2 :],
    )
    m0, m1, g0, g1, o0, o1, total = route_sums(me_ref, meta_ref[...], ins)
    total = total + part_ref[...].astype(F32)
    student_ref[...] = total.astype(BF16)
    diff = total - teacher_ref[...].astype(F32)
    put_route_grads(outs, m0, m1, g0, g1, diff)
    put_d_gates(d_gates_ref, diff, o0, o1)


def far_back_kernel(me_ref, meta_ref, *refs):
    ins, out_ref = refs[:-1], refs[-1]
    m0, m1 = masks_of(me_ref, meta_ref[...], ins)
    out_ref[...] = dot(m0 + m1, get(ins), FIRST).astype(BF16)


def final_kernel(pieces, me_ref, meta_ref, part_ref, near_ref, far_ref, *refs):
    ins, out_ref, d_gates_ref = refs[:pieces], refs[pieces], refs[pieces + 1]
    m0, m1 = masks_of(me_ref, meta_ref[...], ins)
    total = dot(m0 + m1, get(ins), FIRST) + part_ref[...].astype(F32)
    out_ref[...] = total.astype(BF16)
    d_gates_ref[...] = near_ref[...] + far_ref[...]


def weight_kernel(*refs):
    xs, rgs, gates, ups, hids, out_ref = (
        refs[0:4],
        refs[4:8],
        refs[8:12],
        refs[12:16],
        refs[16:20],
        refs[20],
    )
    for m, (acts, rows) in enumerate(((gates, xs), (ups, xs), (hids, rgs))):
        term = dot(acts[0][...], rows[0][...], FIRST)
        for i in range(1, 4):
            term = term + dot(acts[i][...], rows[i][...], FIRST)
        out_ref[m] = term.astype(BF16)


def local(tokens, teacher, routes, gate_weights, weights):
    tok, width = tokens.shape
    experts = lax.axis_size("expert")
    half = experts // 2
    capacity = 4 * tok // experts
    rows = half * capacity
    units = weights.shape[1]
    chunk = min(256, units)
    me = lax.axis_index("expert").reshape(1)

    pieces = [jax.ShapeDtypeStruct((capacity, width), BF16)] * half
    dense = jax.ShapeDtypeStruct((tok, width), BF16)
    pair = jax.ShapeDtypeStruct((2, tok), F32)
    flat = jax.ShapeDtypeStruct((rows, width), BF16)
    acts = jax.ShapeDtypeStruct((rows, units), BF16)
    acts2 = jax.ShapeDtypeStruct((rows, 2 * units), BF16)
    vspec = pl.BlockSpec(memory_space=pltpu.VMEM)
    sspec = pl.BlockSpec(memory_space=pltpu.SMEM)
    matmul = 4 * rows * width * units

    def call(kernel, name, out_shape, scalars, *args, flops=10**8, limit=8):
        many = isinstance(out_shape, list)
        return pl.pallas_call(
            kernel,
            in_specs=[sspec] * scalars + [vspec] * (len(args) - scalars),
            out_specs=[vspec] * len(out_shape) if many else vspec,
            out_shape=out_shape,
            cost_estimate=pl.CostEstimate(
                flops=flops, bytes_accessed=2 * MIB, transcendentals=0
            ),
            compiler_params=pltpu.CompilerParams(vmem_limit_bytes=limit * MIB),
            name=name,
        )(*args)

    def within_half(rows_of):
        got = [rows_of[0]] + [None] * (half - 1)
        for s in range(half - 1, 0, -1):
            got[s] = lax.ppermute(rows_of[s], "expert", [(i, i ^ s) for i in range(experts)])
        return got

    def to_mirror(x):
        return lax.ppermute(x, "expert", [(i, i ^ half) for i in range(experts)])

    def to_sibling(x):
        return lax.ppermute(x, "dp", [(0, 1), (1, 0)])

    far_tokens = to_mirror(tokens)
    own = weights[0].transpose(1, 0, 2)
    other = to_sibling(own)

    def forward(x_pieces, name):
        res = call(
            functools.partial(forward_kernel, half, chunk),
            name,
            pieces + [flat] + [acts] * 2 + [acts2] * 2,
            0,
            own,
            other,
            *x_pieces,
            flops=3 * matmul,
            limit=20,
        )
        return res[:half], res[half:]

    def backward(rg_pieces, fa, fb, name):
        res = call(
            functools.partial(backward_kernel, half, chunk),
            name,
            pieces + [flat] + [acts2] * 2,
            0,
            own,
            other,
            fa,
            fb,
            *rg_pieces,
            flops=3 * matmul,
            limit=20,
        )
        return res[:half], res[half:]

    res = call(
        pack_near_kernel,
        "pack_near",
        [jax.ShapeDtypeStruct((8, tok), F32)] + pieces,
        1,
        me,
        routes.T,
        gate_weights.T,
        tokens,
    )
    meta, x_near = res[0], within_half(res[1:])
    far_meta = to_mirror(meta)
    x_far = within_half(call(pack_far_kernel, "pack_far", pieces, 1, me, far_meta, far_tokens))

    out_near, (xn, hn, hn_other, fan, fbn) = forward(x_near, "forward_near")
    got_near = within_half(out_near)
    rest = to_mirror(
        call(near_sum_kernel, "near_sum", dense, 1, me, meta, teacher, *got_near)
    )
    out_far, (xf, hf, hf_other, faf, fbf) = forward(x_far, "forward_far")
    got_far = within_half(out_far)
    part = to_mirror(call(far_sum_kernel, "far_sum", dense, 1, me, far_meta, *got_far))

    res = call(
        functools.partial(far_grad_kernel, half),
        "far_grad",
        [pair] + pieces,
        1,
        me,
        far_meta,
        rest,
        *got_far,
    )
    d_gates_far, rg_far = to_mirror(res[0]), within_half(res[1:])
    res = call(
        functools.partial(near_grad_kernel, half),
        "near_grad",
        [dense, pair] + pieces,
        1,
        me,
        meta,
        teacher,
        part,
        *got_near,
    )
    student, d_gates_near, rg_near = res[0], res[1], within_half(res[2:])

    grad_far, (rf, df, df_other) = backward(rg_far, faf, fbf, "backward_far")
    back_far = within_half(grad_far)
    part = to_mirror(call(far_back_kernel, "far_back", dense, 1, me, far_meta, *back_far))
    grad_near, (rn, dn, dn_other) = backward(rg_near, fan, fbn, "backward_near")
    back_near = within_half(grad_near)

    whole = pl.BlockSpec((rows, width), lambda i: (0, 0))
    steps = units // chunk
    column = lambda first: pl.BlockSpec((rows, chunk), lambda i: (0, first + i))
    xs = [xf, xn, to_sibling(xf), to_sibling(xn)]
    rgs = [rf, rn, to_sibling(rf), to_sibling(rn)]
    dgus = [df, dn, to_sibling(df_other), to_sibling(dn_other)]
    hids = [hf, hn, to_sibling(hf_other), to_sibling(hn_other)]
    weight_grads = pl.pallas_call(
        weight_kernel,
        grid=(steps,),
        in_specs=[whole] * 8 + [column(0)] * 4 + [column(steps)] * 4 + [column(0)] * 4,
        out_specs=pl.BlockSpec((3, chunk, width), lambda i: (0, i, 0)),
        out_shape=jax.ShapeDtypeStruct((3, units, width), BF16),
        cost_estimate=pl.CostEstimate(
            flops=3 * matmul * 2, bytes_accessed=16 * MIB, transcendentals=0
        ),
        compiler_params=pltpu.CompilerParams(vmem_limit_bytes=20 * MIB),
        name="weight_gradients",
    )(*xs, *rgs, *dgus, *dgus, *hids)

    d_tokens, d_gates = call(
        functools.partial(final_kernel, half),
        "combine_gradients",
        [dense, pair],
        1,
        me,
        meta,
        part,
        d_gates_near,
        d_gates_far,
        *back_near,
    )
    return (student, d_tokens, d_gates.T, weight_grads.transpose(1, 0, 2)[None])


def solution(mesh):
    rows = P(("groups", "expert", "dp"), None)
    return jax.shard_map(
        local,
        mesh=mesh,
        in_specs=(rows, rows, rows, rows, P("expert", "dp", None, None)),
        out_specs=(rows, rows, rows, P(("groups", "expert"), "dp", None, None)),
        check_vma=False,
    )
```

```python
import functools

import jax
import jax.numpy as jnp
from jax import lax
from jax.experimental import pallas as pl
from jax.experimental.pallas import tpu as pltpu
from jax.sharding import PartitionSpec as P

PLAIN = (((1,), (0,)), ((), ()))
LAST = (((1,), (1,)), ((), ()))
FIRST = (((0,), (0,)), ((), ()))
MIB = 1024 * 1024
F32 = jnp.float32
BF16 = jnp.bfloat16


def dot(a, b, dims=PLAIN):
    return lax.dot_general(a, b, dims, preferred_element_type=F32)


def slot_masks(me, meta, pieces, capacity):
    tok = meta.shape[1]
    expert_of = (lax.broadcasted_iota(jnp.int32, (pieces, tok), 0) ^ me).astype(F32)
    first, second = meta[0:1, :] == expert_of, meta[1:2, :] == expert_of
    chosen = jnp.where(first | second, 1.0, 0.0).astype(BF16)
    before = lax.broadcasted_iota(jnp.int32, (tok, tok), 0) < lax.broadcasted_iota(
        jnp.int32, (tok, tok), 1
    )
    rank = dot(chosen, jnp.where(before, 1.0, 0.0).astype(BF16))
    rank0 = jnp.where(first, rank, -1.0)
    rank1 = jnp.where(second, rank, -1.0)
    place = lax.broadcasted_iota(jnp.int32, (capacity, tok), 0).astype(F32)

    def expand(ranks):
        return jnp.concatenate(
            [
                jnp.where(ranks[s : s + 1, :] == place, 1.0, 0.0).astype(BF16)
                for s in range(pieces)
            ],
            axis=0,
        )

    return expand(rank0), expand(rank1)


def put(refs, rows):
    capacity = refs[0].shape[0]
    for s, ref in enumerate(refs):
        ref[...] = rows[s * capacity : (s + 1) * capacity].astype(ref.dtype)


def put_columns(ref, rows):
    side = rows.shape[0]
    for i in range(rows.shape[1] // side):
        ref[i] = rows[:, i * side : (i + 1) * side]


def put_rows(ref, first, value):
    side = value.shape[1]
    for i in range(value.shape[0] // side):
        ref[first + i] = value[i * side : (i + 1) * side, :]


def get_columns(ref):
    return jnp.concatenate([ref[i] for i in range(ref.shape[0])], axis=1)


def get(refs):
    return jnp.concatenate([ref[...] for ref in refs], axis=0)


def masks_of(me_ref, meta, refs):
    return slot_masks(me_ref[0], meta, len(refs), refs[0].shape[0])


def gate_columns(meta):
    columns = meta.T
    return columns[:, 2:3], columns[:, 3:4]


def route_sums(me_ref, meta, refs):
    m0, m1 = masks_of(me_ref, meta, refs)
    got = get(refs)
    g0, g1 = gate_columns(meta)
    o0, o1 = dot(m0, got, FIRST), dot(m1, got, FIRST)
    return m0, m1, g0, g1, o0, o1, g0 * o0 + g1 * o1


def put_d_gates(ref, diff, o0, o1):
    tok = diff.shape[0]
    lane = lax.broadcasted_iota(jnp.int32, (tok, 128), 1)
    d0 = jnp.sum(diff * o0, axis=1, keepdims=True)
    d1 = jnp.sum(diff * o1, axis=1, keepdims=True)
    ref[...] = jnp.where(lane == 0, d0, jnp.where(lane == 1, d1, 0.0)).T[0:2, :]


def put_route_grads(refs, m0, m1, g0, g1, diff):
    grads = jnp.concatenate([(g0 * diff).astype(BF16), (g1 * diff).astype(BF16)], axis=0)
    put(refs, dot(jnp.concatenate([m0, m1], axis=1), grads))


def pack_near_kernel(me_ref, own_ref, routes_ref, gates_ref, tokens_ref, meta_ref, *rows_refs):
    del own_ref
    meta = jnp.concatenate(
        [
            routes_ref[...].astype(F32),
            gates_ref[...],
            jnp.zeros((4, routes_ref.shape[1]), F32),
        ],
        axis=0,
    )
    meta_ref[...] = meta
    m0, m1 = masks_of(me_ref, meta, rows_refs)
    put(rows_refs, dot(m0 + m1, tokens_ref[...]))


def pack_far_kernel(me_ref, meta_ref, tokens_ref, *rows_refs):
    m0, m1 = masks_of(me_ref, meta_ref[...], rows_refs)
    put(rows_refs, dot(m0 + m1, tokens_ref[...]))


def forward_kernel(pieces, own_ref, other_ref, *refs):
    ins, outs, refs = refs[:pieces], refs[pieces : 2 * pieces], refs[2 * pieces :]
    sent_ref, hid_own_ref, fa_ref, fb_ref = refs
    x = get(ins)
    put_columns(sent_ref, x)
    units, width = other_ref.shape[1:]
    hidden = []
    for w_ref, first in ((own_ref, 0), (other_ref, units)):
        both = dot(w_ref[0:2].reshape(2 * units, width), x, LAST)
        gate, up = both[:units], both[units:]
        sig = 0.5 * jnp.tanh(0.5 * gate) + 0.5
        silu = gate * sig
        hidden.append((silu * up).astype(BF16))
        fa_ref[first : first + units, :] = (up * (sig + silu * (1.0 - sig))).astype(BF16)
        fb_ref[first : first + units, :] = silu.astype(BF16)
    hid_own_ref[...] = hidden[0]
    put_rows(sent_ref, width // x.shape[0], hidden[1])
    put(outs, dot(hidden[0], own_ref[2], FIRST) + dot(hidden[1], other_ref[2], FIRST))


def backward_kernel(pieces, own_ref, other_ref, fa_ref, fb_ref, *refs):
    ins, outs, refs = refs[:pieces], refs[pieces : 2 * pieces], refs[2 * pieces :]
    sent_ref, dgu_own_ref = refs
    rg = get(ins)
    put_columns(sent_ref, rg)
    units, width = own_ref.shape[1:]
    both = []
    for w_ref, first in ((own_ref, 0), (other_ref, units)):
        at = slice(first, first + units)
        dh = dot(w_ref[2], rg, LAST)
        dg = (dh * fa_ref[at, :].astype(F32)).astype(BF16)
        du = (dh * fb_ref[at, :].astype(F32)).astype(BF16)
        both.append(jnp.concatenate([dg, du], axis=0))
    dgu_own_ref[...] = both[0]
    put_rows(sent_ref, width // rg.shape[0], both[1])
    put(
        outs,
        dot(both[0], own_ref[0:2].reshape(2 * units, width), FIRST)
        + dot(both[1], other_ref[0:2].reshape(2 * units, width), FIRST),
    )


def near_sum_kernel(me_ref, meta_ref, teacher_ref, *refs):
    ins, out_ref = refs[:-1], refs[-1]
    total = route_sums(me_ref, meta_ref[...], ins)[-1]
    out_ref[...] = (total - teacher_ref[...].astype(F32)).astype(BF16)


def far_sum_kernel(me_ref, meta_ref, *refs):
    ins, out_ref = refs[:-1], refs[-1]
    out_ref[...] = route_sums(me_ref, meta_ref[...], ins)[-1].astype(BF16)


def far_grad_kernel(pieces, me_ref, meta_ref, rest_ref, *refs):
    ins, d_gates_ref, outs = refs[:pieces], refs[pieces], refs[pieces + 1 :]
    m0, m1, g0, g1, o0, o1, total = route_sums(me_ref, meta_ref[...], ins)
    diff = total + rest_ref[...].astype(F32)
    put_route_grads(outs, m0, m1, g0, g1, diff)
    put_d_gates(d_gates_ref, diff, o0, o1)


def near_grad_kernel(pieces, me_ref, meta_ref, teacher_ref, part_ref, *refs):
    ins, student_ref, d_gates_ref, outs = (
        refs[:pieces],
        refs[pieces],
        refs[pieces + 1],
        refs[pieces + 2 :],
    )
    m0, m1, g0, g1, o0, o1, total = route_sums(me_ref, meta_ref[...], ins)
    total = total + part_ref[...].astype(F32)
    student_ref[...] = total.astype(BF16)
    diff = total - teacher_ref[...].astype(F32)
    put_route_grads(outs, m0, m1, g0, g1, diff)
    put_d_gates(d_gates_ref, diff, o0, o1)


def far_back_kernel(me_ref, meta_ref, d_gates_ref, *refs):
    ins, out_ref = refs[:-1], refs[-1]
    m0, m1 = masks_of(me_ref, meta_ref[...], ins)
    tok = m0.shape[1]
    out_ref[:tok, :] = dot(m0 + m1, get(ins), FIRST).astype(BF16)
    value = d_gates_ref[...]
    high = value.astype(BF16)
    low = (value - high.astype(F32)).astype(BF16)
    rest = jnp.zeros((out_ref.shape[0] - tok - 4, tok), BF16)
    out_ref[tok:, :tok] = jnp.concatenate([high, low, rest], axis=0)
    out_ref[tok:, tok:] = jnp.zeros((out_ref.shape[0] - tok, out_ref.shape[1] - tok), BF16)


def final_kernel(pieces, me_ref, meta_ref, part_ref, near_ref, *refs):
    ins, out_ref, d_gates_ref = refs[:pieces], refs[pieces], refs[pieces + 1]
    m0, m1 = masks_of(me_ref, meta_ref[...], ins)
    tok = m0.shape[1]
    total = dot(m0 + m1, get(ins), FIRST) + part_ref[:tok, :].astype(F32)
    out_ref[...] = total.astype(BF16)
    far = part_ref[tok:, :tok].astype(F32)
    d_gates_ref[...] = near_ref[...] + (far[0:2] + far[2:4])


def weight_kernel(*refs):
    refs, out_ref, finished_ref = refs[:-2], refs[-2], refs[-1]
    xs, rgs = [get_columns(r) for r in refs[0:4]], [get_columns(r) for r in refs[4:8]]
    finished_ref[...] = jnp.zeros_like(finished_ref)
    for m, rows in enumerate((xs, xs, rgs)):
        term = None
        for ref, row in zip(refs[8 + 4 * m : 12 + 4 * m], rows):
            act = ref[0] if len(ref.shape) == 3 else ref[...]
            term = dot(act, row) if term is None else term + dot(act, row)
        out_ref[m] = term.astype(BF16)


def local(tokens, teacher, routes, gate_weights, weights):
    tok, width = tokens.shape
    experts = lax.axis_size("expert")
    half = experts // 2
    capacity = 4 * tok // experts
    rows = half * capacity
    units = weights.shape[1]
    me = lax.axis_index("expert").reshape(1)

    pieces = [jax.ShapeDtypeStruct((capacity, width), BF16)] * half
    dense = jax.ShapeDtypeStruct((tok, width), BF16)
    longer = jax.ShapeDtypeStruct((tok + 16, width), BF16)
    pair = jax.ShapeDtypeStruct((2, tok), F32)
    acts = jax.ShapeDtypeStruct((units, rows), BF16)
    across, along = width // rows, units // rows
    sent_x = jax.ShapeDtypeStruct((across + along, rows, rows), BF16)
    sent_g = jax.ShapeDtypeStruct((across + 2 * along, rows, rows), BF16)
    acts2 = jax.ShapeDtypeStruct((2 * units, rows), BF16)
    vspec = pl.BlockSpec(memory_space=pltpu.VMEM)
    sspec = pl.BlockSpec(memory_space=pltpu.SMEM)
    aspec = pl.BlockSpec(memory_space=pl.ANY)
    matmul = 4 * rows * width * units

    def call(
        kernel,
        name,
        out_shape,
        specs,
        *args,
        after=(),
        through=(),
        flops=10**8,
        limit=8,
        scratch=(),
    ):
        many = isinstance(out_shape, list)
        specs = list(specs) + [vspec] * (len(args) - len(specs))
        inputs = len(args) + len(after) + len(through)
        outputs = len(out_shape) if many else 1

        def body(*refs):
            kernel(
                *refs[: len(args)],
                *refs[inputs : inputs + outputs],
                *refs[inputs + outputs + len(through) :],
            )

        out_specs = [vspec] * outputs + [aspec] * len(through)
        out_shapes = (out_shape if many else [out_shape]) + [
            jax.ShapeDtypeStruct(a.shape, a.dtype) for a in through
        ]
        single = not many and not through
        return pl.pallas_call(
            body,
            in_specs=specs + [aspec] * (len(after) + len(through)),
            out_specs=out_specs[0] if single else out_specs,
            out_shape=out_shapes[0] if single else out_shapes,
            input_output_aliases={
                len(args) + len(after) + i: outputs + i for i in range(len(through))
            },
            scratch_shapes=scratch,
            cost_estimate=pl.CostEstimate(
                flops=flops, bytes_accessed=2 * MIB, transcendentals=0
            ),
            compiler_params=pltpu.CompilerParams(vmem_limit_bytes=limit * MIB),
            name=name,
        )(*args, *after, *through)

    def within_half(rows_of):
        got = [rows_of[0]] + [None] * (half - 1)
        for s in range(1, half):
            got[s] = lax.ppermute(rows_of[s], "expert", [(i, i ^ s) for i in range(experts)])
        return got

    def to_mirror(x):
        return lax.ppermute(x, "expert", [(i, i ^ half) for i in range(experts)])

    def to_sibling(x):
        return lax.ppermute(x, "dp", [(0, 1), (1, 0)])

    far_tokens = to_mirror(tokens)
    own = weights[0].transpose(1, 0, 2)
    other = to_sibling(own)

    def forward(x_pieces, name, after=()):
        res = call(
            functools.partial(forward_kernel, half),
            name,
            pieces + [sent_x, acts, acts2, acts2],
            [],
            own,
            other,
            *x_pieces,
            after=after,
            flops=3 * matmul,
            limit=20,
        )
        return res[:half], res[half:]

    def backward(rg_pieces, fa, fb, name, after=(), through=()):
        res = call(
            functools.partial(backward_kernel, half),
            name,
            pieces + [sent_g, acts2],
            [],
            own,
            other,
            fa,
            fb,
            *rg_pieces,
            after=after,
            through=through,
            flops=3 * matmul,
            limit=20,
        )
        return res[:half], res[half:]

    res = call(
        pack_near_kernel,
        "pack_near",
        [jax.ShapeDtypeStruct((8, tok), F32)] + pieces,
        [sspec],
        me,
        own,
        routes.T,
        gate_weights.T,
        tokens,
        limit=10,
    )
    meta, x_near = res[0], within_half(res[1:])
    far_meta = to_mirror(meta)
    x_far = within_half(
        call(pack_far_kernel, "pack_far", pieces, [sspec], me, far_meta, far_tokens)
    )

    out_near, (xn, hn, fan, fbn) = forward(x_near, "forward_near")
    got_near = within_half(out_near)
    rest_rows = call(
        near_sum_kernel, "near_sum", dense, [sspec], me, meta, teacher, *got_near
    )
    rest = to_mirror(rest_rows)
    out_far, (xf, hf, faf, fbf) = forward(x_far, "forward_far", after=[rest_rows])
    got_far = within_half(out_far)
    xf_sib, xn_sib = to_sibling(xf), to_sibling(xn)
    part = to_mirror(call(far_sum_kernel, "far_sum", dense, [sspec], me, far_meta, *got_far))

    res = call(
        functools.partial(far_grad_kernel, half),
        "far_grad",
        [pair] + pieces,
        [sspec],
        me,
        far_meta,
        rest,
        *got_far,
    )
    d_gates_far, rg_far = res[0], within_half(res[1:])
    res = call(
        functools.partial(near_grad_kernel, half),
        "near_grad",
        [dense, pair] + pieces,
        [sspec],
        me,
        meta,
        teacher,
        part,
        *got_near,
    )
    student, d_gates_near, rg_near = res[0], res[1], within_half(res[2:])

    grad_far, (gf, df) = backward(rg_far, faf, fbf, "backward_far", after=[xf_sib, xn_sib])
    back_far = within_half(grad_far)
    part_rows = call(
        far_back_kernel,
        "far_back",
        longer,
        [sspec],
        me,
        far_meta,
        d_gates_far,
        *back_far,
    )
    part = to_mirror(part_rows)
    grad_near, (gn, dn) = backward(rg_near, fan, fbn, "backward_near", after=[back_far[1]])
    gf_sib, gn_sib = to_sibling(gf), to_sibling(gn)
    back_near = within_half(grad_near)

    chunk, steps = rows, along
    columns = pl.BlockSpec((across, rows, rows), lambda i: (0, 0, 0))
    part_of = lambda first: pl.BlockSpec((1, rows, rows), lambda i: (across + first + i, 0, 0))
    block = lambda first: pl.BlockSpec((chunk, rows), lambda i: (first + i, 0))
    specs = [columns] * 8
    for first in (0, steps, 0):
        specs += [block(first)] * 2 + [part_of(first)] * 2
    weight_grads, finished = pl.pallas_call(
        weight_kernel,
        grid=(steps,),
        in_specs=specs,
        out_specs=[
            pl.BlockSpec((3, chunk, width), lambda i: (0, i, 0)),
            pl.BlockSpec((8, 128), lambda i: (0, 0)),
        ],
        out_shape=[
            jax.ShapeDtypeStruct((3, units, width), BF16),
            jax.ShapeDtypeStruct((8, 128), F32),
        ],
        cost_estimate=pl.CostEstimate(
            flops=3 * matmul * 2, bytes_accessed=16 * MIB, transcendentals=0
        ),
        compiler_params=pltpu.CompilerParams(vmem_limit_bytes=20 * MIB),
        name="weight_gradients",
    )(
        *(xf, xn, xf_sib, xn_sib),
        *(gf, gn, gf_sib, gn_sib),
        *(df, dn, gf_sib, gn_sib),
        *(df, dn, gf_sib, gn_sib),
        *(hf, hn, xf_sib, xn_sib),
    )

    d_tokens, d_gates = call(
        functools.partial(final_kernel, half),
        "combine_gradients",
        [dense, pair],
        [sspec],
        me,
        meta,
        part,
        d_gates_near,
        *back_near,
        after=[finished],
    )
    return (student, d_tokens, d_gates.T, weight_grads.transpose(1, 0, 2)[None])


def solution(mesh):
    rows = P(("groups", "expert", "dp"), None)
    return jax.shard_map(
        local,
        mesh=mesh,
        in_specs=(rows, rows, rows, rows, P("expert", "dp", None, None)),
        out_specs=(rows, rows, rows, P(("groups", "expert"), "dp", None, None)),
        check_vma=False,
    )
```

```python
import functools

import jax
import jax.numpy as jnp
from jax import lax
from jax.experimental import pallas as pl
from jax.experimental.pallas import tpu as pltpu
from jax.sharding import PartitionSpec as P

PLAIN = (((1,), (0,)), ((), ()))
LAST = (((1,), (1,)), ((), ()))
FIRST = (((0,), (0,)), ((), ()))
MIB = 1024 * 1024
F32 = jnp.float32
BF16 = jnp.bfloat16


def dot(a, b, dims=PLAIN):
    return lax.dot_general(a, b, dims, preferred_element_type=F32)


def slot_masks(me, meta, pieces, capacity):
    tok = meta.shape[1]
    expert_of = (lax.broadcasted_iota(jnp.int32, (pieces, tok), 0) ^ me).astype(F32)
    first, second = meta[0:1, :] == expert_of, meta[1:2, :] == expert_of
    chosen = jnp.where(first | second, 1.0, 0.0).astype(BF16)
    before = lax.broadcasted_iota(jnp.int32, (tok, tok), 0) < lax.broadcasted_iota(
        jnp.int32, (tok, tok), 1
    )
    rank = dot(chosen, jnp.where(before, 1.0, 0.0).astype(BF16))
    rank0 = jnp.where(first, rank, -1.0)
    rank1 = jnp.where(second, rank, -1.0)
    place = lax.broadcasted_iota(jnp.int32, (capacity, tok), 0).astype(F32)

    def expand(ranks):
        return jnp.concatenate(
            [
                jnp.where(ranks[s : s + 1, :] == place, 1.0, 0.0).astype(BF16)
                for s in range(pieces)
            ],
            axis=0,
        )

    return expand(rank0), expand(rank1)


def put(refs, rows):
    capacity = refs[0].shape[0]
    for s, ref in enumerate(refs):
        ref[...] = rows[s * capacity : (s + 1) * capacity].astype(ref.dtype)


def put_columns(ref, rows):
    side = rows.shape[0]
    for i in range(rows.shape[1] // side):
        ref[i] = rows[:, i * side : (i + 1) * side]


def put_rows(ref, first, value):
    side = value.shape[1]
    for i in range(value.shape[0] // side):
        ref[first + i] = value[i * side : (i + 1) * side, :]


def get_columns(ref):
    return jnp.concatenate([ref[i] for i in range(ref.shape[0])], axis=1)


def get(refs):
    return jnp.concatenate([ref[...] for ref in refs], axis=0)


def masks_of(meta, refs):
    return slot_masks(lax.axis_index("expert"), meta, len(refs), refs[0].shape[0])


def gate_columns(meta):
    columns = meta.T
    return columns[:, 2:3], columns[:, 3:4]


def route_sums(meta, refs):
    m0, m1 = masks_of(meta, refs)
    got = get(refs)
    g0, g1 = gate_columns(meta)
    o0, o1 = dot(m0, got, FIRST), dot(m1, got, FIRST)
    return m0, m1, g0, g1, o0, o1, g0 * o0 + g1 * o1


def put_d_gates(ref, diff, o0, o1):
    tok = diff.shape[0]
    lane = lax.broadcasted_iota(jnp.int32, (tok, 128), 1)
    d0 = jnp.sum(diff * o0, axis=1, keepdims=True)
    d1 = jnp.sum(diff * o1, axis=1, keepdims=True)
    ref[...] = jnp.where(lane == 0, d0, jnp.where(lane == 1, d1, 0.0)).T[0:2, :]


def put_route_grads(refs, m0, m1, g0, g1, diff):
    grads = jnp.concatenate([(g0 * diff).astype(BF16), (g1 * diff).astype(BF16)], axis=0)
    put(refs, dot(jnp.concatenate([m0, m1], axis=1), grads))


def pack_near_kernel(routes_ref, gates_ref, tokens_ref, meta_ref, *rows_refs):
    meta = jnp.concatenate(
        [
            routes_ref[...].astype(F32),
            gates_ref[...],
            jnp.zeros((4, routes_ref.shape[1]), F32),
        ],
        axis=0,
    )
    meta_ref[...] = meta
    m0, m1 = masks_of(meta, rows_refs)
    put(rows_refs, dot(m0 + m1, tokens_ref[...]))


def pack_far_kernel(meta_ref, tokens_ref, *rows_refs):
    m0, m1 = masks_of(meta_ref[...], rows_refs)
    put(rows_refs, dot(m0 + m1, tokens_ref[...]))


def forward_kernel(pieces, own_ref, other_ref, *refs):
    ins, outs, refs = refs[:pieces], refs[pieces : 2 * pieces], refs[2 * pieces :]
    sent_ref, hid_own_ref, fa_ref, fb_ref = refs
    x = get(ins)
    put_columns(sent_ref, x)
    units, width = other_ref.shape[1:]
    hidden = []
    for w_ref, first in ((own_ref, 0), (other_ref, units)):
        both = dot(w_ref[0:2].reshape(2 * units, width), x, LAST)
        gate, up = both[:units], both[units:]
        sig = 0.5 * jnp.tanh(0.5 * gate) + 0.5
        silu = gate * sig
        hidden.append((silu * up).astype(BF16))
        fa_ref[first : first + units, :] = (up * (sig + silu * (1.0 - sig))).astype(BF16)
        fb_ref[first : first + units, :] = silu.astype(BF16)
    hid_own_ref[...] = hidden[0]
    put_rows(sent_ref, width // x.shape[0], hidden[1])
    put(outs, dot(hidden[0], own_ref[2], FIRST) + dot(hidden[1], other_ref[2], FIRST))


def backward_kernel(pieces, own_ref, other_ref, fa_ref, fb_ref, *refs):
    ins, outs, refs = refs[:pieces], refs[pieces : 2 * pieces], refs[2 * pieces :]
    sent_ref, dgu_own_ref = refs
    rg = get(ins)
    put_columns(sent_ref, rg)
    units, width = own_ref.shape[1:]
    both = []
    for w_ref, first in ((own_ref, 0), (other_ref, units)):
        at = slice(first, first + units)
        dh = dot(w_ref[2], rg, LAST)
        dg = (dh * fa_ref[at, :].astype(F32)).astype(BF16)
        du = (dh * fb_ref[at, :].astype(F32)).astype(BF16)
        both.append(jnp.concatenate([dg, du], axis=0))
    dgu_own_ref[...] = both[0]
    put_rows(sent_ref, width // rg.shape[0], both[1])
    put(
        outs,
        dot(both[0], own_ref[0:2].reshape(2 * units, width), FIRST)
        + dot(both[1], other_ref[0:2].reshape(2 * units, width), FIRST),
    )


def near_sum_kernel(meta_ref, teacher_ref, *refs):
    ins, out_ref = refs[:-1], refs[-1]
    total = route_sums(meta_ref[...], ins)[-1]
    out_ref[...] = (total - teacher_ref[...].astype(F32)).astype(BF16)


def far_sum_kernel(meta_ref, *refs):
    ins, out_ref = refs[:-1], refs[-1]
    out_ref[...] = route_sums(meta_ref[...], ins)[-1].astype(BF16)


def far_grad_kernel(pieces, meta_ref, rest_ref, *refs):
    ins, d_gates_ref, outs = refs[:pieces], refs[pieces], refs[pieces + 1 :]
    m0, m1, g0, g1, o0, o1, total = route_sums(meta_ref[...], ins)
    diff = total + rest_ref[...].astype(F32)
    put_route_grads(outs, m0, m1, g0, g1, diff)
    put_d_gates(d_gates_ref, diff, o0, o1)


def near_grad_kernel(pieces, meta_ref, teacher_ref, part_ref, *refs):
    ins, student_ref, d_gates_ref, outs = (
        refs[:pieces],
        refs[pieces],
        refs[pieces + 1],
        refs[pieces + 2 :],
    )
    m0, m1, g0, g1, o0, o1, total = route_sums(meta_ref[...], ins)
    total = total + part_ref[...].astype(F32)
    student_ref[...] = total.astype(BF16)
    diff = total - teacher_ref[...].astype(F32)
    put_route_grads(outs, m0, m1, g0, g1, diff)
    put_d_gates(d_gates_ref, diff, o0, o1)


def far_back_kernel(meta_ref, d_gates_ref, *refs):
    ins, out_ref = refs[:-1], refs[-1]
    m0, m1 = masks_of(meta_ref[...], ins)
    tok = m0.shape[1]
    out_ref[:tok, :] = dot(m0 + m1, get(ins), FIRST).astype(BF16)
    value = d_gates_ref[...]
    high = value.astype(BF16)
    low = (value - high.astype(F32)).astype(BF16)
    rest = jnp.zeros((out_ref.shape[0] - tok - 4, tok), BF16)
    out_ref[tok:, :tok] = jnp.concatenate([high, low, rest], axis=0)
    out_ref[tok:, tok:] = jnp.zeros((out_ref.shape[0] - tok, out_ref.shape[1] - tok), BF16)


def final_kernel(pieces, meta_ref, part_ref, near_ref, *refs):
    ins, out_ref, d_gates_ref = refs[:pieces], refs[pieces], refs[pieces + 1]
    m0, m1 = masks_of(meta_ref[...], ins)
    tok = m0.shape[1]
    total = dot(m0 + m1, get(ins), FIRST) + part_ref[:tok, :].astype(F32)
    out_ref[...] = total.astype(BF16)
    far = part_ref[tok:, :tok].astype(F32)
    d_gates_ref[...] = near_ref[...] + (far[0:2] + far[2:4])


def weight_kernel(*refs):
    refs, out_ref, finished_ref = refs[:-2], refs[-2], refs[-1]
    xs = jnp.concatenate([get_columns(r) for r in refs[0:4]], axis=0)
    rgs = jnp.concatenate([get_columns(r) for r in refs[4:8]], axis=0)
    finished_ref[...] = jnp.zeros_like(finished_ref)
    for m, rows in enumerate((xs, xs, rgs)):
        acts = [
            ref[0] if len(ref.shape) == 3 else ref[...] for ref in refs[8 + 4 * m : 12 + 4 * m]
        ]
        out_ref[m] = dot(jnp.concatenate(acts, axis=1), rows).astype(BF16)


def local(tokens, teacher, routes, gate_weights, weights):
    tok, width = tokens.shape
    experts = lax.axis_size("expert")
    half = experts // 2
    capacity = 4 * tok // experts
    rows = half * capacity
    units = weights.shape[1]

    pieces = [jax.ShapeDtypeStruct((capacity, width), BF16)] * half
    dense = jax.ShapeDtypeStruct((tok, width), BF16)
    longer = jax.ShapeDtypeStruct((tok + 16, width), BF16)
    pair = jax.ShapeDtypeStruct((2, tok), F32)
    acts = jax.ShapeDtypeStruct((units, rows), BF16)
    across, along = width // rows, units // rows
    sent_x = jax.ShapeDtypeStruct((across + along, rows, rows), BF16)
    sent_g = jax.ShapeDtypeStruct((across + 2 * along, rows, rows), BF16)
    acts2 = jax.ShapeDtypeStruct((2 * units, rows), BF16)
    vspec = pl.BlockSpec(memory_space=pltpu.VMEM)
    aspec = pl.BlockSpec(memory_space=pl.ANY)
    matmul = 4 * rows * width * units

    def call(
        kernel,
        name,
        out_shape,
        specs,
        *args,
        after=(),
        through=(),
        flops=10**8,
        limit=8,
        scratch=(),
    ):
        many = isinstance(out_shape, list)
        specs = list(specs) + [vspec] * (len(args) - len(specs))
        inputs = len(args) + len(after) + len(through)
        outputs = len(out_shape) if many else 1

        def body(*refs):
            kernel(
                *refs[: len(args)],
                *refs[inputs : inputs + outputs],
                *refs[inputs + outputs + len(through) :],
            )

        out_specs = [vspec] * outputs + [aspec] * len(through)
        out_shapes = (out_shape if many else [out_shape]) + [
            jax.ShapeDtypeStruct(a.shape, a.dtype) for a in through
        ]
        single = not many and not through
        return pl.pallas_call(
            body,
            in_specs=specs + [aspec] * (len(after) + len(through)),
            out_specs=out_specs[0] if single else out_specs,
            out_shape=out_shapes[0] if single else out_shapes,
            input_output_aliases={
                len(args) + len(after) + i: outputs + i for i in range(len(through))
            },
            scratch_shapes=scratch,
            cost_estimate=pl.CostEstimate(
                flops=flops, bytes_accessed=2 * MIB, transcendentals=0
            ),
            compiler_params=pltpu.CompilerParams(vmem_limit_bytes=limit * MIB),
            name=name,
        )(*args, *after, *through)

    def within_half(rows_of):
        got = [rows_of[0]] + [None] * (half - 1)
        for s in range(1, half):
            got[s] = lax.ppermute(rows_of[s], "expert", [(i, i ^ s) for i in range(experts)])
        return got

    def to_mirror(x):
        return lax.ppermute(x, "expert", [(i, i ^ half) for i in range(experts)])

    def to_sibling(x):
        return lax.ppermute(x, "dp", [(0, 1), (1, 0)])

    far_tokens = to_mirror(tokens)
    own = weights[0].transpose(1, 0, 2)
    other = to_sibling(own)

    def forward(x_pieces, name, after=()):
        res = call(
            functools.partial(forward_kernel, half),
            name,
            pieces + [sent_x, acts, acts2, acts2],
            [],
            own,
            other,
            *x_pieces,
            after=after,
            flops=3 * matmul,
            limit=20,
        )
        return res[:half], res[half:]

    def backward(rg_pieces, fa, fb, name, after=(), through=()):
        res = call(
            functools.partial(backward_kernel, half),
            name,
            pieces + [sent_g, acts2],
            [],
            own,
            other,
            fa,
            fb,
            *rg_pieces,
            after=after,
            through=through,
            flops=3 * matmul,
            limit=20,
        )
        return res[:half], res[half:]

    res = call(
        pack_near_kernel,
        "pack_near",
        [jax.ShapeDtypeStruct((8, tok), F32)] + pieces,
        [],
        routes.T,
        gate_weights.T,
        tokens,
        limit=10,
    )
    meta, x_near = res[0], within_half(res[1:])
    far_meta = to_mirror(meta)
    x_far = within_half(
        call(pack_far_kernel, "pack_far", pieces, [], far_meta, far_tokens)
    )

    out_near, (xn, hn, fan, fbn) = forward(x_near, "forward_near")
    got_near = within_half(out_near)
    rest_rows = call(
        near_sum_kernel, "near_sum", dense, [], meta, teacher, *got_near
    )
    rest = to_mirror(rest_rows)
    out_far, (xf, hf, faf, fbf) = forward(x_far, "forward_far")
    got_far = within_half(out_far)
    xf_sib, xn_sib = to_sibling(xf), to_sibling(xn)
    far_rows = call(far_sum_kernel, "far_sum", dense, [], far_meta, *got_far)
    part = to_mirror(far_rows)

    res = call(
        functools.partial(far_grad_kernel, half),
        "far_grad",
        [pair] + pieces,
        [],
        far_meta,
        rest,
        *got_far,
        after=[far_rows],
    )
    d_gates_far, rg_far = res[0], within_half(res[1:])
    res = call(
        functools.partial(near_grad_kernel, half),
        "near_grad",
        [dense, pair] + pieces,
        [],
        meta,
        teacher,
        part,
        *got_near,
    )
    student, d_gates_near, rg_near = res[0], res[1], within_half(res[2:])

    grad_far, (gf, df) = backward(rg_far, faf, fbf, "backward_far", after=[xf_sib, xn_sib])
    back_far = within_half(grad_far)
    grad_near, (gn, dn) = backward(rg_near, fan, fbn, "backward_near", after=back_far[1:])
    gf_sib, gn_sib = to_sibling(gf), to_sibling(gn)
    part_rows, *grad_near = call(
        far_back_kernel,
        "far_back",
        longer,
        [],
        far_meta,
        d_gates_far,
        *back_far,
        through=grad_near,
    )
    part = to_mirror(part_rows)
    back_near = within_half(grad_near)

    chunk, steps = rows, along
    columns = pl.BlockSpec((across, rows, rows), lambda i: (0, 0, 0))
    part_of = lambda first: pl.BlockSpec((1, rows, rows), lambda i: (across + first + i, 0, 0))
    block = lambda first: pl.BlockSpec((chunk, rows), lambda i: (first + i, 0))
    specs = [columns] * 8
    for first in (0, steps, 0):
        specs += [block(first)] * 2 + [part_of(first)] * 2
    weight_grads, finished = pl.pallas_call(
        weight_kernel,
        grid=(steps,),
        in_specs=specs,
        out_specs=[
            pl.BlockSpec((3, chunk, width), lambda i: (0, i, 0)),
            pl.BlockSpec((8, 128), lambda i: (0, 0)),
        ],
        out_shape=[
            jax.ShapeDtypeStruct((3, units, width), BF16),
            jax.ShapeDtypeStruct((8, 128), F32),
        ],
        cost_estimate=pl.CostEstimate(
            flops=3 * matmul * 2, bytes_accessed=16 * MIB, transcendentals=0
        ),
        compiler_params=pltpu.CompilerParams(vmem_limit_bytes=20 * MIB),
        name="weight_gradients",
    )(
        *(xf, xn, xf_sib, xn_sib),
        *(gf, gn, gf_sib, gn_sib),
        *(df, dn, gf_sib, gn_sib),
        *(df, dn, gf_sib, gn_sib),
        *(hf, hn, xf_sib, xn_sib),
    )

    d_tokens, d_gates = call(
        functools.partial(final_kernel, half),
        "combine_gradients",
        [dense, pair],
        [],
        meta,
        part,
        d_gates_near,
        *back_near,
        after=[finished],
    )
    return (student, d_tokens, d_gates.T, weight_grads.transpose(1, 0, 2)[None])


def solution(mesh):
    rows = P(("groups", "expert", "dp"), None)
    return jax.shard_map(
        local,
        mesh=mesh,
        in_specs=(rows, rows, rows, rows, P("expert", "dp", None, None)),
        out_specs=(rows, rows, rows, P(("groups", "expert"), "dp", None, None)),
        check_vma=False,
    )
```

```python
import functools

import jax
import jax.numpy as jnp
from jax import lax
from jax.experimental import pallas as pl
from jax.experimental.pallas import tpu as pltpu
from jax.sharding import PartitionSpec as P

PLAIN = (((1,), (0,)), ((), ()))
LAST = (((1,), (1,)), ((), ()))
FIRST = (((0,), (0,)), ((), ()))
MIB = 1024 * 1024
F32 = jnp.float32
BF16 = jnp.bfloat16


def dot(a, b, dims=PLAIN):
    return lax.dot_general(a, b, dims, preferred_element_type=F32)


def slot_masks(me, meta, pieces, capacity):
    tok = meta.shape[1]
    expert_of = (lax.broadcasted_iota(jnp.int32, (pieces, tok), 0) ^ me).astype(F32)
    first, second = meta[0:1, :] == expert_of, meta[1:2, :] == expert_of
    chosen = jnp.where(first | second, 1.0, 0.0).astype(BF16)
    before = lax.broadcasted_iota(jnp.int32, (tok, tok), 0) < lax.broadcasted_iota(
        jnp.int32, (tok, tok), 1
    )
    rank = dot(chosen, jnp.where(before, 1.0, 0.0).astype(BF16))
    rank0 = jnp.where(first, rank, -1.0)
    rank1 = jnp.where(second, rank, -1.0)
    place = lax.broadcasted_iota(jnp.int32, (capacity, tok), 0).astype(F32)

    def expand(ranks):
        return jnp.concatenate(
            [
                jnp.where(ranks[s : s + 1, :] == place, 1.0, 0.0).astype(BF16)
                for s in range(pieces)
            ],
            axis=0,
        )

    return expand(rank0), expand(rank1)


def put(refs, rows):
    capacity = refs[0].shape[0]
    for s, ref in enumerate(refs):
        ref[...] = rows[s * capacity : (s + 1) * capacity].astype(ref.dtype)


def put_columns(ref, rows):
    side = rows.shape[0]
    for i in range(rows.shape[1] // side):
        ref[i] = rows[:, i * side : (i + 1) * side]


def put_rows(ref, first, value):
    side = value.shape[1]
    for i in range(value.shape[0] // side):
        ref[first + i] = value[i * side : (i + 1) * side, :]


def get_columns(ref):
    return jnp.concatenate([ref[i] for i in range(ref.shape[0])], axis=1)


def get(refs):
    return jnp.concatenate([ref[...] for ref in refs], axis=0)


def masks_of(meta, refs):
    return slot_masks(lax.axis_index("expert"), meta, len(refs), refs[0].shape[0])


def gate_columns(meta):
    columns = meta.T
    return columns[:, 2:3], columns[:, 3:4]


def route_sums(meta, refs):
    m0, m1 = masks_of(meta, refs)
    got = get(refs)
    g0, g1 = gate_columns(meta)
    o0, o1 = dot(m0, got, FIRST), dot(m1, got, FIRST)
    return m0, m1, g0, g1, o0, o1, g0 * o0 + g1 * o1


def put_d_gates(ref, diff, o0, o1):
    tok = diff.shape[0]
    lane = lax.broadcasted_iota(jnp.int32, (tok, 128), 1)
    d0 = jnp.sum(diff * o0, axis=1, keepdims=True)
    d1 = jnp.sum(diff * o1, axis=1, keepdims=True)
    ref[...] = jnp.where(lane == 0, d0, jnp.where(lane == 1, d1, 0.0)).T[0:2, :]


def put_route_grads(refs, m0, m1, g0, g1, diff):
    grads = jnp.concatenate([(g0 * diff).astype(BF16), (g1 * diff).astype(BF16)], axis=0)
    put(refs, dot(jnp.concatenate([m0, m1], axis=1), grads))


def pack_near_kernel(own_ref, routes_ref, gates_ref, tokens_ref, meta_ref, *rows_refs):
    del own_ref
    meta = jnp.concatenate(
        [
            routes_ref[...].astype(F32),
            gates_ref[...],
            jnp.zeros((4, routes_ref.shape[1]), F32),
        ],
        axis=0,
    )
    meta_ref[...] = meta
    m0, m1 = masks_of(meta, rows_refs)
    put(rows_refs, dot(m0 + m1, tokens_ref[...]))


def pack_far_kernel(meta_ref, tokens_ref, *rows_refs):
    m0, m1 = masks_of(meta_ref[...], rows_refs)
    put(rows_refs, dot(m0 + m1, tokens_ref[...]))


def forward_kernel(pieces, own_ref, other_ref, *refs):
    ins, outs, refs = refs[:pieces], refs[pieces : 2 * pieces], refs[2 * pieces :]
    sent_ref, hid_own_ref, fa_ref, fb_ref = refs
    x = get(ins)
    put_columns(sent_ref, x)
    units, width = other_ref.shape[1:]
    hidden = []
    for w_ref, first in ((own_ref, 0), (other_ref, units)):
        both = dot(w_ref[0:2].reshape(2 * units, width), x, LAST)
        gate, up = both[:units], both[units:]
        sig = 0.5 * jnp.tanh(0.5 * gate) + 0.5
        silu = gate * sig
        hidden.append((silu * up).astype(BF16))
        fa_ref[first : first + units, :] = (up * (sig + silu * (1.0 - sig))).astype(BF16)
        fb_ref[first : first + units, :] = silu.astype(BF16)
    hid_own_ref[...] = hidden[0]
    put_rows(sent_ref, width // x.shape[0], hidden[1])
    put(outs, dot(hidden[0], own_ref[2], FIRST) + dot(hidden[1], other_ref[2], FIRST))


def backward_kernel(pieces, own_ref, other_ref, fa_ref, fb_ref, *refs):
    ins, outs, refs = refs[:pieces], refs[pieces : 2 * pieces], refs[2 * pieces :]
    sent_ref, dgu_own_ref = refs
    rg = get(ins)
    put_columns(sent_ref, rg)
    units, width = own_ref.shape[1:]
    both = []
    for w_ref, first in ((own_ref, 0), (other_ref, units)):
        at = slice(first, first + units)
        dh = dot(w_ref[2], rg, LAST)
        dg = (dh * fa_ref[at, :].astype(F32)).astype(BF16)
        du = (dh * fb_ref[at, :].astype(F32)).astype(BF16)
        both.append(jnp.concatenate([dg, du], axis=0))
    dgu_own_ref[...] = both[0]
    put_rows(sent_ref, width // rg.shape[0], both[1])
    put(
        outs,
        dot(both[0], own_ref[0:2].reshape(2 * units, width), FIRST)
        + dot(both[1], other_ref[0:2].reshape(2 * units, width), FIRST),
    )


def near_sum_kernel(meta_ref, teacher_ref, *refs):
    ins, out_ref = refs[:-1], refs[-1]
    total = route_sums(meta_ref[...], ins)[-1]
    out_ref[...] = (total - teacher_ref[...].astype(F32)).astype(BF16)


def far_grad_kernel(pieces, meta_ref, rest_ref, *refs):
    ins, part_ref, d_gates_ref, outs = (
        refs[:pieces],
        refs[pieces],
        refs[pieces + 1],
        refs[pieces + 2 :],
    )
    m0, m1, g0, g1, o0, o1, total = route_sums(meta_ref[...], ins)
    part_ref[...] = total.astype(BF16)
    diff = total + rest_ref[...].astype(F32)
    put_route_grads(outs, m0, m1, g0, g1, diff)
    put_d_gates(d_gates_ref, diff, o0, o1)


def near_grad_kernel(pieces, meta_ref, teacher_ref, part_ref, *refs):
    ins, student_ref, d_gates_ref, outs = (
        refs[:pieces],
        refs[pieces],
        refs[pieces + 1],
        refs[pieces + 2 :],
    )
    m0, m1, g0, g1, o0, o1, total = route_sums(meta_ref[...], ins)
    total = total + part_ref[...].astype(F32)
    student_ref[...] = total.astype(BF16)
    diff = total - teacher_ref[...].astype(F32)
    put_route_grads(outs, m0, m1, g0, g1, diff)
    put_d_gates(d_gates_ref, diff, o0, o1)


def far_back_kernel(meta_ref, d_gates_ref, *refs):
    ins, out_ref = refs[:-1], refs[-1]
    m0, m1 = masks_of(meta_ref[...], ins)
    tok = m0.shape[1]
    out_ref[:tok, :] = dot(m0 + m1, get(ins), FIRST).astype(BF16)
    value = d_gates_ref[...]
    high = value.astype(BF16)
    low = (value - high.astype(F32)).astype(BF16)
    rest = jnp.zeros((out_ref.shape[0] - tok - 4, tok), BF16)
    out_ref[tok:, :tok] = jnp.concatenate([high, low, rest], axis=0)
    out_ref[tok:, tok:] = jnp.zeros((out_ref.shape[0] - tok, out_ref.shape[1] - tok), BF16)


def final_kernel(pieces, meta_ref, part_ref, near_ref, *refs):
    ins, out_ref, d_gates_ref = refs[:pieces], refs[pieces], refs[pieces + 1]
    m0, m1 = masks_of(meta_ref[...], ins)
    tok = m0.shape[1]
    total = dot(m0 + m1, get(ins), FIRST) + part_ref[:tok, :].astype(F32)
    out_ref[...] = total.astype(BF16)
    far = part_ref[tok:, :tok].astype(F32)
    d_gates_ref[...] = near_ref[...] + (far[0:2] + far[2:4])


def weight_kernel(*refs):
    refs, out_ref, finished_ref = refs[:-2], refs[-2], refs[-1]
    xs = jnp.concatenate([get_columns(r) for r in refs[0:4]], axis=0)
    rgs = jnp.concatenate([get_columns(r) for r in refs[4:8]], axis=0)
    finished_ref[...] = jnp.zeros_like(finished_ref)
    for m, rows in enumerate((xs, xs, rgs)):
        acts = [
            ref[0] if len(ref.shape) == 3 else ref[...] for ref in refs[8 + 4 * m : 12 + 4 * m]
        ]
        out_ref[m] = dot(jnp.concatenate(acts, axis=1), rows).astype(BF16)


def local(tokens, teacher, routes, gate_weights, weights):
    tok, width = tokens.shape
    experts = lax.axis_size("expert")
    half = experts // 2
    capacity = 4 * tok // experts
    rows = half * capacity
    units = weights.shape[1]

    pieces = [jax.ShapeDtypeStruct((capacity, width), BF16)] * half
    dense = jax.ShapeDtypeStruct((tok, width), BF16)
    longer = jax.ShapeDtypeStruct((tok + 16, width), BF16)
    pair = jax.ShapeDtypeStruct((2, tok), F32)
    acts = jax.ShapeDtypeStruct((units, rows), BF16)
    across, along = width // rows, units // rows
    sent_x = jax.ShapeDtypeStruct((across + along, rows, rows), BF16)
    sent_g = jax.ShapeDtypeStruct((across + 2 * along, rows, rows), BF16)
    acts2 = jax.ShapeDtypeStruct((2 * units, rows), BF16)
    vspec = pl.BlockSpec(memory_space=pltpu.VMEM)
    aspec = pl.BlockSpec(memory_space=pl.ANY)
    matmul = 4 * rows * width * units

    def call(
        kernel,
        name,
        out_shape,
        specs,
        *args,
        after=(),
        through=(),
        flops=10**8,
        limit=8,
        scratch=(),
    ):
        many = isinstance(out_shape, list)
        specs = list(specs) + [vspec] * (len(args) - len(specs))
        inputs = len(args) + len(after) + len(through)
        outputs = len(out_shape) if many else 1

        def body(*refs):
            kernel(
                *refs[: len(args)],
                *refs[inputs : inputs + outputs],
                *refs[inputs + outputs + len(through) :],
            )

        out_specs = [vspec] * outputs + [aspec] * len(through)
        out_shapes = (out_shape if many else [out_shape]) + [
            jax.ShapeDtypeStruct(a.shape, a.dtype) for a in through
        ]
        single = not many and not through
        return pl.pallas_call(
            body,
            in_specs=specs + [aspec] * (len(after) + len(through)),
            out_specs=out_specs[0] if single else out_specs,
            out_shape=out_shapes[0] if single else out_shapes,
            input_output_aliases={
                len(args) + len(after) + i: outputs + i for i in range(len(through))
            },
            scratch_shapes=scratch,
            cost_estimate=pl.CostEstimate(
                flops=flops, bytes_accessed=2 * MIB, transcendentals=0
            ),
            compiler_params=pltpu.CompilerParams(vmem_limit_bytes=limit * MIB),
            name=name,
        )(*args, *after, *through)

    def within_half(rows_of):
        got = [rows_of[0]] + [None] * (half - 1)
        for s in range(1, half):
            got[s] = lax.ppermute(rows_of[s], "expert", [(i, i ^ s) for i in range(experts)])
        return got

    def to_mirror(x):
        return lax.ppermute(x, "expert", [(i, i ^ half) for i in range(experts)])

    def to_sibling(x):
        return lax.ppermute(x, "dp", [(0, 1), (1, 0)])

    far_tokens = to_mirror(tokens)
    own = weights[0].transpose(1, 0, 2)
    other = to_sibling(own)

    def forward(x_pieces, name, after=()):
        res = call(
            functools.partial(forward_kernel, half),
            name,
            pieces + [sent_x, acts, acts2, acts2],
            [],
            own,
            other,
            *x_pieces,
            after=after,
            flops=3 * matmul,
            limit=20,
        )
        return res[:half], res[half:]

    def backward(rg_pieces, fa, fb, name, after=(), through=()):
        res = call(
            functools.partial(backward_kernel, half),
            name,
            pieces + [sent_g, acts2],
            [],
            own,
            other,
            fa,
            fb,
            *rg_pieces,
            after=after,
            through=through,
            flops=3 * matmul,
            limit=20,
        )
        return res[:half], res[half:]

    res = call(
        pack_near_kernel,
        "pack_near",
        [jax.ShapeDtypeStruct((8, tok), F32)] + pieces,
        [],
        own,
        routes.T,
        gate_weights.T,
        tokens,
        limit=10,
    )
    meta, x_near = res[0], within_half(res[1:])
    far_meta = to_mirror(meta)
    x_far = within_half(
        call(pack_far_kernel, "pack_far", pieces, [], far_meta, far_tokens)
    )

    out_near, (xn, hn, fan, fbn) = forward(x_near, "forward_near")
    got_near = within_half(out_near)
    out_far, (xf, hf, faf, fbf) = forward(x_far, "forward_far", after=[xn])
    rest_rows, *out_far = call(
        near_sum_kernel,
        "near_sum",
        dense,
        [],
        meta,
        teacher,
        *got_near,
        through=out_far,
    )
    rest = to_mirror(rest_rows)
    got_far = within_half(out_far)
    xf_sib, xn_sib = to_sibling(xf), to_sibling(xn)

    res = call(
        functools.partial(far_grad_kernel, half),
        "far_grad",
        [dense, pair] + pieces,
        [],
        far_meta,
        rest,
        *got_far,
        after=[xf_sib, xn_sib],
    )
    part, d_gates_far, rg_far = to_mirror(res[0]), res[1], within_half(res[2:])
    res = call(
        functools.partial(near_grad_kernel, half),
        "near_grad",
        [dense, pair] + pieces,
        [],
        meta,
        teacher,
        part,
        *got_near,
    )
    student, d_gates_near, rg_near = res[0], res[1], within_half(res[2:])

    grad_far, (gf, df) = backward(rg_far, faf, fbf, "backward_far")
    back_far = within_half(grad_far)
    grad_near, (gn, dn) = backward(rg_near, fan, fbn, "backward_near", after=back_far[1:])
    gf_sib, gn_sib = to_sibling(gf), to_sibling(gn)
    part_rows, *grad_near = call(
        far_back_kernel,
        "far_back",
        longer,
        [],
        far_meta,
        d_gates_far,
        *back_far,
        through=grad_near,
    )
    part = to_mirror(part_rows)
    back_near = within_half(grad_near)

    chunk, steps = rows, along
    columns = pl.BlockSpec((across, rows, rows), lambda i: (0, 0, 0))
    part_of = lambda first: pl.BlockSpec((1, rows, rows), lambda i: (across + first + i, 0, 0))
    block = lambda first: pl.BlockSpec((chunk, rows), lambda i: (first + i, 0))
    specs = [columns] * 8
    for first in (0, steps, 0):
        specs += [block(first)] * 2 + [part_of(first)] * 2
    weight_grads, finished = pl.pallas_call(
        weight_kernel,
        grid=(steps,),
        in_specs=specs,
        out_specs=[
            pl.BlockSpec((3, chunk, width), lambda i: (0, i, 0)),
            pl.BlockSpec((8, 128), lambda i: (0, 0)),
        ],
        out_shape=[
            jax.ShapeDtypeStruct((3, units, width), BF16),
            jax.ShapeDtypeStruct((8, 128), F32),
        ],
        cost_estimate=pl.CostEstimate(
            flops=3 * matmul * 2, bytes_accessed=16 * MIB, transcendentals=0
        ),
        compiler_params=pltpu.CompilerParams(vmem_limit_bytes=20 * MIB),
        name="weight_gradients",
    )(
        *(xf, xn, xf_sib, xn_sib),
        *(gf, gn, gf_sib, gn_sib),
        *(df, dn, gf_sib, gn_sib),
        *(df, dn, gf_sib, gn_sib),
        *(hf, hn, xf_sib, xn_sib),
    )

    d_tokens, d_gates = call(
        functools.partial(final_kernel, half),
        "combine_gradients",
        [dense, pair],
        [],
        meta,
        part,
        d_gates_near,
        *back_near,
        after=[finished],
    )
    return (student, d_tokens, d_gates.T, weight_grads.transpose(1, 0, 2)[None])


def solution(mesh):
    rows = P(("groups", "expert", "dp"), None)
    return jax.shard_map(
        local,
        mesh=mesh,
        in_specs=(rows, rows, rows, rows, P("expert", "dp", None, None)),
        out_specs=(rows, rows, rows, P(("groups", "expert"), "dp", None, None)),
        check_vma=False,
    )
```

```python
import functools

import jax
import jax.numpy as jnp
from jax import lax
from jax.experimental import pallas as pl
from jax.experimental.pallas import tpu as pltpu
from jax.sharding import PartitionSpec as P

PLAIN = (((1,), (0,)), ((), ()))
LAST = (((1,), (1,)), ((), ()))
FIRST = (((0,), (0,)), ((), ()))
MIB = 1024 * 1024
F32 = jnp.float32
BF16 = jnp.bfloat16
FLOPS = {
    "pack_near": 30000000000,
    "pack_far": 30000000000,
    "forward_near": 100000000,
    "forward_far": 3000000000,
    "near_sum": 30000000000,
    "far_grad": 10000000000,
    "near_grad": 30000000000,
    "backward_far": 3000000000,
    "backward_near": 10000000000,
    "far_back": 1000000000,
    "weight_gradients": 30000000000,
    "combine_gradients": 30000000000,
}


def dot(a, b, dims=PLAIN):
    return lax.dot_general(a, b, dims, preferred_element_type=F32)


def slot_masks(me, meta, pieces, capacity):
    tok = meta.shape[1]
    expert_of = (lax.broadcasted_iota(jnp.int32, (pieces, tok), 0) ^ me).astype(F32)
    first, second = meta[0:1, :] == expert_of, meta[1:2, :] == expert_of
    chosen = jnp.where(first | second, 1.0, 0.0).astype(BF16)
    before = lax.broadcasted_iota(jnp.int32, (tok, tok), 0) < lax.broadcasted_iota(
        jnp.int32, (tok, tok), 1
    )
    rank = dot(chosen, jnp.where(before, 1.0, 0.0).astype(BF16))
    rank0 = jnp.where(first, rank, -1.0)
    rank1 = jnp.where(second, rank, -1.0)
    place = lax.broadcasted_iota(jnp.int32, (capacity, tok), 0).astype(F32)

    def expand(ranks):
        return jnp.concatenate(
            [
                jnp.where(ranks[s : s + 1, :] == place, 1.0, 0.0).astype(BF16)
                for s in range(pieces)
            ],
            axis=0,
        )

    return expand(rank0), expand(rank1)


def put(refs, rows):
    capacity = refs[0].shape[0]
    for s, ref in enumerate(refs):
        ref[...] = rows[s * capacity : (s + 1) * capacity].astype(ref.dtype)


def put_columns(ref, rows):
    side = rows.shape[0]
    for i in range(rows.shape[1] // side):
        ref[i] = rows[:, i * side : (i + 1) * side]


def put_rows(ref, first, value):
    side = value.shape[1]
    for i in range(value.shape[0] // side):
        ref[first + i] = value[i * side : (i + 1) * side, :]


def get_columns(ref):
    return jnp.concatenate([ref[i] for i in range(ref.shape[0])], axis=1)


def get(refs):
    return jnp.concatenate([ref[...] for ref in refs], axis=0)


def masks_of(meta, refs):
    return slot_masks(lax.axis_index("expert"), meta, len(refs), refs[0].shape[0])


def gate_columns(meta):
    columns = meta.T
    return columns[:, 2:3], columns[:, 3:4]


def route_sums(meta, refs):
    m0, m1 = masks_of(meta, refs)
    got = get(refs)
    g0, g1 = gate_columns(meta)
    o0, o1 = dot(m0, got, FIRST), dot(m1, got, FIRST)
    return m0, m1, g0, g1, o0, o1, g0 * o0 + g1 * o1


def put_d_gates(ref, diff, o0, o1):
    tok = diff.shape[0]
    lane = lax.broadcasted_iota(jnp.int32, (tok, 128), 1)
    d0 = jnp.sum(diff * o0, axis=1, keepdims=True)
    d1 = jnp.sum(diff * o1, axis=1, keepdims=True)
    ref[...] = jnp.where(lane == 0, d0, jnp.where(lane == 1, d1, 0.0)).T[0:2, :]


def put_route_grads(refs, m0, m1, g0, g1, diff):
    grads = jnp.concatenate([(g0 * diff).astype(BF16), (g1 * diff).astype(BF16)], axis=0)
    put(refs, dot(jnp.concatenate([m0, m1], axis=1), grads))


def pack_near_kernel(own_ref, routes_ref, gates_ref, tokens_ref, meta_ref, *rows_refs):
    del own_ref
    meta = jnp.concatenate(
        [
            routes_ref[...].astype(F32),
            gates_ref[...],
            jnp.zeros((4, routes_ref.shape[1]), F32),
        ],
        axis=0,
    )
    meta_ref[...] = meta
    m0, m1 = masks_of(meta, rows_refs)
    put(rows_refs, dot(m0 + m1, tokens_ref[...]))


def pack_far_kernel(meta_ref, tokens_ref, *rows_refs):
    m0, m1 = masks_of(meta_ref[...], rows_refs)
    put(rows_refs, dot(m0 + m1, tokens_ref[...]))


def forward_kernel(pieces, own_ref, other_ref, *refs):
    ins, outs, refs = refs[:pieces], refs[pieces : 2 * pieces], refs[2 * pieces :]
    sent_ref, hid_own_ref, fa_ref, fb_ref = refs
    x = get(ins)
    put_columns(sent_ref, x)
    units, width = other_ref.shape[1:]
    hidden = []
    for w_ref, first in ((own_ref, 0), (other_ref, units)):
        both = dot(w_ref[0:2].reshape(2 * units, width), x, LAST)
        gate, up = both[:units], both[units:]
        sig = 0.5 * jnp.tanh(0.5 * gate) + 0.5
        silu = gate * sig
        hidden.append((silu * up).astype(BF16))
        fa_ref[first : first + units, :] = (up * (sig + silu * (1.0 - sig))).astype(BF16)
        fb_ref[first : first + units, :] = silu.astype(BF16)
    hid_own_ref[...] = hidden[0]
    put_rows(sent_ref, width // x.shape[0], hidden[1])
    put(outs, dot(hidden[0], own_ref[2], FIRST) + dot(hidden[1], other_ref[2], FIRST))


def backward_kernel(pieces, own_ref, other_ref, fa_ref, fb_ref, *refs):
    ins, outs, refs = refs[:pieces], refs[pieces : 2 * pieces], refs[2 * pieces :]
    sent_ref, dgu_own_ref = refs
    rg = get(ins)
    put_columns(sent_ref, rg)
    units, width = own_ref.shape[1:]
    both = []
    for w_ref, first in ((own_ref, 0), (other_ref, units)):
        at = slice(first, first + units)
        dh = dot(w_ref[2], rg, LAST)
        dg = (dh * fa_ref[at, :].astype(F32)).astype(BF16)
        du = (dh * fb_ref[at, :].astype(F32)).astype(BF16)
        both.append(jnp.concatenate([dg, du], axis=0))
    dgu_own_ref[...] = both[0]
    put_rows(sent_ref, width // rg.shape[0], both[1])
    put(
        outs,
        dot(both[0], own_ref[0:2].reshape(2 * units, width), FIRST)
        + dot(both[1], other_ref[0:2].reshape(2 * units, width), FIRST),
    )


def near_sum_kernel(meta_ref, teacher_ref, *refs):
    ins, out_ref = refs[:-1], refs[-1]
    total = route_sums(meta_ref[...], ins)[-1]
    out_ref[...] = (total - teacher_ref[...].astype(F32)).astype(BF16)


def far_grad_kernel(pieces, meta_ref, rest_ref, *refs):
    ins, part_ref, d_gates_ref, outs = (
        refs[:pieces],
        refs[pieces],
        refs[pieces + 1],
        refs[pieces + 2 :],
    )
    m0, m1, g0, g1, o0, o1, total = route_sums(meta_ref[...], ins)
    part_ref[...] = total.astype(BF16)
    diff = total + rest_ref[...].astype(F32)
    put_route_grads(outs, m0, m1, g0, g1, diff)
    put_d_gates(d_gates_ref, diff, o0, o1)


def near_grad_kernel(pieces, meta_ref, teacher_ref, part_ref, *refs):
    ins, student_ref, d_gates_ref, outs = (
        refs[:pieces],
        refs[pieces],
        refs[pieces + 1],
        refs[pieces + 2 :],
    )
    m0, m1, g0, g1, o0, o1, total = route_sums(meta_ref[...], ins)
    total = total + part_ref[...].astype(F32)
    student_ref[...] = total.astype(BF16)
    diff = total - teacher_ref[...].astype(F32)
    put_route_grads(outs, m0, m1, g0, g1, diff)
    put_d_gates(d_gates_ref, diff, o0, o1)


def far_back_kernel(meta_ref, d_gates_ref, *refs):
    ins, out_ref = refs[:-1], refs[-1]
    m0, m1 = masks_of(meta_ref[...], ins)
    tok = m0.shape[1]
    out_ref[:tok, :] = dot(m0 + m1, get(ins), FIRST).astype(BF16)
    value = d_gates_ref[...]
    high = value.astype(BF16)
    low = (value - high.astype(F32)).astype(BF16)
    rest = jnp.zeros((out_ref.shape[0] - tok - 4, tok), BF16)
    out_ref[tok:, :tok] = jnp.concatenate([high, low, rest], axis=0)
    out_ref[tok:, tok:] = jnp.zeros((out_ref.shape[0] - tok, out_ref.shape[1] - tok), BF16)


def final_kernel(pieces, meta_ref, part_ref, near_ref, *refs):
    ins, out_ref, d_gates_ref = refs[:pieces], refs[pieces], refs[pieces + 1]
    m0, m1 = masks_of(meta_ref[...], ins)
    tok = m0.shape[1]
    total = dot(m0 + m1, get(ins), FIRST) + part_ref[:tok, :].astype(F32)
    out_ref[...] = total.astype(BF16)
    far = part_ref[tok:, :tok].astype(F32)
    d_gates_ref[...] = near_ref[...] + (far[0:2] + far[2:4])


def weight_kernel(across, *refs):
    (xf, xn, xfs, xns, gf, gn, gfs, gns, df, dn, hf, hn, out_hbm, finished, buf, sems) = refs
    finished[...] = jnp.zeros_like(finished)
    units = hf.shape[0]
    side = hf.shape[1]
    part = units // 2

    def columns(*sets):
        return jnp.concatenate(
            [jnp.concatenate([r[i] for i in range(across)], axis=1) for r in sets], axis=0
        )

    def acts(own, sent, first):
        blocks = range(across + first // side, across + (first + part) // side)
        theirs = [jnp.concatenate([r[i] for i in blocks], axis=0) for r in sent]
        return jnp.concatenate([r[first : first + part, :] for r in own] + theirs, axis=1)

    x, rg = columns(xf, xn, xfs, xns), columns(gf, gn, gfs, gns)
    copies = []
    for m, (own, sent, rows, offset) in enumerate(
        (
            ((df, dn), (gfs, gns), x, 0),
            ((df, dn), (gfs, gns), x, units),
            ((hf, hn), (xfs, xns), rg, 0),
        )
    ):
        for first in range(0, units, part):
            slot = len(copies) % 2
            if len(copies) > 1:
                copies[-2].wait()
            buf[slot] = dot(acts(own, sent, offset + first), rows).astype(BF16)
            copies.append(
                pltpu.make_async_copy(
                    buf.at[slot], out_hbm.at[m, pl.ds(first, part)], sems.at[slot]
                )
            )
            copies[-1].start()
    copies[-2].wait()
    copies[-1].wait()


def local(tokens, teacher, routes, gate_weights, weights):
    tok, width = tokens.shape
    experts = lax.axis_size("expert")
    half = experts // 2
    capacity = 4 * tok // experts
    rows = half * capacity
    units = weights.shape[1]

    pieces = [jax.ShapeDtypeStruct((capacity, width), BF16)] * half
    dense = jax.ShapeDtypeStruct((tok, width), BF16)
    longer = jax.ShapeDtypeStruct((tok + 16, width), BF16)
    pair = jax.ShapeDtypeStruct((2, tok), F32)
    acts = jax.ShapeDtypeStruct((units, rows), BF16)
    across, along = width // rows, units // rows
    sent_x = jax.ShapeDtypeStruct((across + along, rows, rows), BF16)
    sent_g = jax.ShapeDtypeStruct((across + 2 * along, rows, rows), BF16)
    acts2 = jax.ShapeDtypeStruct((2 * units, rows), BF16)
    vspec = pl.BlockSpec(memory_space=pltpu.VMEM)
    aspec = pl.BlockSpec(memory_space=pl.ANY)

    def call(
        kernel,
        name,
        out_shape,
        specs,
        *args,
        after=(),
        through=(),
        limit=8,
        scratch=(),
        in_hbm=0,
    ):
        many = isinstance(out_shape, list)
        specs = list(specs) + [vspec] * (len(args) - len(specs))
        inputs = len(args) + len(after) + len(through)
        outputs = len(out_shape) if many else 1

        def body(*refs):
            kernel(
                *refs[: len(args)],
                *refs[inputs : inputs + outputs],
                *refs[inputs + outputs + len(through) :],
            )

        out_specs = [aspec] * in_hbm + [vspec] * (outputs - in_hbm) + [aspec] * len(through)
        out_shapes = (out_shape if many else [out_shape]) + [
            jax.ShapeDtypeStruct(a.shape, a.dtype) for a in through
        ]
        single = not many and not through
        return pl.pallas_call(
            body,
            in_specs=specs + [aspec] * (len(after) + len(through)),
            out_specs=out_specs[0] if single else out_specs,
            out_shape=out_shapes[0] if single else out_shapes,
            input_output_aliases={
                len(args) + len(after) + i: outputs + i for i in range(len(through))
            },
            scratch_shapes=scratch,
            cost_estimate=pl.CostEstimate(
                flops=FLOPS.get(name, 10**8), bytes_accessed=2 * MIB, transcendentals=0
            ),
            compiler_params=pltpu.CompilerParams(vmem_limit_bytes=limit * MIB),
            name=name,
        )(*args, *after, *through)

    def within_half(rows_of):
        got = [rows_of[0]] + [None] * (half - 1)
        for s in range(1, half):
            got[s] = lax.ppermute(rows_of[s], "expert", [(i, i ^ s) for i in range(experts)])
        return got

    def to_mirror(x):
        return lax.ppermute(x, "expert", [(i, i ^ half) for i in range(experts)])

    def to_sibling(x):
        return lax.ppermute(x, "dp", [(0, 1), (1, 0)])

    far_tokens = to_mirror(tokens)
    own = weights[0].transpose(1, 0, 2)
    other = to_sibling(own)

    def forward(x_pieces, name, after=()):
        res = call(
            functools.partial(forward_kernel, half),
            name,
            pieces + [sent_x, acts, acts2, acts2],
            [],
            own,
            other,
            *x_pieces,
            after=after,
            limit=20,
        )
        return res[:half], res[half:]

    def backward(rg_pieces, fa, fb, name, after=(), through=()):
        res = call(
            functools.partial(backward_kernel, half),
            name,
            pieces + [sent_g, acts2],
            [],
            own,
            other,
            fa,
            fb,
            *rg_pieces,
            after=after,
            through=through,
            limit=20,
        )
        return res[:half], res[half:]

    res = call(
        pack_near_kernel,
        "pack_near",
        [jax.ShapeDtypeStruct((8, tok), F32)] + pieces,
        [],
        own,
        routes.T,
        gate_weights.T,
        tokens,
        limit=10,
    )
    meta, x_near = res[0], within_half(res[1:])
    far_meta = to_mirror(meta)
    x_far = within_half(
        call(pack_far_kernel, "pack_far", pieces, [], far_meta, far_tokens)
    )

    out_near, (xn, hn, fan, fbn) = forward(x_near, "forward_near")
    got_near = within_half(out_near)
    out_far, (xf, hf, faf, fbf) = forward(x_far, "forward_far", after=[xn])
    rest_rows, *out_far = call(
        near_sum_kernel,
        "near_sum",
        dense,
        [],
        meta,
        teacher,
        *got_near,
        through=out_far,
    )
    rest = to_mirror(rest_rows)
    got_far = within_half(out_far)
    xf_sib, xn_sib = to_sibling(xf), to_sibling(xn)

    res = call(
        functools.partial(far_grad_kernel, half),
        "far_grad",
        [dense, pair] + pieces,
        [],
        far_meta,
        rest,
        *got_far,
        after=[xf_sib, xn_sib],
    )
    part, d_gates_far, rg_far = to_mirror(res[0]), res[1], within_half(res[2:])
    grad_far, (gf, df) = backward(rg_far, faf, fbf, "backward_far")
    res = call(
        functools.partial(near_grad_kernel, half),
        "near_grad",
        [dense, pair] + pieces,
        [],
        meta,
        teacher,
        part,
        *got_near,
        after=[df],
    )
    student, d_gates_near, rg_near = res[0], res[1], within_half(res[2:])

    back_far = within_half(grad_far)
    part_rows = call(
        far_back_kernel, "far_back", longer, [], far_meta, d_gates_far, *back_far
    )
    part = to_mirror(part_rows)
    grad_near, (gn, dn) = backward(rg_near, fan, fbn, "backward_near", after=[part_rows])
    gf_sib, gn_sib = to_sibling(gf), to_sibling(gn)
    back_near = within_half(grad_near)

    weight_grads, finished = call(
        functools.partial(weight_kernel, across),
        "weight_gradients",
        [
            jax.ShapeDtypeStruct((3, units, width), BF16),
            jax.ShapeDtypeStruct((8, 128), F32),
        ],
        [],
        *(xf, xn, xf_sib, xn_sib),
        *(gf, gn, gf_sib, gn_sib),
        *(df, dn, hf, hn),
        after=[],
        limit=24,
        scratch=[
            pltpu.VMEM((2, units // 2, width), BF16),
            pltpu.SemaphoreType.DMA((2,)),
        ],
        in_hbm=1,
    )

    d_tokens, d_gates = call(
        functools.partial(final_kernel, half),
        "combine_gradients",
        [dense, pair],
        [],
        meta,
        part,
        d_gates_near,
        *back_near,
        after=[finished],
    )
    return (student, d_tokens, d_gates.T, weight_grads.transpose(1, 0, 2)[None])


def solution(mesh):
    rows = P(("groups", "expert", "dp"), None)
    return jax.shard_map(
        local,
        mesh=mesh,
        in_specs=(rows, rows, rows, rows, P("expert", "dp", None, None)),
        out_specs=(rows, rows, rows, P(("groups", "expert"), "dp", None, None)),
        check_vma=False,
    )
```

```python
import functools

import jax
import jax.numpy as jnp
from jax import lax
from jax.experimental import pallas as pl
from jax.experimental.pallas import tpu as pltpu
from jax.sharding import PartitionSpec as P

PLAIN = (((1,), (0,)), ((), ()))
LAST = (((1,), (1,)), ((), ()))
FIRST = (((0,), (0,)), ((), ()))
MIB = 1024 * 1024
F32 = jnp.float32
BF16 = jnp.bfloat16
FLOPS = {
    "pack_near": 30000000000,
    "pack_far": 30000000000,
    "forward_near": 100000000,
    "forward_far": 3000000000,
    "near_sum": 30000000000,
    "far_grad": 10000000000,
    "near_grad": 30000000000,
    "backward_far": 3000000000,
    "backward_near": 10000000000,
    "far_back": 1000000000,
    "weight_gradients": 30000000000,
    "combine_gradients": 30000000000,
}


def dot(a, b, dims=PLAIN):
    return lax.dot_general(a, b, dims, preferred_element_type=F32)


def slot_masks(me, meta, pieces, capacity):
    tok = meta.shape[1]
    expert_of = (lax.broadcasted_iota(jnp.int32, (pieces, tok), 0) ^ me).astype(F32)
    first, second = meta[0:1, :] == expert_of, meta[1:2, :] == expert_of
    chosen = jnp.where(first | second, 1.0, 0.0).astype(BF16)
    before = lax.broadcasted_iota(jnp.int32, (tok, tok), 0) < lax.broadcasted_iota(
        jnp.int32, (tok, tok), 1
    )
    rank = dot(chosen, jnp.where(before, 1.0, 0.0).astype(BF16))
    rank0 = jnp.where(first, rank, -1.0)
    rank1 = jnp.where(second, rank, -1.0)
    place = lax.broadcasted_iota(jnp.int32, (capacity, tok), 0).astype(F32)

    def expand(ranks):
        return jnp.concatenate(
            [
                jnp.where(ranks[s : s + 1, :] == place, 1.0, 0.0).astype(BF16)
                for s in range(pieces)
            ],
            axis=0,
        )

    return expand(rank0), expand(rank1)


def put(refs, rows):
    capacity = refs[0].shape[0]
    for s, ref in enumerate(refs):
        ref[...] = rows[s * capacity : (s + 1) * capacity].astype(ref.dtype)


def put_columns(ref, rows):
    side = rows.shape[0]
    for i in range(rows.shape[1] // side):
        ref[i] = rows[:, i * side : (i + 1) * side]


def put_rows(ref, first, value):
    side = value.shape[1]
    for i in range(value.shape[0] // side):
        ref[first + i] = value[i * side : (i + 1) * side, :]


def get_columns(ref):
    return jnp.concatenate([ref[i] for i in range(ref.shape[0])], axis=1)


def get(refs):
    refs = refs[:1] + refs[:0:-1]
    return jnp.concatenate([ref[...] for ref in refs], axis=0)


def masks_of(meta, refs):
    return slot_masks(lax.axis_index("expert"), meta, len(refs), refs[0].shape[0])


def gate_columns(meta):
    columns = meta.T
    return columns[:, 2:3], columns[:, 3:4]


def route_sums(meta, refs):
    m0, m1 = masks_of(meta, refs)
    got = get(refs)
    g0, g1 = gate_columns(meta)
    o0, o1 = dot(m0, got, FIRST), dot(m1, got, FIRST)
    return m0, m1, g0, g1, o0, o1, g0 * o0 + g1 * o1


def put_d_gates(ref, diff, o0, o1):
    tok = diff.shape[0]
    lane = lax.broadcasted_iota(jnp.int32, (tok, 128), 1)
    d0 = jnp.sum(diff * o0, axis=1, keepdims=True)
    d1 = jnp.sum(diff * o1, axis=1, keepdims=True)
    ref[...] = jnp.where(lane == 0, d0, jnp.where(lane == 1, d1, 0.0)).T[0:2, :]


def put_route_grads(refs, m0, m1, g0, g1, diff):
    grads = jnp.concatenate([(g0 * diff).astype(BF16), (g1 * diff).astype(BF16)], axis=0)
    put(refs, dot(jnp.concatenate([m0, m1], axis=1), grads))


def pack_near_kernel(own_ref, routes_ref, gates_ref, tokens_ref, meta_ref, *rows_refs):
    del own_ref
    meta = jnp.concatenate(
        [
            routes_ref[...].astype(F32),
            gates_ref[...],
            jnp.zeros((4, routes_ref.shape[1]), F32),
        ],
        axis=0,
    )
    meta_ref[...] = meta
    m0, m1 = masks_of(meta, rows_refs)
    put(rows_refs, dot(m0 + m1, tokens_ref[...]))


def pack_far_kernel(meta_ref, tokens_ref, *rows_refs):
    m0, m1 = masks_of(meta_ref[...], rows_refs)
    put(rows_refs, dot(m0 + m1, tokens_ref[...]))


def forward_kernel(pieces, own_ref, other_ref, *refs):
    ins, outs, refs = refs[:pieces], refs[pieces : 2 * pieces], refs[2 * pieces :]
    sent_ref, hid_own_ref, fa_ref, fb_ref = refs
    x = get(ins)
    put_columns(sent_ref, x)
    units, width = other_ref.shape[1:]
    hidden = []
    for w_ref, first in ((own_ref, 0), (other_ref, units)):
        both = dot(w_ref[0:2].reshape(2 * units, width), x, LAST)
        gate, up = both[:units], both[units:]
        sig = 0.5 * jnp.tanh(0.5 * gate) + 0.5
        silu = gate * sig
        hidden.append((silu * up).astype(BF16))
        fa_ref[first : first + units, :] = (up * (sig + silu * (1.0 - sig))).astype(BF16)
        fb_ref[first : first + units, :] = silu.astype(BF16)
    hid_own_ref[...] = hidden[0]
    put_rows(sent_ref, width // x.shape[0], hidden[1])
    put(outs, dot(hidden[0], own_ref[2], FIRST) + dot(hidden[1], other_ref[2], FIRST))


def backward_kernel(pieces, own_ref, other_ref, fa_ref, fb_ref, *refs):
    ins, outs, refs = refs[:pieces], refs[pieces : 2 * pieces], refs[2 * pieces :]
    sent_ref, dgu_own_ref = refs
    rg = get(ins)
    put_columns(sent_ref, rg)
    units, width = own_ref.shape[1:]
    both = []
    for w_ref, first in ((own_ref, 0), (other_ref, units)):
        at = slice(first, first + units)
        dh = dot(w_ref[2], rg, LAST)
        dg = (dh * fa_ref[at, :].astype(F32)).astype(BF16)
        du = (dh * fb_ref[at, :].astype(F32)).astype(BF16)
        both.append(jnp.concatenate([dg, du], axis=0))
    dgu_own_ref[...] = both[0]
    put_rows(sent_ref, width // rg.shape[0], both[1])
    put(
        outs,
        dot(both[0], own_ref[0:2].reshape(2 * units, width), FIRST)
        + dot(both[1], other_ref[0:2].reshape(2 * units, width), FIRST),
    )


def near_sum_kernel(meta_ref, teacher_ref, *refs):
    ins, out_ref = refs[:-1], refs[-1]
    total = route_sums(meta_ref[...], ins)[-1]
    out_ref[...] = (total - teacher_ref[...].astype(F32)).astype(BF16)


def far_grad_kernel(pieces, meta_ref, rest_ref, *refs):
    ins, part_ref, d_gates_ref, outs = (
        refs[:pieces],
        refs[pieces],
        refs[pieces + 1],
        refs[pieces + 2 :],
    )
    m0, m1, g0, g1, o0, o1, total = route_sums(meta_ref[...], ins)
    part_ref[...] = total.astype(BF16)
    diff = total + rest_ref[...].astype(F32)
    put_route_grads(outs, m0, m1, g0, g1, diff)
    put_d_gates(d_gates_ref, diff, o0, o1)


def near_grad_kernel(pieces, meta_ref, teacher_ref, part_ref, *refs):
    ins, student_ref, d_gates_ref, outs = (
        refs[:pieces],
        refs[pieces],
        refs[pieces + 1],
        refs[pieces + 2 :],
    )
    m0, m1, g0, g1, o0, o1, total = route_sums(meta_ref[...], ins)
    total = total + part_ref[...].astype(F32)
    student_ref[...] = total.astype(BF16)
    diff = total - teacher_ref[...].astype(F32)
    put_route_grads(outs, m0, m1, g0, g1, diff)
    put_d_gates(d_gates_ref, diff, o0, o1)


def far_back_kernel(meta_ref, d_gates_ref, *refs):
    ins, out_ref = refs[:-1], refs[-1]
    m0, m1 = masks_of(meta_ref[...], ins)
    tok = m0.shape[1]
    out_ref[:tok, :] = dot(m0 + m1, get(ins), FIRST).astype(BF16)
    value = d_gates_ref[...]
    high = value.astype(BF16)
    low = (value - high.astype(F32)).astype(BF16)
    rest = jnp.zeros((out_ref.shape[0] - tok - 4, tok), BF16)
    out_ref[tok:, :tok] = jnp.concatenate([high, low, rest], axis=0)
    out_ref[tok:, tok:] = jnp.zeros((out_ref.shape[0] - tok, out_ref.shape[1] - tok), BF16)


def final_kernel(pieces, meta_ref, part_ref, near_ref, *refs):
    ins, out_ref, d_gates_ref = refs[:pieces], refs[pieces], refs[pieces + 1]
    m0, m1 = masks_of(meta_ref[...], ins)
    tok = m0.shape[1]
    total = dot(m0 + m1, get(ins), FIRST) + part_ref[:tok, :].astype(F32)
    out_ref[...] = total.astype(BF16)
    far = part_ref[tok:, :tok].astype(F32)
    d_gates_ref[...] = near_ref[...] + (far[0:2] + far[2:4])


def weight_kernel(across, *refs):
    (xf, xn, xfs, xns, gf, gn, gfs, gns, df, dn, hf, hn, out_hbm, finished, buf, sems) = refs
    finished[...] = jnp.zeros_like(finished)
    units = hf.shape[0]
    side = hf.shape[1]

    def acts(own, sent, first):
        blocks = range(across + first // side, across + (first + units) // side)
        theirs = [jnp.concatenate([r[i] for i in blocks], axis=0) for r in sent]
        return jnp.concatenate([r[first : first + units, :] for r in own] + theirs, axis=1)

    x, rg = (xf, xn, xfs, xns), (gf, gn, gfs, gns)
    copies = []
    for m, (own, sent, rows, first) in enumerate(
        (
            ((hf, hn), (xfs, xns), rg, 0),
            ((df, dn), (gfs, gns), x, 0),
            ((df, dn), (gfs, gns), x, units),
        )
    ):
        row = (m + 2) % 3
        for i in range(across):
            at = pl.ds(i * side, side)
            column = jnp.concatenate([r[i] for r in rows], axis=0)
            buf[row, :, at] = dot(acts(own, sent, first), column).astype(BF16)
            copies.append(
                pltpu.make_async_copy(
                    buf.at[row, :, at], out_hbm.at[row, :, at], sems.at[row, i]
                )
            )
            copies[-1].start()
    for copy in copies:
        copy.wait()


def local(tokens, teacher, routes, gate_weights, weights):
    tok, width = tokens.shape
    experts = lax.axis_size("expert")
    half = experts // 2
    capacity = 4 * tok // experts
    rows = half * capacity
    units = weights.shape[1]

    pieces = [jax.ShapeDtypeStruct((capacity, width), BF16)] * half
    dense = jax.ShapeDtypeStruct((tok, width), BF16)
    longer = jax.ShapeDtypeStruct((tok + 16, width), BF16)
    pair = jax.ShapeDtypeStruct((2, tok), F32)
    acts = jax.ShapeDtypeStruct((units, rows), BF16)
    across, along = width // rows, units // rows
    sent_x = jax.ShapeDtypeStruct((across + along, rows, rows), BF16)
    sent_g = jax.ShapeDtypeStruct((across + 2 * along, rows, rows), BF16)
    acts2 = jax.ShapeDtypeStruct((2 * units, rows), BF16)
    vspec = pl.BlockSpec(memory_space=pltpu.VMEM)
    aspec = pl.BlockSpec(memory_space=pl.ANY)

    def call(
        kernel,
        name,
        out_shape,
        specs,
        *args,
        after=(),
        through=(),
        limit=8,
        scratch=(),
        in_hbm=0,
    ):
        many = isinstance(out_shape, list)
        specs = list(specs) + [vspec] * (len(args) - len(specs))
        inputs = len(args) + len(after) + len(through)
        outputs = len(out_shape) if many else 1

        def body(*refs):
            kernel(
                *refs[: len(args)],
                *refs[inputs : inputs + outputs],
                *refs[inputs + outputs + len(through) :],
            )

        out_specs = [aspec] * in_hbm + [vspec] * (outputs - in_hbm) + [aspec] * len(through)
        out_shapes = (out_shape if many else [out_shape]) + [
            jax.ShapeDtypeStruct(a.shape, a.dtype) for a in through
        ]
        single = not many and not through
        return pl.pallas_call(
            body,
            in_specs=specs + [aspec] * (len(after) + len(through)),
            out_specs=out_specs[0] if single else out_specs,
            out_shape=out_shapes[0] if single else out_shapes,
            input_output_aliases={
                len(args) + len(after) + i: outputs + i for i in range(len(through))
            },
            scratch_shapes=scratch,
            cost_estimate=pl.CostEstimate(
                flops=FLOPS.get(name, 10**8), bytes_accessed=2 * MIB, transcendentals=0
            ),
            compiler_params=pltpu.CompilerParams(vmem_limit_bytes=limit * MIB),
            name=name,
        )(*args, *after, *through)

    def within_half(rows_of):
        return [rows_of[0]] + [
            lax.ppermute(rows_of[s], "expert", [(i, i ^ s) for i in range(experts)])
            for s in range(half - 1, 0, -1)
        ]

    def to_mirror(x):
        return lax.ppermute(x, "expert", [(i, i ^ half) for i in range(experts)])

    def to_sibling(x):
        return lax.ppermute(x, "dp", [(0, 1), (1, 0)])

    far_tokens = to_mirror(tokens)
    own = weights[0].transpose(1, 0, 2)
    other = to_sibling(own)

    def forward(x_pieces, name, after=()):
        res = call(
            functools.partial(forward_kernel, half),
            name,
            pieces + [sent_x, acts, acts2, acts2],
            [],
            own,
            other,
            *x_pieces,
            after=after,
            limit=20,
        )
        return res[:half], res[half:]

    def backward(rg_pieces, fa, fb, name, after=(), through=()):
        res = call(
            functools.partial(backward_kernel, half),
            name,
            pieces + [sent_g, acts2],
            [],
            own,
            other,
            fa,
            fb,
            *rg_pieces,
            after=after,
            through=through,
            limit=20,
        )
        return res[:half], res[half:]

    res = call(
        pack_near_kernel,
        "pack_near",
        [jax.ShapeDtypeStruct((8, tok), F32)] + pieces,
        [],
        own,
        routes.T,
        gate_weights.T,
        tokens,
        limit=10,
    )
    meta, x_near = res[0], within_half(res[1:])
    far_meta = to_mirror(meta)
    x_far = within_half(
        call(pack_far_kernel, "pack_far", pieces, [], far_meta, far_tokens)
    )

    out_near, (xn, hn, fan, fbn) = forward(x_near, "forward_near")
    got_near = within_half(out_near)
    out_far, (xf, hf, faf, fbf) = forward(x_far, "forward_far", after=[xn])
    rest_rows, *out_far = call(
        near_sum_kernel,
        "near_sum",
        dense,
        [],
        meta,
        teacher,
        *got_near,
        through=out_far,
    )
    rest = to_mirror(rest_rows)
    got_far = within_half(out_far)
    xf_sib, xn_sib = to_sibling(xf), to_sibling(xn)

    res = call(
        functools.partial(far_grad_kernel, half),
        "far_grad",
        [dense, pair] + pieces,
        [],
        far_meta,
        rest,
        *got_far,
        after=[xf_sib, xn_sib],
    )
    part, d_gates_far, rg_far = to_mirror(res[0]), res[1], within_half(res[2:])
    grad_far, (gf, df) = backward(rg_far, faf, fbf, "backward_far")
    res = call(
        functools.partial(near_grad_kernel, half),
        "near_grad",
        [dense, pair] + pieces,
        [],
        meta,
        teacher,
        part,
        *got_near,
        after=[df],
    )
    student, d_gates_near, rg_near = res[0], res[1], within_half(res[2:])

    back_far = within_half(grad_far)
    part_rows = call(
        far_back_kernel, "far_back", longer, [], far_meta, d_gates_far, *back_far
    )
    part = to_mirror(part_rows)
    grad_near, (gn, dn) = backward(rg_near, fan, fbn, "backward_near", after=[part_rows] + back_far[1:])
    gf_sib, gn_sib = to_sibling(gf), to_sibling(gn)
    back_near = within_half(grad_near)

    weight_grads, finished = call(
        functools.partial(weight_kernel, across),
        "weight_gradients",
        [
            jax.ShapeDtypeStruct((3, units, width), BF16),
            jax.ShapeDtypeStruct((8, 128), F32),
        ],
        [],
        *(xf, xn, xf_sib, xn_sib),
        *(gf, gn, gf_sib, gn_sib),
        *(df, dn, hf, hn),
        after=[],
        limit=24,
        scratch=[
            pltpu.VMEM((3, units, width), BF16),
            pltpu.SemaphoreType.DMA((3, across)),
        ],
        in_hbm=1,
    )

    d_tokens, d_gates = call(
        functools.partial(final_kernel, half),
        "combine_gradients",
        [dense, pair],
        [],
        meta,
        part,
        d_gates_near,
        *back_near,
        after=[finished],
    )
    return (student, d_tokens, d_gates.T, weight_grads.transpose(1, 0, 2)[None])


def solution(mesh):
    rows = P(("groups", "expert", "dp"), None)
    return jax.shard_map(
        local,
        mesh=mesh,
        in_specs=(rows, rows, rows, rows, P("expert", "dp", None, None)),
        out_specs=(rows, rows, rows, P(("groups", "expert"), "dp", None, None)),
        check_vma=False,
    )
```

```python
import functools

import jax
import jax.numpy as jnp
from jax import lax
from jax.experimental import pallas as pl
from jax.experimental.pallas import tpu as pltpu
from jax.sharding import PartitionSpec as P

PLAIN = (((1,), (0,)), ((), ()))
LAST = (((1,), (1,)), ((), ()))
FIRST = (((0,), (0,)), ((), ()))
MIB = 1024 * 1024
F32 = jnp.float32
BF16 = jnp.bfloat16
FLOPS = {
    "pack_near": 30000000000,
    "pack_far": 30000000000,
    "forward_near": 100000000,
    "forward_far": 3000000000,
    "near_sum": 30000000000,
    "far_grad": 10000000000,
    "near_grad": 30000000000,
    "backward_far": 3000000000,
    "backward_near": 10000000000,
    "far_back": 1000000000,
    "weight_gradients": 30000000000,
    "combine_gradients": 30000000000,
    "order_rest": 30000000000,
    "order_back": 30000000000,
    "order_far": 30000000000,
}


def dot(a, b, dims=PLAIN):
    return lax.dot_general(a, b, dims, preferred_element_type=F32)


def slot_masks(me, meta, pieces, capacity):
    tok = meta.shape[1]
    expert_of = (lax.broadcasted_iota(jnp.int32, (pieces, tok), 0) ^ me).astype(F32)
    first, second = meta[0:1, :] == expert_of, meta[1:2, :] == expert_of
    chosen = jnp.where(first | second, 1.0, 0.0).astype(BF16)
    before = lax.broadcasted_iota(jnp.int32, (tok, tok), 0) < lax.broadcasted_iota(
        jnp.int32, (tok, tok), 1
    )
    rank = dot(chosen, jnp.where(before, 1.0, 0.0).astype(BF16))
    rank0 = jnp.where(first, rank, -1.0)
    rank1 = jnp.where(second, rank, -1.0)
    place = lax.broadcasted_iota(jnp.int32, (capacity, tok), 0).astype(F32)

    def expand(ranks):
        return jnp.concatenate(
            [
                jnp.where(ranks[s : s + 1, :] == place, 1.0, 0.0).astype(BF16)
                for s in range(pieces)
            ],
            axis=0,
        )

    return expand(rank0), expand(rank1)


def put(refs, rows):
    capacity = refs[0].shape[0]
    for s, ref in enumerate(refs):
        ref[...] = rows[s * capacity : (s + 1) * capacity].astype(ref.dtype)


def put_columns(ref, rows):
    side = rows.shape[0]
    for i in range(rows.shape[1] // side):
        ref[i] = rows[:, i * side : (i + 1) * side]


def put_rows(ref, first, value):
    side = value.shape[1]
    for i in range(value.shape[0] // side):
        ref[first + i] = value[i * side : (i + 1) * side, :]


def get_columns(ref):
    return jnp.concatenate([ref[i] for i in range(ref.shape[0])], axis=1)


def get(refs):
    refs = refs[:1] + refs[:0:-1]
    return jnp.concatenate([ref[...] for ref in refs], axis=0)


def masks_of(meta, refs):
    return slot_masks(lax.axis_index("expert"), meta, len(refs), refs[0].shape[0])


def gate_columns(meta):
    columns = meta.T
    return columns[:, 2:3], columns[:, 3:4]


def route_sums(meta, refs):
    m0, m1 = masks_of(meta, refs)
    got = get(refs)
    g0, g1 = gate_columns(meta)
    o0, o1 = dot(m0, got, FIRST), dot(m1, got, FIRST)
    return m0, m1, g0, g1, o0, o1, g0 * o0 + g1 * o1


def put_d_gates(ref, diff, o0, o1):
    tok = diff.shape[0]
    lane = lax.broadcasted_iota(jnp.int32, (tok, 128), 1)
    d0 = jnp.sum(diff * o0, axis=1, keepdims=True)
    d1 = jnp.sum(diff * o1, axis=1, keepdims=True)
    ref[...] = jnp.where(lane == 0, d0, jnp.where(lane == 1, d1, 0.0)).T[0:2, :]


def put_route_grads(refs, m0, m1, g0, g1, diff):
    grads = jnp.concatenate([(g0 * diff).astype(BF16), (g1 * diff).astype(BF16)], axis=0)
    put(refs, dot(jnp.concatenate([m0, m1], axis=1), grads))


def pack_near_kernel(own_ref, routes_ref, gates_ref, tokens_ref, meta_ref, *rows_refs):
    del own_ref
    meta = jnp.concatenate(
        [
            routes_ref[...].astype(F32),
            gates_ref[...],
            jnp.zeros((4, routes_ref.shape[1]), F32),
        ],
        axis=0,
    )
    meta_ref[...] = meta
    m0, m1 = masks_of(meta, rows_refs)
    put(rows_refs, dot(m0 + m1, tokens_ref[...]))


def pack_far_kernel(meta_ref, tokens_ref, *rows_refs):
    m0, m1 = masks_of(meta_ref[...], rows_refs)
    put(rows_refs, dot(m0 + m1, tokens_ref[...]))


def forward_kernel(pieces, own_ref, other_ref, *refs):
    ins, outs, refs = refs[:pieces], refs[pieces : 2 * pieces], refs[2 * pieces :]
    sent_ref, hid_own_ref, fa_ref, fb_ref = refs
    x = get(ins)
    put_columns(sent_ref, x)
    units, width = other_ref.shape[1:]
    hidden = []
    for w_ref, first in ((own_ref, 0), (other_ref, units)):
        both = dot(w_ref[0:2].reshape(2 * units, width), x, LAST)
        gate, up = both[:units], both[units:]
        sig = 0.5 * jnp.tanh(0.5 * gate) + 0.5
        silu = gate * sig
        hidden.append((silu * up).astype(BF16))
        fa_ref[first : first + units, :] = (up * (sig + silu * (1.0 - sig))).astype(BF16)
        fb_ref[first : first + units, :] = silu.astype(BF16)
    hid_own_ref[...] = hidden[0]
    put_rows(sent_ref, width // x.shape[0], hidden[1])
    put(outs, dot(hidden[0], own_ref[2], FIRST) + dot(hidden[1], other_ref[2], FIRST))


def backward_kernel(pieces, own_ref, other_ref, fa_ref, fb_ref, *refs):
    ins, outs, refs = refs[:pieces], refs[pieces : 2 * pieces], refs[2 * pieces :]
    sent_ref, dgu_own_ref = refs
    rg = get(ins)
    put_columns(sent_ref, rg)
    units, width = own_ref.shape[1:]
    both = []
    for w_ref, first in ((own_ref, 0), (other_ref, units)):
        at = slice(first, first + units)
        dh = dot(w_ref[2], rg, LAST)
        dg = (dh * fa_ref[at, :].astype(F32)).astype(BF16)
        du = (dh * fb_ref[at, :].astype(F32)).astype(BF16)
        both.append(jnp.concatenate([dg, du], axis=0))
    dgu_own_ref[...] = both[0]
    put_rows(sent_ref, width // rg.shape[0], both[1])
    put(
        outs,
        dot(both[0], own_ref[0:2].reshape(2 * units, width), FIRST)
        + dot(both[1], other_ref[0:2].reshape(2 * units, width), FIRST),
    )


def near_sum_kernel(meta_ref, teacher_ref, *refs):
    ins, out_ref = refs[:-1], refs[-1]
    total = route_sums(meta_ref[...], ins)[-1]
    out_ref[...] = (total - teacher_ref[...].astype(F32)).astype(BF16)


def far_grad_kernel(pieces, meta_ref, rest_ref, *refs):
    ins, part_ref, d_gates_ref, outs = (
        refs[:pieces],
        refs[pieces],
        refs[pieces + 1],
        refs[pieces + 2 :],
    )
    m0, m1, g0, g1, o0, o1, total = route_sums(meta_ref[...], ins)
    part_ref[...] = total.astype(BF16)
    diff = total + rest_ref[...].astype(F32)
    put_route_grads(outs, m0, m1, g0, g1, diff)
    put_d_gates(d_gates_ref, diff, o0, o1)


def near_grad_kernel(pieces, meta_ref, teacher_ref, part_ref, *refs):
    ins, student_ref, d_gates_ref, outs = (
        refs[:pieces],
        refs[pieces],
        refs[pieces + 1],
        refs[pieces + 2 :],
    )
    m0, m1, g0, g1, o0, o1, total = route_sums(meta_ref[...], ins)
    total = total + part_ref[...].astype(F32)
    student_ref[...] = total.astype(BF16)
    diff = total - teacher_ref[...].astype(F32)
    put_route_grads(outs, m0, m1, g0, g1, diff)
    put_d_gates(d_gates_ref, diff, o0, o1)


def far_back_kernel(meta_ref, d_gates_ref, *refs):
    ins, out_ref = refs[:-1], refs[-1]
    m0, m1 = masks_of(meta_ref[...], ins)
    tok = m0.shape[1]
    out_ref[:tok, :] = dot(m0 + m1, get(ins), FIRST).astype(BF16)
    value = d_gates_ref[...]
    high = value.astype(BF16)
    low = (value - high.astype(F32)).astype(BF16)
    rest = jnp.zeros((out_ref.shape[0] - tok - 4, tok), BF16)
    out_ref[tok:, :tok] = jnp.concatenate([high, low, rest], axis=0)
    out_ref[tok:, tok:] = jnp.zeros((out_ref.shape[0] - tok, out_ref.shape[1] - tok), BF16)


def final_kernel(pieces, meta_ref, part_ref, near_ref, *refs):
    ins, out_ref, d_gates_ref = refs[:pieces], refs[pieces], refs[pieces + 1]
    m0, m1 = masks_of(meta_ref[...], ins)
    tok = m0.shape[1]
    total = dot(m0 + m1, get(ins), FIRST) + part_ref[:tok, :].astype(F32)
    out_ref[...] = total.astype(BF16)
    far = part_ref[tok:, :tok].astype(F32)
    d_gates_ref[...] = near_ref[...] + (far[0:2] + far[2:4])


def weight_kernel(across, *refs):
    (xf, xn, xfs, xns, gf, gn, gfs, gns, df, dn, hf, hn, out_hbm, finished, buf, sems) = refs
    finished[...] = jnp.zeros_like(finished)
    units = hf.shape[0]
    side = hf.shape[1]

    def acts(own, sent, first):
        blocks = range(across + first // side, across + (first + units) // side)
        theirs = [jnp.concatenate([r[i] for i in blocks], axis=0) for r in sent]
        return jnp.concatenate([r[first : first + units, :] for r in own] + theirs, axis=1)

    x, rg = (xf, xn, xfs, xns), (gf, gn, gfs, gns)
    copies = []
    for m, (own, sent, rows, first) in enumerate(
        (
            ((hf, hn), (xfs, xns), rg, 0),
            ((df, dn), (gfs, gns), x, 0),
            ((df, dn), (gfs, gns), x, units),
        )
    ):
        row = (m + 2) % 3
        for i in range(across):
            at = pl.ds(i * side, side)
            column = jnp.concatenate([r[i] for r in rows], axis=0)
            buf[row, :, at] = dot(acts(own, sent, first), column).astype(BF16)
            copies.append(
                pltpu.make_async_copy(
                    buf.at[row, :, at], out_hbm.at[row, :, at], sems.at[row, i]
                )
            )
            copies[-1].start()
    for copy in copies:
        copy.wait()


def order_kernel(tiny_ref):
    tiny_ref[...] = jnp.zeros_like(tiny_ref)


def local(tokens, teacher, routes, gate_weights, weights):
    tok, width = tokens.shape
    experts = lax.axis_size("expert")
    half = experts // 2
    capacity = 4 * tok // experts
    rows = half * capacity
    units = weights.shape[1]

    pieces = [jax.ShapeDtypeStruct((capacity, width), BF16)] * half
    dense = jax.ShapeDtypeStruct((tok, width), BF16)
    longer = jax.ShapeDtypeStruct((tok + 16, width), BF16)
    pair = jax.ShapeDtypeStruct((2, tok), F32)
    acts = jax.ShapeDtypeStruct((units, rows), BF16)
    across, along = width // rows, units // rows
    sent_x = jax.ShapeDtypeStruct((across + along, rows, rows), BF16)
    sent_g = jax.ShapeDtypeStruct((across + 2 * along, rows, rows), BF16)
    acts2 = jax.ShapeDtypeStruct((2 * units, rows), BF16)
    tiny = jax.ShapeDtypeStruct((8, 128), F32)
    vspec = pl.BlockSpec(memory_space=pltpu.VMEM)
    aspec = pl.BlockSpec(memory_space=pl.ANY)

    def call(
        kernel,
        name,
        out_shape,
        specs,
        *args,
        after=(),
        through=(),
        limit=8,
        scratch=(),
        in_hbm=0,
    ):
        many = isinstance(out_shape, list)
        specs = list(specs) + [vspec] * (len(args) - len(specs))
        inputs = len(args) + len(after) + len(through)
        outputs = len(out_shape) if many else 1

        def body(*refs):
            kernel(
                *refs[: len(args)],
                *refs[inputs : inputs + outputs],
                *refs[inputs + outputs + len(through) :],
            )

        out_specs = [aspec] * in_hbm + [vspec] * (outputs - in_hbm) + [aspec] * len(through)
        out_shapes = (out_shape if many else [out_shape]) + [
            jax.ShapeDtypeStruct(a.shape, a.dtype) for a in through
        ]
        single = not many and not through
        return pl.pallas_call(
            body,
            in_specs=specs + [aspec] * (len(after) + len(through)),
            out_specs=out_specs[0] if single else out_specs,
            out_shape=out_shapes[0] if single else out_shapes,
            input_output_aliases={
                len(args) + len(after) + i: outputs + i for i in range(len(through))
            },
            scratch_shapes=scratch,
            cost_estimate=pl.CostEstimate(
                flops=FLOPS.get(name, 10**8), bytes_accessed=2 * MIB, transcendentals=0
            ),
            compiler_params=pltpu.CompilerParams(vmem_limit_bytes=limit * MIB),
            name=name,
        )(*args, *after, *through)

    def within_half(rows_of):
        return [rows_of[0]] + [
            lax.ppermute(rows_of[s], "expert", [(i, i ^ s) for i in range(experts)])
            for s in range(half - 1, 0, -1)
        ]

    def to_mirror(x):
        return lax.ppermute(x, "expert", [(i, i ^ half) for i in range(experts)])

    def to_sibling(x):
        return lax.ppermute(x, "dp", [(0, 1), (1, 0)])

    far_tokens = to_mirror(tokens)
    own = weights[0].transpose(1, 0, 2)
    other = to_sibling(own)

    def forward(x_pieces, name, after=()):
        res = call(
            functools.partial(forward_kernel, half),
            name,
            pieces + [sent_x, acts, acts2, acts2],
            [],
            own,
            other,
            *x_pieces,
            after=after,
            limit=20,
        )
        return res[:half], res[half:]

    def backward(rg_pieces, fa, fb, name, after=(), through=()):
        res = call(
            functools.partial(backward_kernel, half),
            name,
            pieces + [sent_g, acts2],
            [],
            own,
            other,
            fa,
            fb,
            *rg_pieces,
            after=after,
            through=through,
            limit=20,
        )
        return res[:half], res[half:]

    res = call(
        pack_near_kernel,
        "pack_near",
        [jax.ShapeDtypeStruct((8, tok), F32)] + pieces,
        [],
        own,
        routes.T,
        gate_weights.T,
        tokens,
        limit=10,
    )
    meta, x_near = res[0], within_half(res[1:])
    far_meta = to_mirror(meta)
    x_far = within_half(
        call(pack_far_kernel, "pack_far", pieces, [], far_meta, far_tokens)
    )

    out_near, (xn, hn, fan, fbn) = forward(x_near, "forward_near", after=[x_far[0]])
    xn_sib = to_sibling(xn)
    far_here, hn = call(
        order_kernel, "order_far", [tiny], [], after=x_far[1:], through=[hn]
    )
    got_near = within_half(out_near)
    rest_rows = call(
        near_sum_kernel,
        "near_sum",
        dense,
        [],
        meta,
        teacher,
        *got_near,
    )
    rest = to_mirror(rest_rows)
    out_far, (xf, hf, faf, fbf) = forward(x_far, "forward_far", after=[far_here, xn_sib, rest_rows])
    got_far = within_half(out_far)
    _, rest, hf = call(
        order_kernel, "order_rest", [tiny], [], after=[], through=[rest, hf]
    )
    xf_sib = to_sibling(xf)

    res = call(
        functools.partial(far_grad_kernel, half),
        "far_grad",
        [dense, pair] + pieces,
        [],
        far_meta,
        rest,
        *got_far,
        after=[xf_sib, xn_sib],
    )
    part, d_gates_far, rg_far = to_mirror(res[0]), res[1], within_half(res[2:])
    grad_far, (gf, df) = backward(rg_far, faf, fbf, "backward_far")
    res = call(
        functools.partial(near_grad_kernel, half),
        "near_grad",
        [dense, pair] + pieces,
        [],
        meta,
        teacher,
        part,
        *got_near,
        after=[df],
    )
    student, d_gates_near, rg_near = res[0], res[1], within_half(res[2:])

    back_far = within_half(grad_far)
    gf_sib = to_sibling(gf)
    part_rows = call(
        far_back_kernel, "far_back", longer, [], far_meta, d_gates_far, *back_far
    )
    part = to_mirror(part_rows)
    grad_near, (gn, dn) = backward(rg_near, fan, fbn, "backward_near", after=[part_rows, gf_sib])
    gn_sib = to_sibling(gn)
    back_near = within_half(grad_near)

    _, part, dn = call(order_kernel, "order_back", [tiny], [], through=[part, dn])
    weight_grads, finished = call(
        functools.partial(weight_kernel, across),
        "weight_gradients",
        [
            jax.ShapeDtypeStruct((3, units, width), BF16),
            jax.ShapeDtypeStruct((8, 128), F32),
        ],
        [],
        *(xf, xn, xf_sib, xn_sib),
        *(gf, gn, gf_sib, gn_sib),
        *(df, dn, hf, hn),
        after=[],
        limit=24,
        scratch=[
            pltpu.VMEM((3, units, width), BF16),
            pltpu.SemaphoreType.DMA((3, across)),
        ],
        in_hbm=1,
    )

    d_tokens, d_gates = call(
        functools.partial(final_kernel, half),
        "combine_gradients",
        [dense, pair],
        [],
        meta,
        part,
        d_gates_near,
        *back_near,
        after=[finished],
    )
    return (student, d_tokens, d_gates.T, weight_grads.transpose(1, 0, 2)[None])


def solution(mesh):
    rows = P(("groups", "expert", "dp"), None)
    return jax.shard_map(
        local,
        mesh=mesh,
        in_specs=(rows, rows, rows, rows, P("expert", "dp", None, None)),
        out_specs=(rows, rows, rows, P(("groups", "expert"), "dp", None, None)),
        check_vma=False,
    )
```

```python
import functools

import jax
import jax.numpy as jnp
from jax import lax
from jax.experimental import pallas as pl
from jax.experimental.pallas import tpu as pltpu
from jax.sharding import PartitionSpec as P

PLAIN = (((1,), (0,)), ((), ()))
LAST = (((1,), (1,)), ((), ()))
FIRST = (((0,), (0,)), ((), ()))
MIB = 1024 * 1024
F32 = jnp.float32
BF16 = jnp.bfloat16
FLOPS = {
    "pack_near": 30000000000,
    "pack_far": 30000000000,
    "forward_near": 100000000,
    "forward_far": 3000000000,
    "near_sum": 30000000000,
    "far_grad": 10000000000,
    "near_grad": 30000000000,
    "backward_far": 3000000000,
    "backward_near": 10000000000,
    "far_back": 10000000000,
    "weight_near": 30000000000,
    "combine_gradients": 30000000000,
    "order_rest": 30000000000,
    "order_back": 30000000000,
    "order_far": 30000000000,
    "weight_far": 2400000000,
}


def dot(a, b, dims=PLAIN):
    return lax.dot_general(a, b, dims, preferred_element_type=F32)


def slot_masks(me, meta, pieces, capacity):
    tok = meta.shape[1]
    expert_of = (lax.broadcasted_iota(jnp.int32, (pieces, tok), 0) ^ me).astype(F32)
    first, second = meta[0:1, :] == expert_of, meta[1:2, :] == expert_of
    chosen = jnp.where(first | second, 1.0, 0.0).astype(BF16)
    before = lax.broadcasted_iota(jnp.int32, (tok, tok), 0) < lax.broadcasted_iota(
        jnp.int32, (tok, tok), 1
    )
    rank = dot(chosen, jnp.where(before, 1.0, 0.0).astype(BF16))
    rank0 = jnp.where(first, rank, -1.0)
    rank1 = jnp.where(second, rank, -1.0)
    place = lax.broadcasted_iota(jnp.int32, (capacity, tok), 0).astype(F32)

    def expand(ranks):
        return jnp.concatenate(
            [
                jnp.where(ranks[s : s + 1, :] == place, 1.0, 0.0).astype(BF16)
                for s in range(pieces)
            ],
            axis=0,
        )

    return expand(rank0), expand(rank1)


def put(refs, rows):
    capacity = refs[0].shape[0]
    for s, ref in enumerate(refs):
        ref[...] = rows[s * capacity : (s + 1) * capacity].astype(ref.dtype)


def put_columns(ref, rows):
    side = rows.shape[0]
    for i in range(rows.shape[1] // side):
        ref[i] = rows[:, i * side : (i + 1) * side]


def put_rows(ref, first, value):
    side = value.shape[1]
    for i in range(value.shape[0] // side):
        ref[first + i] = value[i * side : (i + 1) * side, :]


def get_columns(ref):
    return jnp.concatenate([ref[i] for i in range(ref.shape[0])], axis=1)


def get(refs):
    refs = refs[:1] + refs[:0:-1]
    return jnp.concatenate([ref[...] for ref in refs], axis=0)


def masks_of(meta, refs):
    return slot_masks(lax.axis_index("expert"), meta, len(refs), refs[0].shape[0])


def gate_columns(meta):
    columns = meta.T
    return columns[:, 2:3], columns[:, 3:4]


def route_sums(meta, refs):
    m0, m1 = masks_of(meta, refs)
    got = get(refs)
    g0, g1 = gate_columns(meta)
    o0, o1 = dot(m0, got, FIRST), dot(m1, got, FIRST)
    return m0, m1, g0, g1, o0, o1, g0 * o0 + g1 * o1


def put_d_gates(ref, diff, o0, o1):
    tok = diff.shape[0]
    lane = lax.broadcasted_iota(jnp.int32, (tok, 128), 1)
    d0 = jnp.sum(diff * o0, axis=1, keepdims=True)
    d1 = jnp.sum(diff * o1, axis=1, keepdims=True)
    ref[...] = jnp.where(lane == 0, d0, jnp.where(lane == 1, d1, 0.0)).T[0:2, :]


def put_route_grads(refs, m0, m1, g0, g1, diff):
    grads = jnp.concatenate([(g0 * diff).astype(BF16), (g1 * diff).astype(BF16)], axis=0)
    put(refs, dot(jnp.concatenate([m0, m1], axis=1), grads))


def pack_near_kernel(own_ref, routes_ref, gates_ref, tokens_ref, meta_ref, *rows_refs):
    del own_ref
    meta = jnp.concatenate(
        [
            routes_ref[...].astype(F32),
            gates_ref[...],
            jnp.zeros((4, routes_ref.shape[1]), F32),
        ],
        axis=0,
    )
    meta_ref[...] = meta
    m0, m1 = masks_of(meta, rows_refs)
    put(rows_refs, dot(m0 + m1, tokens_ref[...]))


def pack_far_kernel(meta_ref, tokens_ref, *rows_refs):
    m0, m1 = masks_of(meta_ref[...], rows_refs)
    put(rows_refs, dot(m0 + m1, tokens_ref[...]))


def forward_kernel(pieces, own_ref, other_ref, *refs):
    ins, outs, refs = refs[:pieces], refs[pieces : 2 * pieces], refs[2 * pieces :]
    sent_ref, hid_own_ref, fa_ref, fb_ref = refs
    x = get(ins)
    put_columns(sent_ref, x)
    units, width = other_ref.shape[1:]
    hidden = []
    for w_ref, first in ((own_ref, 0), (other_ref, units)):
        both = dot(w_ref[0:2].reshape(2 * units, width), x, LAST)
        gate, up = both[:units], both[units:]
        sig = 0.5 * jnp.tanh(0.5 * gate) + 0.5
        silu = gate * sig
        hidden.append((silu * up).astype(BF16))
        fa_ref[first : first + units, :] = (up * (sig + silu * (1.0 - sig))).astype(BF16)
        fb_ref[first : first + units, :] = silu.astype(BF16)
    hid_own_ref[...] = hidden[0]
    put_rows(sent_ref, width // x.shape[0], hidden[1])
    put(outs, dot(hidden[0], own_ref[2], FIRST) + dot(hidden[1], other_ref[2], FIRST))


def backward_kernel(pieces, own_ref, other_ref, fa_ref, fb_ref, *refs):
    ins, outs, refs = refs[:pieces], refs[pieces : 2 * pieces], refs[2 * pieces :]
    sent_ref, dgu_own_ref = refs
    rg = get(ins)
    put_columns(sent_ref, rg)
    units, width = own_ref.shape[1:]
    both = []
    for w_ref, first in ((own_ref, 0), (other_ref, units)):
        at = slice(first, first + units)
        dh = dot(w_ref[2], rg, LAST)
        dg = (dh * fa_ref[at, :].astype(F32)).astype(BF16)
        du = (dh * fb_ref[at, :].astype(F32)).astype(BF16)
        both.append(jnp.concatenate([dg, du], axis=0))
    dgu_own_ref[...] = both[0]
    put_rows(sent_ref, width // rg.shape[0], both[1])
    put(
        outs,
        dot(both[0], own_ref[0:2].reshape(2 * units, width), FIRST)
        + dot(both[1], other_ref[0:2].reshape(2 * units, width), FIRST),
    )


def near_sum_kernel(meta_ref, teacher_ref, *refs):
    ins, out_ref = refs[:-1], refs[-1]
    total = route_sums(meta_ref[...], ins)[-1]
    out_ref[...] = (total - teacher_ref[...].astype(F32)).astype(BF16)


def far_grad_kernel(pieces, meta_ref, rest_ref, *refs):
    ins, part_ref, d_gates_ref, outs = (
        refs[:pieces],
        refs[pieces],
        refs[pieces + 1],
        refs[pieces + 2 :],
    )
    m0, m1, g0, g1, o0, o1, total = route_sums(meta_ref[...], ins)
    part_ref[...] = total.astype(BF16)
    diff = total + rest_ref[...].astype(F32)
    put_route_grads(outs, m0, m1, g0, g1, diff)
    put_d_gates(d_gates_ref, diff, o0, o1)


def near_grad_kernel(pieces, meta_ref, teacher_ref, part_ref, *refs):
    ins, student_ref, d_gates_ref, outs = (
        refs[:pieces],
        refs[pieces],
        refs[pieces + 1],
        refs[pieces + 2 :],
    )
    m0, m1, g0, g1, o0, o1, total = route_sums(meta_ref[...], ins)
    total = total + part_ref[...].astype(F32)
    student_ref[...] = total.astype(BF16)
    diff = total - teacher_ref[...].astype(F32)
    put_route_grads(outs, m0, m1, g0, g1, diff)
    put_d_gates(d_gates_ref, diff, o0, o1)


def far_back_kernel(meta_ref, d_gates_ref, *refs):
    ins, out_ref = refs[:-1], refs[-1]
    m0, m1 = masks_of(meta_ref[...], ins)
    tok = m0.shape[1]
    out_ref[:tok, :] = dot(m0 + m1, get(ins), FIRST).astype(BF16)
    value = d_gates_ref[...]
    high = value.astype(BF16)
    low = (value - high.astype(F32)).astype(BF16)
    rest = jnp.zeros((out_ref.shape[0] - tok - 4, tok), BF16)
    out_ref[tok:, :tok] = jnp.concatenate([high, low, rest], axis=0)
    out_ref[tok:, tok:] = jnp.zeros((out_ref.shape[0] - tok, out_ref.shape[1] - tok), BF16)


def final_kernel(pieces, meta_ref, part_ref, near_ref, *refs):
    ins, out_ref, d_gates_ref = refs[:pieces], refs[pieces], refs[pieces + 1]
    m0, m1 = masks_of(meta_ref[...], ins)
    tok = m0.shape[1]
    total = dot(m0 + m1, get(ins), FIRST) + part_ref[:tok, :].astype(F32)
    out_ref[...] = total.astype(BF16)
    far = part_ref[tok:, :tok].astype(F32)
    d_gates_ref[...] = near_ref[...] + (far[0:2] + far[2:4])


def weight_blocks(across, x, sent_x, g, sent_g, d, h):
    units, side = h.shape

    def acts(own, sent, first):
        blocks = range(across + first // side, across + (first + units) // side)
        theirs = jnp.concatenate([sent[i] for i in blocks], axis=0)
        return jnp.concatenate([own[first : first + units, :], theirs], axis=1)

    for row, own, sent, rows, first in (
        (2, h, sent_x, (g, sent_g), 0),
        (0, d, sent_g, (x, sent_x), 0),
        (1, d, sent_g, (x, sent_x), units),
    ):
        for i in range(across):
            column = jnp.concatenate([r[i] for r in rows], axis=0)
            yield row, i, dot(acts(own, sent, first), column)


def weight_far_kernel(across, x, sent_x, g, sent_g, d, h, out_ref, tiny_ref):
    tiny_ref[...] = jnp.zeros_like(tiny_ref)
    side = h.shape[1]
    for row, i, value in weight_blocks(across, x, sent_x, g, sent_g, d, h):
        out_ref[row, :, i * side : (i + 1) * side] = value.astype(BF16)


def weight_near_kernel(
    across, far_ref, x, sent_x, g, sent_g, d, h, out_hbm, tiny_ref, buf, sems
):
    tiny_ref[...] = jnp.zeros_like(tiny_ref)
    side = h.shape[1]
    copies = []
    for row, i, value in weight_blocks(across, x, sent_x, g, sent_g, d, h):
        at = pl.ds(i * side, side)
        buf[row, :, at] = (value + far_ref[row, :, at].astype(F32)).astype(BF16)
        copies.append(
            pltpu.make_async_copy(buf.at[row, :, at], out_hbm.at[row, :, at], sems.at[row, i])
        )
        copies[-1].start()
    for copy in copies:
        copy.wait()


def order_kernel():
    pass


def local(tokens, teacher, routes, gate_weights, weights):
    tok, width = tokens.shape
    experts = lax.axis_size("expert")
    half = experts // 2
    capacity = 4 * tok // experts
    rows = half * capacity
    units = weights.shape[1]

    pieces = [jax.ShapeDtypeStruct((capacity, width), BF16)] * half
    dense = jax.ShapeDtypeStruct((tok, width), BF16)
    longer = jax.ShapeDtypeStruct((tok + 16, width), BF16)
    pair = jax.ShapeDtypeStruct((2, tok), F32)
    acts = jax.ShapeDtypeStruct((units, rows), BF16)
    across, along = width // rows, units // rows
    sent_x = jax.ShapeDtypeStruct((across + along, rows, rows), BF16)
    sent_g = jax.ShapeDtypeStruct((across + 2 * along, rows, rows), BF16)
    acts2 = jax.ShapeDtypeStruct((2 * units, rows), BF16)
    tiny = jax.ShapeDtypeStruct((8, 128), F32)
    vspec = pl.BlockSpec(memory_space=pltpu.VMEM)
    aspec = pl.BlockSpec(memory_space=pl.ANY)

    def call(
        kernel,
        name,
        out_shape,
        specs,
        *args,
        after=(),
        through=(),
        limit=8,
        scratch=(),
        in_hbm=0,
    ):
        many = isinstance(out_shape, list)
        specs = list(specs) + [vspec] * (len(args) - len(specs))
        inputs = len(args) + len(after) + len(through)
        outputs = len(out_shape) if many else 1

        def body(*refs):
            kernel(
                *refs[: len(args)],
                *refs[inputs : inputs + outputs],
                *refs[inputs + outputs + len(through) :],
            )

        out_specs = [aspec] * in_hbm + [vspec] * (outputs - in_hbm) + [aspec] * len(through)
        out_shapes = (out_shape if many else [out_shape]) + [
            jax.ShapeDtypeStruct(a.shape, a.dtype) for a in through
        ]
        single = not many and not through
        return pl.pallas_call(
            body,
            in_specs=specs + [aspec] * (len(after) + len(through)),
            out_specs=out_specs[0] if single else out_specs,
            out_shape=out_shapes[0] if single else out_shapes,
            input_output_aliases={
                len(args) + len(after) + i: outputs + i for i in range(len(through))
            },
            scratch_shapes=scratch,
            cost_estimate=pl.CostEstimate(
                flops=FLOPS.get(name, 10**8), bytes_accessed=2 * MIB, transcendentals=0
            ),
            compiler_params=pltpu.CompilerParams(vmem_limit_bytes=limit * MIB),
            name=name,
        )(*args, *after, *through)

    def within_half(rows_of):
        return [rows_of[0]] + [
            lax.ppermute(rows_of[s], "expert", [(i, i ^ s) for i in range(experts)])
            for s in range(half - 1, 0, -1)
        ]

    def to_mirror(x):
        return lax.ppermute(x, "expert", [(i, i ^ half) for i in range(experts)])

    def to_sibling(x):
        return lax.ppermute(x, "dp", [(0, 1), (1, 0)])

    far_tokens = to_mirror(tokens)
    own = weights[0].transpose(1, 0, 2)
    other = to_sibling(own)

    def forward(x_pieces, name, after=()):
        res = call(
            functools.partial(forward_kernel, half),
            name,
            pieces + [sent_x, acts, acts2, acts2],
            [],
            own,
            other,
            *x_pieces,
            after=after,
            limit=20,
        )
        return res[:half], res[half:]

    def backward(rg_pieces, fa, fb, name, after=(), through=()):
        res = call(
            functools.partial(backward_kernel, half),
            name,
            pieces + [sent_g, acts2],
            [],
            own,
            other,
            fa,
            fb,
            *rg_pieces,
            after=after,
            through=through,
            limit=20,
        )
        return res[:half], res[half:]

    res = call(
        pack_near_kernel,
        "pack_near",
        [jax.ShapeDtypeStruct((8, tok), F32)] + pieces,
        [],
        own,
        routes.T,
        gate_weights.T,
        tokens,
        limit=10,
    )
    meta, x_near = res[0], within_half(res[1:])
    far_meta = to_mirror(meta)
    x_far = within_half(
        call(pack_far_kernel, "pack_far", pieces, [], far_meta, far_tokens)
    )

    out_near, (xn, hn, fan, fbn) = forward(x_near, "forward_near")
    got_near = within_half(out_near)
    out_far, (xf, hf, faf, fbf) = forward(x_far, "forward_far", after=[xn])
    rest_rows, *out_far = call(
        near_sum_kernel,
        "near_sum",
        dense,
        [],
        meta,
        teacher,
        *got_near,
        through=out_far,
    )
    rest = to_mirror(rest_rows)
    got_far = within_half(out_far)
    xf_sib, xn_sib = to_sibling(xf), to_sibling(xn)

    res = call(
        functools.partial(far_grad_kernel, half),
        "far_grad",
        [dense, pair] + pieces,
        [],
        far_meta,
        rest,
        *got_far,
        after=[xf_sib, xn_sib],
    )
    part, d_gates_far, rg_far = to_mirror(res[0]), res[1], within_half(res[2:])
    grad_far, (gf, df) = backward(rg_far, faf, fbf, "backward_far")
    res = call(
        functools.partial(near_grad_kernel, half),
        "near_grad",
        [dense, pair] + pieces,
        [],
        meta,
        teacher,
        part,
        *got_near,
        after=[df],
    )
    student, d_gates_near, rg_near = res[0], res[1], within_half(res[2:])

    back_far = within_half(grad_far)
    gf_sib = to_sibling(gf)
    far_weights, far_done = call(
        functools.partial(weight_far_kernel, across),
        "weight_far",
        [jax.ShapeDtypeStruct((3, units, width), BF16), tiny],
        [],
        *(xf, xf_sib, gf, gf_sib, df, hf),
        after=[back_far[1]],
        limit=16,
    )
    part_rows = call(
        far_back_kernel, "far_back", longer, [], far_meta, d_gates_far, *back_far, after=[far_done]
    )
    part = to_mirror(part_rows)
    grad_near, (gn, dn) = backward(rg_near, fan, fbn, "backward_near", after=[part_rows, gf_sib, far_done])
    gn_sib = to_sibling(gn)
    back_near = within_half(grad_near)

    part, dn = call(order_kernel, "order_back", [], [], through=[part, dn])
    weight_grads, finished = call(
        functools.partial(weight_near_kernel, across),
        "weight_near",
        [jax.ShapeDtypeStruct((3, units, width), BF16), tiny],
        [],
        *(far_weights, xn, xn_sib, gn, gn_sib, dn, hn),
        limit=24,
        scratch=[
            pltpu.VMEM((3, units, width), BF16),
            pltpu.SemaphoreType.DMA((3, across)),
        ],
        in_hbm=1,
    )

    d_tokens, d_gates = call(
        functools.partial(final_kernel, half),
        "combine_gradients",
        [dense, pair],
        [],
        meta,
        part,
        d_gates_near,
        *back_near,
        after=[finished],
    )
    return (student, d_tokens, d_gates.T, weight_grads.transpose(1, 0, 2)[None])


def solution(mesh):
    rows = P(("groups", "expert", "dp"), None)
    return jax.shard_map(
        local,
        mesh=mesh,
        in_specs=(rows, rows, rows, rows, P("expert", "dp", None, None)),
        out_specs=(rows, rows, rows, P(("groups", "expert"), "dp", None, None)),
        check_vma=False,
    )
```

```python
import functools

import jax
import jax.numpy as jnp
from jax import lax
from jax.experimental import pallas as pl
from jax.experimental.pallas import tpu as pltpu
from jax.sharding import PartitionSpec as P

PLAIN = (((1,), (0,)), ((), ()))
LAST = (((1,), (1,)), ((), ()))
FIRST = (((0,), (0,)), ((), ()))
MIB = 1024 * 1024
F32 = jnp.float32
BF16 = jnp.bfloat16
FLOPS = {
    "pack_near": 30000000000,
    "pack_far": 30000000000,
    "forward_near": 100000000,
    "forward_far": 3000000000,
    "near_sum": 30000000000,
    "far_grad": 10000000000,
    "near_grad": 30000000000,
    "backward_far": 3000000000,
    "backward_near": 10000000000,
    "far_back": 10000000000,
    "weight_near": 30000000000,
    "combine_gradients": 30000000000,
    "order_rest": 30000000000,
    "order_back": 30000000000,
    "order_return": 0,
    "weight_far": 2400000000,
}


def dot(a, b, dims=PLAIN):
    return lax.dot_general(a, b, dims, preferred_element_type=F32)


def slot_masks(me, meta, pieces, capacity):
    tok = meta.shape[1]
    expert_of = (lax.broadcasted_iota(jnp.int32, (pieces, tok), 0) ^ me).astype(F32)
    first, second = meta[0:1, :] == expert_of, meta[1:2, :] == expert_of
    chosen = jnp.where(first | second, 1.0, 0.0).astype(BF16)
    before = lax.broadcasted_iota(jnp.int32, (tok, tok), 0) < lax.broadcasted_iota(
        jnp.int32, (tok, tok), 1
    )
    rank = dot(chosen, jnp.where(before, 1.0, 0.0).astype(BF16))
    rank0 = jnp.where(first, rank, -1.0)
    rank1 = jnp.where(second, rank, -1.0)
    place = lax.broadcasted_iota(jnp.int32, (capacity, tok), 0).astype(F32)

    def expand(ranks):
        return jnp.concatenate(
            [
                jnp.where(ranks[s : s + 1, :] == place, 1.0, 0.0).astype(BF16)
                for s in range(pieces)
            ],
            axis=0,
        )

    return expand(rank0), expand(rank1)


def put(refs, rows):
    capacity = refs[0].shape[0]
    for s, ref in enumerate(refs):
        ref[...] = rows[s * capacity : (s + 1) * capacity].astype(ref.dtype)


def put_columns(ref, rows):
    side = rows.shape[0]
    for i in range(rows.shape[1] // side):
        ref[i] = rows[:, i * side : (i + 1) * side]


def put_rows(ref, first, value):
    side = value.shape[1]
    for i in range(value.shape[0] // side):
        ref[first + i] = value[i * side : (i + 1) * side, :]


def get_columns(ref):
    return jnp.concatenate([ref[i] for i in range(ref.shape[0])], axis=1)


def get(refs):
    refs = refs[:1] + refs[:0:-1]
    return jnp.concatenate([ref[...] for ref in refs], axis=0)


def masks_of(meta, refs):
    return slot_masks(lax.axis_index("expert"), meta, len(refs), refs[0].shape[0])


def gate_columns(meta):
    columns = meta.T
    return columns[:, 2:3], columns[:, 3:4]


def route_sums(meta, refs):
    m0, m1 = masks_of(meta, refs)
    got = get(refs)
    g0, g1 = gate_columns(meta)
    o0, o1 = dot(m0, got, FIRST), dot(m1, got, FIRST)
    return m0, m1, g0, g1, o0, o1, g0 * o0 + g1 * o1


def put_d_gates(ref, diff, o0, o1):
    tok = diff.shape[0]
    lane = lax.broadcasted_iota(jnp.int32, (tok, 128), 1)
    d0 = jnp.sum(diff * o0, axis=1, keepdims=True)
    d1 = jnp.sum(diff * o1, axis=1, keepdims=True)
    ref[...] = jnp.where(lane == 0, d0, jnp.where(lane == 1, d1, 0.0)).T[0:2, :]


def put_route_grads(refs, m0, m1, g0, g1, diff):
    grads = jnp.concatenate([(g0 * diff).astype(BF16), (g1 * diff).astype(BF16)], axis=0)
    put(refs, dot(jnp.concatenate([m0, m1], axis=1), grads))


def pack_near_kernel(own_ref, routes_ref, gates_ref, tokens_ref, meta_ref, *rows_refs):
    del own_ref
    meta = jnp.concatenate(
        [
            routes_ref[...].astype(F32),
            gates_ref[...],
            jnp.zeros((4, routes_ref.shape[1]), F32),
        ],
        axis=0,
    )
    meta_ref[...] = meta
    m0, m1 = masks_of(meta, rows_refs)
    put(rows_refs, dot(m0 + m1, tokens_ref[...]))


def pack_far_kernel(meta_ref, tokens_ref, *rows_refs):
    m0, m1 = masks_of(meta_ref[...], rows_refs)
    put(rows_refs, dot(m0 + m1, tokens_ref[...]))


def forward_kernel(pieces, own_ref, other_ref, *refs):
    ins, outs, refs = refs[:pieces], refs[pieces : 2 * pieces], refs[2 * pieces :]
    sent_ref, hid_own_ref, fa_ref, fb_ref = refs
    x = get(ins)
    put_columns(sent_ref, x)
    units, width = other_ref.shape[1:]
    hidden = []
    for w_ref, first in ((own_ref, 0), (other_ref, units)):
        both = dot(w_ref[0:2].reshape(2 * units, width), x, LAST)
        gate, up = both[:units], both[units:]
        sig = 0.5 * jnp.tanh(0.5 * gate) + 0.5
        silu = gate * sig
        hidden.append((silu * up).astype(BF16))
        fa_ref[first : first + units, :] = (up * (sig + silu * (1.0 - sig))).astype(BF16)
        fb_ref[first : first + units, :] = silu.astype(BF16)
    hid_own_ref[...] = hidden[0]
    put_rows(sent_ref, width // x.shape[0], hidden[1])
    put(outs, dot(hidden[0], own_ref[2], FIRST) + dot(hidden[1], other_ref[2], FIRST))


def backward_kernel(pieces, own_ref, other_ref, fa_ref, fb_ref, *refs):
    ins, outs, refs = refs[:pieces], refs[pieces : 2 * pieces], refs[2 * pieces :]
    sent_ref, dgu_own_ref = refs
    rg = get(ins)
    put_columns(sent_ref, rg)
    units, width = own_ref.shape[1:]
    both = []
    for w_ref, first in ((own_ref, 0), (other_ref, units)):
        at = slice(first, first + units)
        dh = dot(w_ref[2], rg, LAST)
        dg = (dh * fa_ref[at, :].astype(F32)).astype(BF16)
        du = (dh * fb_ref[at, :].astype(F32)).astype(BF16)
        both.append(jnp.concatenate([dg, du], axis=0))
    dgu_own_ref[...] = both[0]
    put_rows(sent_ref, width // rg.shape[0], both[1])
    put(
        outs,
        dot(both[0], own_ref[0:2].reshape(2 * units, width), FIRST)
        + dot(both[1], other_ref[0:2].reshape(2 * units, width), FIRST),
    )


def near_sum_kernel(meta_ref, teacher_ref, *refs):
    ins, out_ref = refs[:-1], refs[-1]
    total = route_sums(meta_ref[...], ins)[-1]
    out_ref[...] = (total - teacher_ref[...].astype(F32)).astype(BF16)


def far_grad_kernel(pieces, meta_ref, rest_ref, *refs):
    ins, part_ref, d_gates_ref, outs = (
        refs[:pieces],
        refs[pieces],
        refs[pieces + 1],
        refs[pieces + 2 :],
    )
    m0, m1, g0, g1, o0, o1, total = route_sums(meta_ref[...], ins)
    part_ref[...] = total.astype(BF16)
    diff = total + rest_ref[...].astype(F32)
    put_route_grads(outs, m0, m1, g0, g1, diff)
    put_d_gates(d_gates_ref, diff, o0, o1)


def near_grad_kernel(pieces, meta_ref, teacher_ref, part_ref, *refs):
    ins, student_ref, d_gates_ref, outs = (
        refs[:pieces],
        refs[pieces],
        refs[pieces + 1],
        refs[pieces + 2 :],
    )
    m0, m1, g0, g1, o0, o1, total = route_sums(meta_ref[...], ins)
    total = total + part_ref[...].astype(F32)
    student_ref[...] = total.astype(BF16)
    diff = total - teacher_ref[...].astype(F32)
    put_route_grads(outs, m0, m1, g0, g1, diff)
    put_d_gates(d_gates_ref, diff, o0, o1)


def far_back_kernel(meta_ref, d_gates_ref, *refs):
    ins, out_ref = refs[:-1], refs[-1]
    m0, m1 = masks_of(meta_ref[...], ins)
    tok = m0.shape[1]
    out_ref[:tok, :] = dot(m0 + m1, get(ins), FIRST).astype(BF16)
    value = d_gates_ref[...]
    high = value.astype(BF16)
    low = (value - high.astype(F32)).astype(BF16)
    rest = jnp.zeros((out_ref.shape[0] - tok - 4, tok), BF16)
    out_ref[tok:, :tok] = jnp.concatenate([high, low, rest], axis=0)
    out_ref[tok:, tok:] = jnp.zeros((out_ref.shape[0] - tok, out_ref.shape[1] - tok), BF16)


def final_kernel(pieces, meta_ref, part_ref, near_ref, *refs):
    ins, out_ref, d_gates_ref = refs[:pieces], refs[pieces], refs[pieces + 1]
    m0, m1 = masks_of(meta_ref[...], ins)
    tok = m0.shape[1]
    total = dot(m0 + m1, get(ins), FIRST) + part_ref[:tok, :].astype(F32)
    out_ref[...] = total.astype(BF16)
    far = part_ref[tok:, :tok].astype(F32)
    d_gates_ref[...] = near_ref[...] + (far[0:2] + far[2:4])


def weight_blocks(across, x, sent_x, g, sent_g, d, h):
    units, side = h.shape

    def acts(own, sent, first):
        blocks = range(across + first // side, across + (first + units) // side)
        theirs = jnp.concatenate([sent[i] for i in blocks], axis=0)
        return jnp.concatenate([own[first : first + units, :], theirs], axis=1)

    for row, own, sent, rows, first in (
        (2, h, sent_x, (g, sent_g), 0),
        (0, d, sent_g, (x, sent_x), 0),
        (1, d, sent_g, (x, sent_x), units),
    ):
        for i in range(across):
            column = jnp.concatenate([r[i] for r in rows], axis=0)
            yield row, i, dot(acts(own, sent, first), column)


def weight_far_kernel(across, x, sent_x, g, sent_g, d, h, out_ref, tiny_ref):
    tiny_ref[...] = jnp.zeros_like(tiny_ref)
    side = h.shape[1]
    for row, i, value in weight_blocks(across, x, sent_x, g, sent_g, d, h):
        out_ref[row, :, i * side : (i + 1) * side] = value.astype(BF16)


def weight_near_kernel(
    across, far_ref, x, sent_x, g, sent_g, d, h, out_hbm, tiny_ref, buf, sems
):
    tiny_ref[...] = jnp.zeros_like(tiny_ref)
    side = h.shape[1]
    copies = []
    for row, i, value in weight_blocks(across, x, sent_x, g, sent_g, d, h):
        at = pl.ds(i * side, side)
        buf[row, :, at] = (value + far_ref[row, :, at].astype(F32)).astype(BF16)
        copies.append(
            pltpu.make_async_copy(buf.at[row, :, at], out_hbm.at[row, :, at], sems.at[row, i])
        )
        copies[-1].start()
    for copy in copies:
        copy.wait()


def order_kernel():
    pass


def local(tokens, teacher, routes, gate_weights, weights):
    tok, width = tokens.shape
    experts = lax.axis_size("expert")
    half = experts // 2
    capacity = 4 * tok // experts
    rows = half * capacity
    units = weights.shape[1]

    pieces = [jax.ShapeDtypeStruct((capacity, width), BF16)] * half
    dense = jax.ShapeDtypeStruct((tok, width), BF16)
    longer = jax.ShapeDtypeStruct((tok + 16, width), BF16)
    pair = jax.ShapeDtypeStruct((2, tok), F32)
    acts = jax.ShapeDtypeStruct((units, rows), BF16)
    across, along = width // rows, units // rows
    sent_x = jax.ShapeDtypeStruct((across + along, rows, rows), BF16)
    sent_g = jax.ShapeDtypeStruct((across + 2 * along, rows, rows), BF16)
    acts2 = jax.ShapeDtypeStruct((2 * units, rows), BF16)
    tiny = jax.ShapeDtypeStruct((8, 128), F32)
    vspec = pl.BlockSpec(memory_space=pltpu.VMEM)
    aspec = pl.BlockSpec(memory_space=pl.ANY)

    def call(
        kernel,
        name,
        out_shape,
        specs,
        *args,
        after=(),
        through=(),
        limit=8,
        scratch=(),
        in_hbm=0,
    ):
        many = isinstance(out_shape, list)
        specs = list(specs) + [vspec] * (len(args) - len(specs))
        inputs = len(args) + len(after) + len(through)
        outputs = len(out_shape) if many else 1

        def body(*refs):
            kernel(
                *refs[: len(args)],
                *refs[inputs : inputs + outputs],
                *refs[inputs + outputs + len(through) :],
            )

        out_specs = [aspec] * in_hbm + [vspec] * (outputs - in_hbm) + [aspec] * len(through)
        out_shapes = (out_shape if many else [out_shape]) + [
            jax.ShapeDtypeStruct(a.shape, a.dtype) for a in through
        ]
        single = not many and not through
        return pl.pallas_call(
            body,
            in_specs=specs + [aspec] * (len(after) + len(through)),
            out_specs=out_specs[0] if single else out_specs,
            out_shape=out_shapes[0] if single else out_shapes,
            input_output_aliases={
                len(args) + len(after) + i: outputs + i for i in range(len(through))
            },
            scratch_shapes=scratch,
            cost_estimate=pl.CostEstimate(
                flops=FLOPS.get(name, 10**8), bytes_accessed=2 * MIB, transcendentals=0
            ),
            compiler_params=pltpu.CompilerParams(vmem_limit_bytes=limit * MIB),
            name=name,
        )(*args, *after, *through)

    def within_half(rows_of):
        return [rows_of[0]] + [
            lax.ppermute(rows_of[s], "expert", [(i, i ^ s) for i in range(experts)])
            for s in range(half - 1, 0, -1)
        ]

    def to_mirror(x):
        return lax.ppermute(x, "expert", [(i, i ^ half) for i in range(experts)])

    def to_sibling(x):
        return lax.ppermute(x, "dp", [(0, 1), (1, 0)])

    far_tokens = to_mirror(tokens)
    own = weights[0].transpose(1, 0, 2)
    other = to_sibling(own)

    def forward(x_pieces, name, after=()):
        res = call(
            functools.partial(forward_kernel, half),
            name,
            pieces + [sent_x, acts, acts2, acts2],
            [],
            own,
            other,
            *x_pieces,
            after=after,
            limit=20,
        )
        return res[:half], res[half:]

    def backward(rg_pieces, fa, fb, name, after=(), through=()):
        res = call(
            functools.partial(backward_kernel, half),
            name,
            pieces + [sent_g, acts2],
            [],
            own,
            other,
            fa,
            fb,
            *rg_pieces,
            after=after,
            through=through,
            limit=20,
        )
        return res[:half], res[half:]

    res = call(
        pack_near_kernel,
        "pack_near",
        [jax.ShapeDtypeStruct((8, tok), F32)] + pieces,
        [],
        own,
        routes.T,
        gate_weights.T,
        tokens,
        limit=10,
    )
    meta, x_near = res[0], within_half(res[1:])
    far_meta = to_mirror(meta)
    x_far = within_half(
        call(pack_far_kernel, "pack_far", pieces, [], far_meta, far_tokens)
    )

    out_near, (xn, hn, fan, fbn) = forward(x_near, "forward_near")
    got_near = within_half(out_near)
    out_far, (xf, hf, faf, fbf) = forward(x_far, "forward_far", after=[xn])
    rest_rows, *out_far = call(
        near_sum_kernel,
        "near_sum",
        dense,
        [],
        meta,
        teacher,
        *got_near,
        through=out_far,
    )
    rest = to_mirror(rest_rows)
    xf_sib, xn_sib = to_sibling(xf), to_sibling(xn)
    out_far = call(order_kernel, "order_return", [], [], after=[xn_sib], through=out_far)
    (rest,) = call(order_kernel, "order_rest", [], [], after=out_far[:1], through=[rest])
    got_far = within_half(out_far)

    res = call(
        functools.partial(far_grad_kernel, half),
        "far_grad",
        [dense, pair] + pieces,
        [],
        far_meta,
        rest,
        *got_far,
        after=[xf_sib, xn_sib],
    )
    part, d_gates_far, rg_far = to_mirror(res[0]), res[1], within_half(res[2:])
    grad_far, (gf, df) = backward(rg_far, faf, fbf, "backward_far")
    res = call(
        functools.partial(near_grad_kernel, half),
        "near_grad",
        [dense, pair] + pieces,
        [],
        meta,
        teacher,
        part,
        *got_near,
        after=[df],
    )
    student, d_gates_near, rg_near = res[0], res[1], within_half(res[2:])

    back_far = within_half(grad_far)
    gf_sib = to_sibling(gf)
    part_rows = call(
        far_back_kernel, "far_back", longer, [], far_meta, d_gates_far, *back_far
    )
    part = to_mirror(part_rows)
    far_weights, far_done = call(
        functools.partial(weight_far_kernel, across),
        "weight_far",
        [jax.ShapeDtypeStruct((3, units, width), BF16), tiny],
        [],
        *(xf, xf_sib, gf, gf_sib, df, hf),
        after=[part_rows],
        limit=16,
    )
    grad_near, (gn, dn) = backward(rg_near, fan, fbn, "backward_near", after=[part_rows, gf_sib, far_done])
    gn_sib = to_sibling(gn)
    back_near = within_half(grad_near)

    part, dn = call(order_kernel, "order_back", [], [], through=[part, dn])
    weight_grads, finished = call(
        functools.partial(weight_near_kernel, across),
        "weight_near",
        [jax.ShapeDtypeStruct((3, units, width), BF16), tiny],
        [],
        *(far_weights, xn, xn_sib, gn, gn_sib, dn, hn),
        limit=24,
        scratch=[
            pltpu.VMEM((3, units, width), BF16),
            pltpu.SemaphoreType.DMA((3, across)),
        ],
        in_hbm=1,
    )

    d_tokens, d_gates = call(
        functools.partial(final_kernel, half),
        "combine_gradients",
        [dense, pair],
        [],
        meta,
        part,
        d_gates_near,
        *back_near,
        after=[finished],
    )
    return (student, d_tokens, d_gates.T, weight_grads.transpose(1, 0, 2)[None])


def solution(mesh):
    rows = P(("groups", "expert", "dp"), None)
    return jax.shard_map(
        local,
        mesh=mesh,
        in_specs=(rows, rows, rows, rows, P("expert", "dp", None, None)),
        out_specs=(rows, rows, rows, P(("groups", "expert"), "dp", None, None)),
        check_vma=False,
    )
```

```python
import functools

import jax
import jax.numpy as jnp
from jax import lax
from jax.experimental import pallas as pl
from jax.experimental.pallas import tpu as pltpu
from jax.sharding import PartitionSpec as P

PLAIN = (((1,), (0,)), ((), ()))
LAST = (((1,), (1,)), ((), ()))
FIRST = (((0,), (0,)), ((), ()))
MIB = 1024 * 1024
F32 = jnp.float32
BF16 = jnp.bfloat16
FLOPS = {
    "pack_near": 30000000000,
    "pack_far": 30000000000,
    "forward_near": 100000000,
    "forward_far": 3000000000,
    "near_sum": 30000000000,
    "far_grad": 10000000000,
    "near_grad": 30000000000,
    "backward_far": 3000000000,
    "backward_near": 10000000000,
    "far_back": 10000000000,
    "weight_near": 30000000000,
    "combine_gradients": 30000000000,
    "order_rest": 30000000000,
    "order_back": 30000000000,
    "order_return": 0,
    "weight_far": 2400000000,
}


def dot(a, b, dims=PLAIN):
    return lax.dot_general(a, b, dims, preferred_element_type=F32)


def slot_masks(me, meta, pieces, capacity):
    tok = meta.shape[1]
    expert_of = (lax.broadcasted_iota(jnp.int32, (pieces, tok), 0) ^ me).astype(F32)
    first, second = meta[0:1, :] == expert_of, meta[1:2, :] == expert_of
    chosen = jnp.where(first | second, 1.0, 0.0).astype(BF16)
    before = lax.broadcasted_iota(jnp.int32, (tok, tok), 0) < lax.broadcasted_iota(
        jnp.int32, (tok, tok), 1
    )
    rank = dot(chosen, jnp.where(before, 1.0, 0.0).astype(BF16))
    rank0 = jnp.where(first, rank, -1.0)
    rank1 = jnp.where(second, rank, -1.0)
    place = lax.broadcasted_iota(jnp.int32, (capacity, tok), 0).astype(F32)

    def expand(ranks):
        return jnp.concatenate(
            [
                jnp.where(ranks[s : s + 1, :] == place, 1.0, 0.0).astype(BF16)
                for s in range(pieces)
            ],
            axis=0,
        )

    return expand(rank0), expand(rank1)


def put(refs, rows):
    capacity = refs[0].shape[0]
    for s, ref in enumerate(refs):
        ref[...] = rows[s * capacity : (s + 1) * capacity].astype(ref.dtype)


def put_columns(ref, rows):
    side = rows.shape[0]
    for i in range(rows.shape[1] // side):
        ref[i] = rows[:, i * side : (i + 1) * side]


def put_rows(ref, first, value):
    side = value.shape[1]
    for i in range(value.shape[0] // side):
        ref[first + i] = value[i * side : (i + 1) * side, :]


def get_columns(ref):
    return jnp.concatenate([ref[i] for i in range(ref.shape[0])], axis=1)


def get(refs):
    refs = refs[:1] + refs[:0:-1]
    return jnp.concatenate([ref[...] for ref in refs], axis=0)


def keep_masks(masks_ref, meta, refs):
    m0, m1 = slot_masks(lax.axis_index("expert"), meta, len(refs), refs[0].shape[0])
    masks_ref[0] = m0
    masks_ref[1] = m1
    return m0 + m1


def gate_columns(meta):
    columns = meta.T
    return columns[:, 2:3], columns[:, 3:4]


def route_sums(meta, masks_ref, refs):
    m0, m1 = masks_ref[0], masks_ref[1]
    got = get(refs)
    g0, g1 = gate_columns(meta)
    o0, o1 = dot(m0, got, FIRST), dot(m1, got, FIRST)
    return m0, m1, g0, g1, o0, o1, g0 * o0 + g1 * o1


def put_d_gates(ref, diff, o0, o1):
    tok = diff.shape[0]
    lane = lax.broadcasted_iota(jnp.int32, (tok, 128), 1)
    d0 = jnp.sum(diff * o0, axis=1, keepdims=True)
    d1 = jnp.sum(diff * o1, axis=1, keepdims=True)
    ref[...] = jnp.where(lane == 0, d0, jnp.where(lane == 1, d1, 0.0)).T[0:2, :]


def put_route_grads(refs, m0, m1, g0, g1, diff):
    grads = jnp.concatenate([(g0 * diff).astype(BF16), (g1 * diff).astype(BF16)], axis=0)
    put(refs, dot(jnp.concatenate([m0, m1], axis=1), grads))


def pack_near_kernel(
    own_ref, routes_ref, gates_ref, tokens_ref, meta_ref, masks_ref, *rows_refs
):
    del own_ref
    meta = jnp.concatenate(
        [
            routes_ref[...].astype(F32),
            gates_ref[...],
            jnp.zeros((4, routes_ref.shape[1]), F32),
        ],
        axis=0,
    )
    meta_ref[...] = meta
    put(rows_refs, dot(keep_masks(masks_ref, meta, rows_refs), tokens_ref[...]))


def pack_far_kernel(meta_ref, tokens_ref, masks_ref, *rows_refs):
    put(rows_refs, dot(keep_masks(masks_ref, meta_ref[...], rows_refs), tokens_ref[...]))


def forward_kernel(pieces, own_ref, other_ref, *refs):
    ins, outs, refs = refs[:pieces], refs[pieces : 2 * pieces], refs[2 * pieces :]
    sent_ref, hid_own_ref, fa_ref, fb_ref = refs
    x = get(ins)
    put_columns(sent_ref, x)
    units, width = other_ref.shape[1:]
    hidden = []
    for w_ref, first in ((own_ref, 0), (other_ref, units)):
        both = dot(w_ref[0:2].reshape(2 * units, width), x, LAST)
        gate, up = both[:units], both[units:]
        sig = 0.5 * jnp.tanh(0.5 * gate) + 0.5
        silu = gate * sig
        hidden.append((silu * up).astype(BF16))
        fa_ref[first : first + units, :] = (up * (sig + silu * (1.0 - sig))).astype(BF16)
        fb_ref[first : first + units, :] = silu.astype(BF16)
    hid_own_ref[...] = hidden[0]
    put_rows(sent_ref, width // x.shape[0], hidden[1])
    put(outs, dot(hidden[0], own_ref[2], FIRST) + dot(hidden[1], other_ref[2], FIRST))


def backward_kernel(pieces, own_ref, other_ref, fa_ref, fb_ref, *refs):
    ins, outs, refs = refs[:pieces], refs[pieces : 2 * pieces], refs[2 * pieces :]
    sent_ref, dgu_own_ref = refs
    rg = get(ins)
    put_columns(sent_ref, rg)
    units, width = own_ref.shape[1:]
    both = []
    for w_ref, first in ((own_ref, 0), (other_ref, units)):
        at = slice(first, first + units)
        dh = dot(w_ref[2], rg, LAST)
        dg = (dh * fa_ref[at, :].astype(F32)).astype(BF16)
        du = (dh * fb_ref[at, :].astype(F32)).astype(BF16)
        both.append(jnp.concatenate([dg, du], axis=0))
    dgu_own_ref[...] = both[0]
    put_rows(sent_ref, width // rg.shape[0], both[1])
    put(
        outs,
        dot(both[0], own_ref[0:2].reshape(2 * units, width), FIRST)
        + dot(both[1], other_ref[0:2].reshape(2 * units, width), FIRST),
    )


def near_sum_kernel(meta_ref, masks_ref, teacher_ref, *refs):
    ins, out_ref = refs[:-1], refs[-1]
    total = route_sums(meta_ref[...], masks_ref, ins)[-1]
    out_ref[...] = (total - teacher_ref[...].astype(F32)).astype(BF16)


def far_grad_kernel(pieces, meta_ref, masks_ref, rest_ref, *refs):
    ins, part_ref, d_gates_ref, outs = (
        refs[:pieces],
        refs[pieces],
        refs[pieces + 1],
        refs[pieces + 2 :],
    )
    m0, m1, g0, g1, o0, o1, total = route_sums(meta_ref[...], masks_ref, ins)
    part_ref[...] = total.astype(BF16)
    diff = total + rest_ref[...].astype(F32)
    put_route_grads(outs, m0, m1, g0, g1, diff)
    put_d_gates(d_gates_ref, diff, o0, o1)


def near_grad_kernel(pieces, meta_ref, masks_ref, teacher_ref, part_ref, *refs):
    ins, student_ref, d_gates_ref, outs = (
        refs[:pieces],
        refs[pieces],
        refs[pieces + 1],
        refs[pieces + 2 :],
    )
    m0, m1, g0, g1, o0, o1, total = route_sums(meta_ref[...], masks_ref, ins)
    total = total + part_ref[...].astype(F32)
    student_ref[...] = total.astype(BF16)
    diff = total - teacher_ref[...].astype(F32)
    put_route_grads(outs, m0, m1, g0, g1, diff)
    put_d_gates(d_gates_ref, diff, o0, o1)


def far_back_kernel(masks_ref, d_gates_ref, *refs):
    ins, out_ref = refs[:-1], refs[-1]
    tok = masks_ref.shape[2]
    out_ref[:tok, :] = dot(masks_ref[0] + masks_ref[1], get(ins), FIRST).astype(BF16)
    value = d_gates_ref[...]
    high = value.astype(BF16)
    low = (value - high.astype(F32)).astype(BF16)
    rest = jnp.zeros((out_ref.shape[0] - tok - 4, tok), BF16)
    out_ref[tok:, :tok] = jnp.concatenate([high, low, rest], axis=0)
    out_ref[tok:, tok:] = jnp.zeros((out_ref.shape[0] - tok, out_ref.shape[1] - tok), BF16)


def final_kernel(pieces, masks_ref, part_ref, near_ref, student_ref, *refs):
    ins, student_hbm, out_ref, d_gates_ref, sem = refs[:pieces], *refs[pieces:]
    copy = pltpu.make_async_copy(student_ref, student_hbm, sem)
    copy.start()
    tok = masks_ref.shape[2]
    total = dot(masks_ref[0] + masks_ref[1], get(ins), FIRST) + part_ref[:tok, :].astype(F32)
    out_ref[...] = total.astype(BF16)
    far = part_ref[tok:, :tok].astype(F32)
    d_gates_ref[...] = near_ref[...] + (far[0:2] + far[2:4])
    copy.wait()


def weight_blocks(across, x, sent_x, g, sent_g, d, h):
    units, side = h.shape

    def acts(own, sent, first):
        blocks = range(across + first // side, across + (first + units) // side)
        theirs = jnp.concatenate([sent[i] for i in blocks], axis=0)
        return jnp.concatenate([own[first : first + units, :], theirs], axis=1)

    for row, own, sent, rows, first in (
        (2, h, sent_x, (g, sent_g), 0),
        (0, d, sent_g, (x, sent_x), 0),
        (1, d, sent_g, (x, sent_x), units),
    ):
        for i in range(across):
            column = jnp.concatenate([r[i] for r in rows], axis=0)
            yield row, i, dot(acts(own, sent, first), column)


def weight_far_kernel(across, x, sent_x, g, sent_g, d, h, out_ref, tiny_ref):
    tiny_ref[...] = jnp.zeros_like(tiny_ref)
    side = h.shape[1]
    for row, i, value in weight_blocks(across, x, sent_x, g, sent_g, d, h):
        out_ref[row, :, i * side : (i + 1) * side] = value.astype(BF16)


def weight_near_kernel(
    across, far_ref, x, sent_x, g, sent_g, d, h, out_hbm, tiny_ref, buf, sems
):
    tiny_ref[...] = jnp.zeros_like(tiny_ref)
    side = h.shape[1]
    copies = []
    for row, i, value in weight_blocks(across, x, sent_x, g, sent_g, d, h):
        at = pl.ds(i * side, side)
        buf[row, :, at] = (value + far_ref[row, :, at].astype(F32)).astype(BF16)
        copies.append(
            pltpu.make_async_copy(buf.at[row, :, at], out_hbm.at[row, :, at], sems.at[row, i])
        )
        copies[-1].start()
    for copy in copies:
        copy.wait()


def order_kernel():
    pass


def local(tokens, teacher, routes, gate_weights, weights):
    tok, width = tokens.shape
    experts = lax.axis_size("expert")
    half = experts // 2
    capacity = 4 * tok // experts
    rows = half * capacity
    units = weights.shape[1]

    pieces = [jax.ShapeDtypeStruct((capacity, width), BF16)] * half
    dense = jax.ShapeDtypeStruct((tok, width), BF16)
    longer = jax.ShapeDtypeStruct((tok + 16, width), BF16)
    pair = jax.ShapeDtypeStruct((2, tok), F32)
    acts = jax.ShapeDtypeStruct((units, rows), BF16)
    across, along = width // rows, units // rows
    sent_x = jax.ShapeDtypeStruct((across + along, rows, rows), BF16)
    sent_g = jax.ShapeDtypeStruct((across + 2 * along, rows, rows), BF16)
    acts2 = jax.ShapeDtypeStruct((2 * units, rows), BF16)
    tiny = jax.ShapeDtypeStruct((8, 128), F32)
    masks = jax.ShapeDtypeStruct((2, rows, tok), BF16)
    vspec = pl.BlockSpec(memory_space=pltpu.VMEM)
    aspec = pl.BlockSpec(memory_space=pl.ANY)

    def call(
        kernel,
        name,
        out_shape,
        specs,
        *args,
        after=(),
        through=(),
        limit=8,
        scratch=(),
        in_hbm=0,
    ):
        many = isinstance(out_shape, list)
        specs = list(specs) + [vspec] * (len(args) - len(specs))
        inputs = len(args) + len(after) + len(through)
        outputs = len(out_shape) if many else 1

        def body(*refs):
            kernel(
                *refs[: len(args)],
                *refs[inputs : inputs + outputs],
                *refs[inputs + outputs + len(through) :],
            )

        out_specs = [aspec] * in_hbm + [vspec] * (outputs - in_hbm) + [aspec] * len(through)
        out_shapes = (out_shape if many else [out_shape]) + [
            jax.ShapeDtypeStruct(a.shape, a.dtype) for a in through
        ]
        single = not many and not through
        return pl.pallas_call(
            body,
            in_specs=specs + [aspec] * (len(after) + len(through)),
            out_specs=out_specs[0] if single else out_specs,
            out_shape=out_shapes[0] if single else out_shapes,
            input_output_aliases={
                len(args) + len(after) + i: outputs + i for i in range(len(through))
            },
            scratch_shapes=scratch,
            cost_estimate=pl.CostEstimate(
                flops=FLOPS.get(name, 10**8), bytes_accessed=2 * MIB, transcendentals=0
            ),
            compiler_params=pltpu.CompilerParams(vmem_limit_bytes=limit * MIB),
            name=name,
        )(*args, *after, *through)

    def within_half(rows_of):
        return [rows_of[0]] + [
            lax.ppermute(rows_of[s], "expert", [(i, i ^ s) for i in range(experts)])
            for s in range(half - 1, 0, -1)
        ]

    def to_mirror(x):
        return lax.ppermute(x, "expert", [(i, i ^ half) for i in range(experts)])

    def to_sibling(x):
        return lax.ppermute(x, "dp", [(0, 1), (1, 0)])

    far_tokens = to_mirror(tokens)
    own = weights[0].transpose(1, 0, 2)
    other = to_sibling(own)

    def forward(x_pieces, name, after=()):
        res = call(
            functools.partial(forward_kernel, half),
            name,
            pieces + [sent_x, acts, acts2, acts2],
            [],
            own,
            other,
            *x_pieces,
            after=after,
            limit=20,
        )
        return res[:half], res[half:]

    def backward(rg_pieces, fa, fb, name, after=(), through=()):
        res = call(
            functools.partial(backward_kernel, half),
            name,
            pieces + [sent_g, acts2],
            [],
            own,
            other,
            fa,
            fb,
            *rg_pieces,
            after=after,
            through=through,
            limit=20,
        )
        return res[:half], res[half:]

    res = call(
        pack_near_kernel,
        "pack_near",
        [jax.ShapeDtypeStruct((8, tok), F32), masks] + pieces,
        [],
        own,
        routes.T,
        gate_weights.T,
        tokens,
        limit=10,
    )
    meta, near_masks, x_near = res[0], res[1], within_half(res[2:])
    far_meta = to_mirror(meta)
    res = call(pack_far_kernel, "pack_far", [masks] + pieces, [], far_meta, far_tokens)
    far_masks, x_far = res[0], within_half(res[1:])

    out_near, (xn, hn, fan, fbn) = forward(x_near, "forward_near")
    got_near = within_half(out_near)
    out_far, (xf, hf, faf, fbf) = forward(x_far, "forward_far", after=[xn])
    rest_rows, *out_far = call(
        near_sum_kernel,
        "near_sum",
        dense,
        [],
        meta,
        near_masks,
        teacher,
        *got_near,
        through=out_far,
    )
    rest = to_mirror(rest_rows)
    xf_sib, xn_sib = to_sibling(xf), to_sibling(xn)
    out_far = call(order_kernel, "order_return", [], [], after=[xn_sib], through=out_far)
    (rest,) = call(order_kernel, "order_rest", [], [], after=out_far[:1], through=[rest])
    got_far = within_half(out_far)

    res = call(
        functools.partial(far_grad_kernel, half),
        "far_grad",
        [dense, pair] + pieces,
        [],
        far_meta,
        far_masks,
        rest,
        *got_far,
        after=[xf_sib, xn_sib],
    )
    part, d_gates_far, rg_far = to_mirror(res[0]), res[1], within_half(res[2:])
    grad_far, (gf, df) = backward(rg_far, faf, fbf, "backward_far")
    res = call(
        functools.partial(near_grad_kernel, half),
        "near_grad",
        [dense, pair] + pieces,
        [],
        meta,
        near_masks,
        teacher,
        part,
        *got_near,
        after=[df],
    )
    student, d_gates_near, rg_near = res[0], res[1], within_half(res[2:])

    back_far = within_half(grad_far)
    gf_sib = to_sibling(gf)
    part_rows = call(
        far_back_kernel, "far_back", longer, [], far_masks, d_gates_far, *back_far
    )
    part = to_mirror(part_rows)
    far_weights, far_done = call(
        functools.partial(weight_far_kernel, across),
        "weight_far",
        [jax.ShapeDtypeStruct((3, units, width), BF16), tiny],
        [],
        *(xf, xf_sib, gf, gf_sib, df, hf),
        after=[part_rows],
        limit=16,
    )
    grad_near, (gn, dn) = backward(rg_near, fan, fbn, "backward_near", after=[part_rows, gf_sib, far_done])
    gn_sib = to_sibling(gn)
    back_near = within_half(grad_near)

    part, dn = call(order_kernel, "order_back", [], [], through=[part, dn])
    weight_grads, finished = call(
        functools.partial(weight_near_kernel, across),
        "weight_near",
        [jax.ShapeDtypeStruct((3, units, width), BF16), tiny],
        [],
        *(far_weights, xn, xn_sib, gn, gn_sib, dn, hn),
        limit=24,
        scratch=[
            pltpu.VMEM((3, units, width), BF16),
            pltpu.SemaphoreType.DMA((3, across)),
        ],
        in_hbm=1,
    )

    student, d_tokens, d_gates = call(
        functools.partial(final_kernel, half),
        "combine_gradients",
        [dense, dense, pair],
        [],
        near_masks,
        part,
        d_gates_near,
        student,
        *back_near,
        after=[finished],
        scratch=[pltpu.SemaphoreType.DMA],
        in_hbm=1,
    )
    return (student, d_tokens, d_gates.T, weight_grads.transpose(1, 0, 2)[None])


def solution(mesh):
    rows = P(("groups", "expert", "dp"), None)
    return jax.shard_map(
        local,
        mesh=mesh,
        in_specs=(rows, rows, rows, rows, P("expert", "dp", None, None)),
        out_specs=(rows, rows, rows, P(("groups", "expert"), "dp", None, None)),
        check_vma=False,
    )
```

```python
import functools

import jax
import jax.numpy as jnp
from jax import lax
from jax.experimental import pallas as pl
from jax.experimental.pallas import tpu as pltpu
from jax.sharding import PartitionSpec as P

PLAIN = (((1,), (0,)), ((), ()))
LAST = (((1,), (1,)), ((), ()))
FIRST = (((0,), (0,)), ((), ()))
MIB = 1024 * 1024
F32 = jnp.float32
BF16 = jnp.bfloat16
FLOPS = {
    "pack_near": 30000000000,
    "pack_far": 30000000000,
    "forward_near": 100000000,
    "forward_far": 3000000000,
    "near_sum": 30000000000,
    "far_grad": 10000000000,
    "near_grad": 30000000000,
    "backward_far": 3000000000,
    "backward_near": 10000000000,
    "far_back": 10000000000,
    "weight_near": 30000000000,
    "combine_gradients": 30000000000,
    "order_rest": 30000000000,
    "order_back": 30000000000,
    "order_return": 0,
    "weight_far": 2400000000,
}


def dot(a, b, dims=PLAIN):
    return lax.dot_general(a, b, dims, preferred_element_type=F32)


def slot_masks(me, meta, pieces, capacity):
    tok = meta.shape[1]
    expert_of = (lax.broadcasted_iota(jnp.int32, (pieces, tok), 0) ^ me).astype(F32)
    first, second = meta[0:1, :] == expert_of, meta[1:2, :] == expert_of
    chosen = jnp.where(first | second, 1.0, 0.0).astype(BF16)
    before = lax.broadcasted_iota(jnp.int32, (tok, tok), 0) < lax.broadcasted_iota(
        jnp.int32, (tok, tok), 1
    )
    rank = dot(chosen, jnp.where(before, 1.0, 0.0).astype(BF16))
    rank0 = jnp.where(first, rank, -1.0)
    rank1 = jnp.where(second, rank, -1.0)
    place = lax.broadcasted_iota(jnp.int32, (capacity, tok), 0).astype(F32)

    def expand(ranks):
        return jnp.concatenate(
            [
                jnp.where(ranks[s : s + 1, :] == place, 1.0, 0.0).astype(BF16)
                for s in range(pieces)
            ],
            axis=0,
        )

    return expand(rank0), expand(rank1)


def put(refs, rows):
    capacity = refs[0].shape[0]
    for s, ref in enumerate(refs):
        ref[...] = rows[s * capacity : (s + 1) * capacity].astype(ref.dtype)


def put_columns(ref, rows):
    side = rows.shape[0]
    for i in range(rows.shape[1] // side):
        ref[i] = rows[:, i * side : (i + 1) * side]


def put_rows(ref, first, value):
    side = value.shape[1]
    for i in range(value.shape[0] // side):
        ref[first + i] = value[i * side : (i + 1) * side, :]


def get_columns(ref):
    return jnp.concatenate([ref[i] for i in range(ref.shape[0])], axis=1)


def get(refs):
    refs = refs[:1] + refs[:0:-1]
    return jnp.concatenate([ref[...] for ref in refs], axis=0)


def keep_masks(masks_ref, meta, refs):
    m0, m1 = slot_masks(lax.axis_index("expert"), meta, len(refs), refs[0].shape[0])
    masks_ref[0] = m0
    masks_ref[1] = m1
    return m0 + m1


def gate_columns(meta):
    columns = meta.T
    return columns[:, 2:3], columns[:, 3:4]


def route_sums(meta, masks_ref, refs):
    m0, m1 = masks_ref[0], masks_ref[1]
    got = get(refs)
    g0, g1 = gate_columns(meta)
    o0, o1 = dot(m0, got, FIRST), dot(m1, got, FIRST)
    return m0, m1, g0, g1, o0, o1, g0 * o0 + g1 * o1


def put_d_gates(ref, diff, o0, o1):
    tok = diff.shape[0]
    lane = lax.broadcasted_iota(jnp.int32, (tok, 128), 1)
    d0 = jnp.sum(diff * o0, axis=1, keepdims=True)
    d1 = jnp.sum(diff * o1, axis=1, keepdims=True)
    ref[...] = jnp.where(lane == 0, d0, jnp.where(lane == 1, d1, 0.0)).T[0:2, :]


def put_route_grads(refs, m0, m1, g0, g1, diff):
    grads = jnp.concatenate([(g0 * diff).astype(BF16), (g1 * diff).astype(BF16)], axis=0)
    put(refs, dot(jnp.concatenate([m0, m1], axis=1), grads))


def pack_near_kernel(
    own_ref, routes_ref, gates_ref, tokens_ref, meta_ref, masks_ref, *rows_refs
):
    del own_ref
    meta = jnp.concatenate(
        [
            routes_ref[...].astype(F32),
            gates_ref[...],
            jnp.zeros((4, routes_ref.shape[1]), F32),
        ],
        axis=0,
    )
    meta_ref[...] = meta
    put(rows_refs, dot(keep_masks(masks_ref, meta, rows_refs), tokens_ref[...]))


def pack_far_kernel(meta_ref, tokens_ref, masks_ref, *rows_refs):
    put(rows_refs, dot(keep_masks(masks_ref, meta_ref[...], rows_refs), tokens_ref[...]))


def forward_kernel(pieces, own_ref, other_ref, *refs):
    ins, outs, refs = refs[:pieces], refs[pieces : 2 * pieces], refs[2 * pieces :]
    sent_ref, hid_own_ref, fa_ref, fb_ref = refs
    x = get(ins)
    put_columns(sent_ref, x)
    units, width = other_ref.shape[1:]
    halves = ((own_ref, 0), (other_ref, units))
    products = [dot(w_ref[0:2].reshape(2 * units, width), x, LAST) for w_ref, _ in halves]
    total = None
    for (w_ref, first), both in zip(halves, products):
        gate, up = both[:units], both[units:]
        sig = 0.5 * jnp.tanh(0.5 * gate) + 0.5
        silu = gate * sig
        hidden = (silu * up).astype(BF16)
        fa_ref[first : first + units, :] = (up * (sig + silu * (1.0 - sig))).astype(BF16)
        fb_ref[first : first + units, :] = silu.astype(BF16)
        if w_ref is own_ref:
            hid_own_ref[...] = hidden
        else:
            put_rows(sent_ref, width // x.shape[0], hidden)
        out = dot(hidden, w_ref[2], FIRST)
        total = out if total is None else total + out
    put(outs, total)


def backward_kernel(pieces, own_ref, other_ref, fa_ref, fb_ref, *refs):
    ins, outs, refs = refs[:pieces], refs[pieces : 2 * pieces], refs[2 * pieces :]
    sent_ref, dgu_own_ref = refs
    rg = get(ins)
    put_columns(sent_ref, rg)
    units, width = own_ref.shape[1:]
    halves = ((own_ref, 0), (other_ref, units))
    products = [dot(w_ref[2], rg, LAST) for w_ref, _ in halves]
    total = None
    for (w_ref, first), dh in zip(halves, products):
        at = slice(first, first + units)
        dg = (dh * fa_ref[at, :].astype(F32)).astype(BF16)
        du = (dh * fb_ref[at, :].astype(F32)).astype(BF16)
        dgu = jnp.concatenate([dg, du], axis=0)
        if w_ref is own_ref:
            dgu_own_ref[...] = dgu
        else:
            put_rows(sent_ref, width // rg.shape[0], dgu)
        out = dot(dgu, w_ref[0:2].reshape(2 * units, width), FIRST)
        total = out if total is None else total + out
    put(outs, total)


def near_sum_kernel(meta_ref, masks_ref, teacher_ref, *refs):
    ins, out_ref = refs[:-1], refs[-1]
    total = route_sums(meta_ref[...], masks_ref, ins)[-1]
    out_ref[...] = (total - teacher_ref[...].astype(F32)).astype(BF16)


def far_grad_kernel(pieces, meta_ref, masks_ref, rest_ref, *refs):
    ins, part_ref, d_gates_ref, outs = (
        refs[:pieces],
        refs[pieces],
        refs[pieces + 1],
        refs[pieces + 2 :],
    )
    m0, m1, g0, g1, o0, o1, total = route_sums(meta_ref[...], masks_ref, ins)
    part_ref[...] = total.astype(BF16)
    diff = total + rest_ref[...].astype(F32)
    put_route_grads(outs, m0, m1, g0, g1, diff)
    put_d_gates(d_gates_ref, diff, o0, o1)


def near_grad_kernel(pieces, meta_ref, masks_ref, teacher_ref, part_ref, *refs):
    ins, student_ref, d_gates_ref, outs = (
        refs[:pieces],
        refs[pieces],
        refs[pieces + 1],
        refs[pieces + 2 :],
    )
    m0, m1, g0, g1, o0, o1, total = route_sums(meta_ref[...], masks_ref, ins)
    total = total + part_ref[...].astype(F32)
    student_ref[...] = total.astype(BF16)
    diff = total - teacher_ref[...].astype(F32)
    put_route_grads(outs, m0, m1, g0, g1, diff)
    put_d_gates(d_gates_ref, diff, o0, o1)


def far_back_kernel(masks_ref, d_gates_ref, *refs):
    ins, out_ref = refs[:-1], refs[-1]
    tok = masks_ref.shape[2]
    out_ref[:tok, :] = dot(masks_ref[0] + masks_ref[1], get(ins), FIRST).astype(BF16)
    value = d_gates_ref[...]
    high = value.astype(BF16)
    low = (value - high.astype(F32)).astype(BF16)
    rest = jnp.zeros((out_ref.shape[0] - tok - 4, tok), BF16)
    out_ref[tok:, :tok] = jnp.concatenate([high, low, rest], axis=0)
    out_ref[tok:, tok:] = jnp.zeros((out_ref.shape[0] - tok, out_ref.shape[1] - tok), BF16)


def final_kernel(pieces, masks_ref, part_ref, near_ref, *refs):
    ins, out_ref, d_gates_ref = refs[:pieces], refs[pieces], refs[pieces + 1]
    tok = masks_ref.shape[2]
    total = dot(masks_ref[0] + masks_ref[1], get(ins), FIRST) + part_ref[:tok, :].astype(F32)
    out_ref[...] = total.astype(BF16)
    far = part_ref[tok:, :tok].astype(F32)
    d_gates_ref[...] = near_ref[...] + (far[0:2] + far[2:4])


def weight_blocks(across, x, sent_x, g, sent_g, d, h):
    units, side = h.shape

    def acts(own, sent, first):
        blocks = range(across + first // side, across + (first + units) // side)
        theirs = jnp.concatenate([sent[i] for i in blocks], axis=0)
        return jnp.concatenate([own[first : first + units, :], theirs], axis=1)

    for row, own, sent, rows, first in (
        (2, h, sent_x, (g, sent_g), 0),
        (0, d, sent_g, (x, sent_x), 0),
        (1, d, sent_g, (x, sent_x), units),
    ):
        for i in range(across):
            column = jnp.concatenate([r[i] for r in rows], axis=0)
            yield row, i, dot(acts(own, sent, first), column)


def weight_far_kernel(across, x, sent_x, g, sent_g, d, h, out_ref, tiny_ref):
    tiny_ref[...] = jnp.zeros_like(tiny_ref)
    side = h.shape[1]
    for row, i, value in weight_blocks(across, x, sent_x, g, sent_g, d, h):
        out_ref[row, :, i * side : (i + 1) * side] = value.astype(BF16)


def weight_near_kernel(
    across, far_ref, x, sent_x, g, sent_g, d, h, out_hbm, tiny_ref, buf, sems
):
    tiny_ref[...] = jnp.zeros_like(tiny_ref)
    side = h.shape[1]
    copies = []
    for row, i, value in weight_blocks(across, x, sent_x, g, sent_g, d, h):
        at = pl.ds(i * side, side)
        buf[row, :, at] = (value + far_ref[row, :, at].astype(F32)).astype(BF16)
        copies.append(
            pltpu.make_async_copy(buf.at[row, :, at], out_hbm.at[row, :, at], sems.at[row, i])
        )
        copies[-1].start()
    for copy in copies:
        copy.wait()


def order_kernel():
    pass


def local(tokens, teacher, routes, gate_weights, weights):
    tok, width = tokens.shape
    experts = lax.axis_size("expert")
    half = experts // 2
    capacity = 4 * tok // experts
    rows = half * capacity
    units = weights.shape[1]

    pieces = [jax.ShapeDtypeStruct((capacity, width), BF16)] * half
    dense = jax.ShapeDtypeStruct((tok, width), BF16)
    longer = jax.ShapeDtypeStruct((tok + 16, width), BF16)
    pair = jax.ShapeDtypeStruct((2, tok), F32)
    acts = jax.ShapeDtypeStruct((units, rows), BF16)
    across, along = width // rows, units // rows
    sent_x = jax.ShapeDtypeStruct((across + along, rows, rows), BF16)
    sent_g = jax.ShapeDtypeStruct((across + 2 * along, rows, rows), BF16)
    acts2 = jax.ShapeDtypeStruct((2 * units, rows), BF16)
    tiny = jax.ShapeDtypeStruct((8, 128), F32)
    masks = jax.ShapeDtypeStruct((2, rows, tok), BF16)
    vspec = pl.BlockSpec(memory_space=pltpu.VMEM)
    aspec = pl.BlockSpec(memory_space=pl.ANY)

    def call(
        kernel,
        name,
        out_shape,
        specs,
        *args,
        after=(),
        through=(),
        limit=8,
        scratch=(),
        in_hbm=0,
    ):
        many = isinstance(out_shape, list)
        specs = list(specs) + [vspec] * (len(args) - len(specs))
        inputs = len(args) + len(after) + len(through)
        outputs = len(out_shape) if many else 1

        def body(*refs):
            kernel(
                *refs[: len(args)],
                *refs[inputs : inputs + outputs],
                *refs[inputs + outputs + len(through) :],
            )

        out_specs = [aspec] * in_hbm + [vspec] * (outputs - in_hbm) + [aspec] * len(through)
        out_shapes = (out_shape if many else [out_shape]) + [
            jax.ShapeDtypeStruct(a.shape, a.dtype) for a in through
        ]
        single = not many and not through
        return pl.pallas_call(
            body,
            in_specs=specs + [aspec] * (len(after) + len(through)),
            out_specs=out_specs[0] if single else out_specs,
            out_shape=out_shapes[0] if single else out_shapes,
            input_output_aliases={
                len(args) + len(after) + i: outputs + i for i in range(len(through))
            },
            scratch_shapes=scratch,
            cost_estimate=pl.CostEstimate(
                flops=FLOPS.get(name, 10**8), bytes_accessed=2 * MIB, transcendentals=0
            ),
            compiler_params=pltpu.CompilerParams(vmem_limit_bytes=limit * MIB),
            name=name,
        )(*args, *after, *through)

    def within_half(rows_of):
        return [rows_of[0]] + [
            lax.ppermute(rows_of[s], "expert", [(i, i ^ s) for i in range(experts)])
            for s in range(half - 1, 0, -1)
        ]

    def to_mirror(x):
        return lax.ppermute(x, "expert", [(i, i ^ half) for i in range(experts)])

    def to_sibling(x):
        return lax.ppermute(x, "dp", [(0, 1), (1, 0)])

    far_tokens = to_mirror(tokens)
    own = weights[0].transpose(1, 0, 2)
    other = to_sibling(own)

    def forward(x_pieces, name, after=()):
        res = call(
            functools.partial(forward_kernel, half),
            name,
            pieces + [sent_x, acts, acts2, acts2],
            [],
            own,
            other,
            *x_pieces,
            after=after,
            limit=20,
        )
        return res[:half], res[half:]

    def backward(rg_pieces, fa, fb, name, after=(), through=()):
        res = call(
            functools.partial(backward_kernel, half),
            name,
            pieces + [sent_g, acts2],
            [],
            own,
            other,
            fa,
            fb,
            *rg_pieces,
            after=after,
            through=through,
            limit=20,
        )
        return res[:half], res[half:]

    res = call(
        pack_near_kernel,
        "pack_near",
        [jax.ShapeDtypeStruct((8, tok), F32), masks] + pieces,
        [],
        own,
        routes.T,
        gate_weights.T,
        tokens,
        limit=10,
    )
    meta, near_masks, x_near = res[0], res[1], within_half(res[2:])
    far_meta = to_mirror(meta)
    res = call(pack_far_kernel, "pack_far", [masks] + pieces, [], far_meta, far_tokens)
    far_masks, x_far = res[0], within_half(res[1:])

    out_near, (xn, hn, fan, fbn) = forward(x_near, "forward_near")
    got_near = within_half(out_near)
    out_far, (xf, hf, faf, fbf) = forward(x_far, "forward_far", after=[xn])
    rest_rows, *out_far = call(
        near_sum_kernel,
        "near_sum",
        dense,
        [],
        meta,
        near_masks,
        teacher,
        *got_near,
        through=out_far,
    )
    rest = to_mirror(rest_rows)
    xf_sib, xn_sib = to_sibling(xf), to_sibling(xn)
    out_far = call(order_kernel, "order_return", [], [], after=[xn_sib], through=out_far)
    (rest,) = call(order_kernel, "order_rest", [], [], after=out_far[:1], through=[rest])
    got_far = within_half(out_far)

    res = call(
        functools.partial(far_grad_kernel, half),
        "far_grad",
        [dense, pair] + pieces,
        [],
        far_meta,
        far_masks,
        rest,
        *got_far,
        after=[xf_sib, xn_sib],
    )
    part, d_gates_far, rg_far = to_mirror(res[0]), res[1], within_half(res[2:])
    grad_far, (gf, df) = backward(rg_far, faf, fbf, "backward_far")
    res = call(
        functools.partial(near_grad_kernel, half),
        "near_grad",
        [dense, pair] + pieces,
        [],
        meta,
        near_masks,
        teacher,
        part,
        *got_near,
        after=[df],
    )
    student, d_gates_near, rg_near = res[0], res[1], within_half(res[2:])

    back_far = within_half(grad_far)
    gf_sib = to_sibling(gf)
    part_rows = call(
        far_back_kernel, "far_back", longer, [], far_masks, d_gates_far, *back_far
    )
    part = to_mirror(part_rows)
    far_weights, far_done = call(
        functools.partial(weight_far_kernel, across),
        "weight_far",
        [jax.ShapeDtypeStruct((3, units, width), BF16), tiny],
        [],
        *(xf, xf_sib, gf, gf_sib, df, hf),
        after=[part_rows],
        limit=16,
    )
    grad_near, (gn, dn) = backward(rg_near, fan, fbn, "backward_near", after=[part_rows, gf_sib, far_done])
    gn_sib = to_sibling(gn)
    back_near = within_half(grad_near)

    part, dn = call(order_kernel, "order_back", [], [], through=[part, dn])
    weight_grads, finished = call(
        functools.partial(weight_near_kernel, across),
        "weight_near",
        [jax.ShapeDtypeStruct((3, units, width), BF16), tiny],
        [],
        *(far_weights, xn, xn_sib, gn, gn_sib, dn, hn),
        limit=24,
        scratch=[
            pltpu.VMEM((3, units, width), BF16),
            pltpu.SemaphoreType.DMA((3, across)),
        ],
        in_hbm=1,
    )

    d_tokens, d_gates = call(
        functools.partial(final_kernel, half),
        "combine_gradients",
        [dense, pair],
        [],
        near_masks,
        part,
        d_gates_near,
        *back_near,
        after=[finished],
    )
    return (student, d_tokens, d_gates.T, weight_grads.transpose(1, 0, 2)[None])


def solution(mesh):
    rows = P(("groups", "expert", "dp"), None)
    return jax.shard_map(
        local,
        mesh=mesh,
        in_specs=(rows, rows, rows, rows, P("expert", "dp", None, None)),
        out_specs=(rows, rows, rows, P(("groups", "expert"), "dp", None, None)),
        check_vma=False,
    )
```

```python
import functools

import jax
import jax.numpy as jnp
from jax import lax
from jax.experimental import pallas as pl
from jax.experimental.pallas import tpu as pltpu
from jax.sharding import PartitionSpec as P

PLAIN = (((1,), (0,)), ((), ()))
LAST = (((1,), (1,)), ((), ()))
FIRST = (((0,), (0,)), ((), ()))
MIB = 1024 * 1024
F32 = jnp.float32
BF16 = jnp.bfloat16
FLOPS = {
    "pack_near": 30000000000,
    "pack_far": 30000000000,
    "forward_near": 100000000,
    "forward_far": 3000000000,
    "near_sum": 30000000000,
    "far_grad": 10000000000,
    "near_grad": 30000000000,
    "backward_far": 3000000000,
    "backward_near": 10000000000,
    "far_back": 10000000000,
    "weight_near": 30000000000,
    "combine_gradients": 30000000000,
    "order_rest": 30000000000,
    "order_back": 30000000000,
    "order_return": 0,
    "weight_far": 2400000000,
}


def dot(a, b, dims=PLAIN):
    return lax.dot_general(a, b, dims, preferred_element_type=F32)


def slot_masks(me, meta, pieces, capacity):
    tok = meta.shape[1]
    expert_of = (lax.broadcasted_iota(jnp.int32, (pieces, tok), 0) ^ me).astype(F32)
    first, second = meta[0:1, :] == expert_of, meta[1:2, :] == expert_of
    chosen = jnp.where(first | second, 1.0, 0.0).astype(BF16)
    before = lax.broadcasted_iota(jnp.int32, (tok, tok), 0) < lax.broadcasted_iota(
        jnp.int32, (tok, tok), 1
    )
    rank = dot(chosen, jnp.where(before, 1.0, 0.0).astype(BF16))
    rank0 = jnp.where(first, rank, -1.0)
    rank1 = jnp.where(second, rank, -1.0)
    place = lax.broadcasted_iota(jnp.int32, (capacity, tok), 0).astype(F32)

    def expand(ranks):
        return jnp.concatenate(
            [
                jnp.where(ranks[s : s + 1, :] == place, 1.0, 0.0).astype(BF16)
                for s in range(pieces)
            ],
            axis=0,
        )

    return expand(rank0), expand(rank1)


def put(refs, rows):
    capacity = refs[0].shape[0]
    for s, ref in enumerate(refs):
        ref[...] = rows[s * capacity : (s + 1) * capacity].astype(ref.dtype)


def put_columns(ref, rows):
    side = rows.shape[0]
    for i in range(rows.shape[1] // side):
        ref[i] = rows[:, i * side : (i + 1) * side]


def put_rows(ref, first, value):
    side = value.shape[1]
    for i in range(value.shape[0] // side):
        ref[first + i] = value[i * side : (i + 1) * side, :]


def get_columns(ref):
    return jnp.concatenate([ref[i] for i in range(ref.shape[0])], axis=1)


def get(refs):
    refs = refs[:1] + refs[:0:-1]
    return jnp.concatenate([ref[...] for ref in refs], axis=0)


def keep_masks(masks_ref, meta, refs):
    m0, m1 = slot_masks(lax.axis_index("expert"), meta, len(refs), refs[0].shape[0])
    masks_ref[0] = m0
    masks_ref[1] = m1
    return m0 + m1


def gate_columns(meta):
    columns = meta.T
    return columns[:, 2:3], columns[:, 3:4]


def route_sums(meta, masks_ref, refs):
    m0, m1 = masks_ref[0], masks_ref[1]
    got = get(refs)
    g0, g1 = gate_columns(meta)
    o0, o1 = dot(m0, got, FIRST), dot(m1, got, FIRST)
    return m0, m1, g0, g1, o0, o1, g0 * o0 + g1 * o1


def d_gates_of(diff, o0, o1):
    tok = diff.shape[0]
    lane = lax.broadcasted_iota(jnp.int32, (tok, 128), 1)
    d0 = jnp.sum(diff * o0, axis=1, keepdims=True)
    d1 = jnp.sum(diff * o1, axis=1, keepdims=True)
    return jnp.where(lane == 0, d0, jnp.where(lane == 1, d1, 0.0)).T[0:2, :]


def put_route_grads(refs, m0, m1, g0, g1, diff):
    grads = jnp.concatenate([(g0 * diff).astype(BF16), (g1 * diff).astype(BF16)], axis=0)
    put(refs, dot(jnp.concatenate([m0, m1], axis=1), grads))


def pack_near_kernel(
    own_ref, routes_ref, gates_ref, tokens_ref, meta_ref, masks_ref, *rows_refs
):
    del own_ref
    meta = jnp.concatenate(
        [
            routes_ref[...].astype(F32),
            gates_ref[...],
            jnp.zeros((4, routes_ref.shape[1]), F32),
        ],
        axis=0,
    )
    meta_ref[...] = meta
    put(rows_refs, dot(keep_masks(masks_ref, meta, rows_refs), tokens_ref[...]))


def pack_far_kernel(meta_ref, tokens_ref, masks_ref, *rows_refs):
    put(rows_refs, dot(keep_masks(masks_ref, meta_ref[...], rows_refs), tokens_ref[...]))


def forward_kernel(pieces, own_ref, other_ref, *refs):
    ins, outs, refs = refs[:pieces], refs[pieces : 2 * pieces], refs[2 * pieces :]
    sent_ref, hid_own_ref, fa_ref, fb_ref = refs
    x = get(ins)
    put_columns(sent_ref, x)
    units, width = other_ref.shape[1:]
    halves = ((own_ref, 0), (other_ref, units))
    products = [dot(w_ref[0:2].reshape(2 * units, width), x, LAST) for w_ref, _ in halves]
    total = None
    for (w_ref, first), both in zip(halves, products):
        gate, up = both[:units], both[units:]
        sig = 0.5 * jnp.tanh(0.5 * gate) + 0.5
        silu = gate * sig
        hidden = (silu * up).astype(BF16)
        fa_ref[first : first + units, :] = (up * (sig + silu * (1.0 - sig))).astype(BF16)
        fb_ref[first : first + units, :] = silu.astype(BF16)
        if w_ref is own_ref:
            hid_own_ref[...] = hidden
        else:
            put_rows(sent_ref, width // x.shape[0], hidden)
        out = dot(hidden, w_ref[2], FIRST)
        total = out if total is None else total + out
    put(outs, total)


def backward_kernel(pieces, own_ref, other_ref, fa_ref, fb_ref, *refs):
    ins, outs, refs = refs[:pieces], refs[pieces : 2 * pieces], refs[2 * pieces :]
    sent_ref, dgu_own_ref = refs
    rg = get(ins)
    put_columns(sent_ref, rg)
    units, width = own_ref.shape[1:]
    halves = ((own_ref, 0), (other_ref, units))
    products = [dot(w_ref[2], rg, LAST) for w_ref, _ in halves]
    total = None
    for (w_ref, first), dh in zip(halves, products):
        at = slice(first, first + units)
        dg = (dh * fa_ref[at, :].astype(F32)).astype(BF16)
        du = (dh * fb_ref[at, :].astype(F32)).astype(BF16)
        dgu = jnp.concatenate([dg, du], axis=0)
        if w_ref is own_ref:
            dgu_own_ref[...] = dgu
        else:
            put_rows(sent_ref, width // rg.shape[0], dgu)
        out = dot(dgu, w_ref[0:2].reshape(2 * units, width), FIRST)
        total = out if total is None else total + out
    put(outs, total)


def near_sum_kernel(meta_ref, masks_ref, teacher_ref, *refs):
    ins, out_ref = refs[:-1], refs[-1]
    total = route_sums(meta_ref[...], masks_ref, ins)[-1]
    out_ref[...] = (total - teacher_ref[...].astype(F32)).astype(BF16)


def far_grad_kernel(pieces, meta_ref, masks_ref, rest_ref, *refs):
    ins, part_ref, outs = refs[:pieces], refs[pieces], refs[pieces + 1 :]
    m0, m1, g0, g1, o0, o1, total = route_sums(meta_ref[...], masks_ref, ins)
    tok = total.shape[0]
    part_ref[:tok, :] = total.astype(BF16)
    diff = total + rest_ref[...].astype(F32)
    put_route_grads(outs, m0, m1, g0, g1, diff)
    value = d_gates_of(diff, o0, o1)
    high = value.astype(BF16)
    low = (value - high.astype(F32)).astype(BF16)
    rest = jnp.zeros((part_ref.shape[0] - tok - 4, tok), BF16)
    part_ref[tok:, :tok] = jnp.concatenate([high, low, rest], axis=0)
    part_ref[tok:, tok:] = jnp.zeros((part_ref.shape[0] - tok, part_ref.shape[1] - tok), BF16)


def near_grad_kernel(pieces, meta_ref, masks_ref, teacher_ref, part_ref, *refs):
    ins, student_ref, d_gates_ref, outs = (
        refs[:pieces],
        refs[pieces],
        refs[pieces + 1],
        refs[pieces + 2 :],
    )
    m0, m1, g0, g1, o0, o1, total = route_sums(meta_ref[...], masks_ref, ins)
    tok = total.shape[0]
    total = total + part_ref[:tok, :].astype(F32)
    student_ref[...] = total.astype(BF16)
    diff = total - teacher_ref[...].astype(F32)
    put_route_grads(outs, m0, m1, g0, g1, diff)
    far = part_ref[tok:, :tok].astype(F32)
    d_gates_ref[...] = d_gates_of(diff, o0, o1) + (far[0:2] + far[2:4])


def far_back_kernel(masks_ref, *refs):
    ins, out_ref = refs[:-1], refs[-1]
    out_ref[...] = dot(masks_ref[0] + masks_ref[1], get(ins), FIRST).astype(BF16)


def final_kernel(masks_ref, part_ref, *refs):
    ins, out_ref = refs[:-1], refs[-1]
    total = dot(masks_ref[0] + masks_ref[1], get(ins), FIRST) + part_ref[...].astype(F32)
    out_ref[...] = total.astype(BF16)


def weight_blocks(across, x, sent_x, g, sent_g, d, h):
    units, side = h.shape

    def acts(own, sent, first):
        blocks = range(across + first // side, across + (first + units) // side)
        theirs = jnp.concatenate([sent[i] for i in blocks], axis=0)
        return jnp.concatenate([own[first : first + units, :], theirs], axis=1)

    for row, own, sent, rows, first in (
        (2, h, sent_x, (g, sent_g), 0),
        (0, d, sent_g, (x, sent_x), 0),
        (1, d, sent_g, (x, sent_x), units),
    ):
        for i in range(across):
            column = jnp.concatenate([r[i] for r in rows], axis=0)
            yield row, i, dot(acts(own, sent, first), column)


def weight_far_kernel(across, x, sent_x, g, sent_g, d, h, out_ref, tiny_ref):
    tiny_ref[...] = jnp.zeros_like(tiny_ref)
    side = h.shape[1]
    for row, i, value in weight_blocks(across, x, sent_x, g, sent_g, d, h):
        out_ref[row, :, i * side : (i + 1) * side] = value.astype(BF16)


def weight_near_kernel(
    across, far_ref, x, sent_x, g, sent_g, d, h, out_hbm, tiny_ref, buf, sems
):
    tiny_ref[...] = jnp.zeros_like(tiny_ref)
    side = h.shape[1]
    copies = []
    for row, i, value in weight_blocks(across, x, sent_x, g, sent_g, d, h):
        at = pl.ds(i * side, side)
        buf[row, :, at] = (value + far_ref[row, :, at].astype(F32)).astype(BF16)
        copies.append(
            pltpu.make_async_copy(buf.at[row, :, at], out_hbm.at[row, :, at], sems.at[row, i])
        )
        copies[-1].start()
    for copy in copies:
        copy.wait()


def order_kernel():
    pass


def local(tokens, teacher, routes, gate_weights, weights):
    tok, width = tokens.shape
    experts = lax.axis_size("expert")
    half = experts // 2
    capacity = 4 * tok // experts
    rows = half * capacity
    units = weights.shape[1]

    pieces = [jax.ShapeDtypeStruct((capacity, width), BF16)] * half
    dense = jax.ShapeDtypeStruct((tok, width), BF16)
    longer = jax.ShapeDtypeStruct((tok + 16, width), BF16)
    pair = jax.ShapeDtypeStruct((2, tok), F32)
    acts = jax.ShapeDtypeStruct((units, rows), BF16)
    across, along = width // rows, units // rows
    sent_x = jax.ShapeDtypeStruct((across + along, rows, rows), BF16)
    sent_g = jax.ShapeDtypeStruct((across + 2 * along, rows, rows), BF16)
    acts2 = jax.ShapeDtypeStruct((2 * units, rows), BF16)
    tiny = jax.ShapeDtypeStruct((8, 128), F32)
    masks = jax.ShapeDtypeStruct((2, rows, tok), BF16)
    vspec = pl.BlockSpec(memory_space=pltpu.VMEM)
    aspec = pl.BlockSpec(memory_space=pl.ANY)

    def call(
        kernel,
        name,
        out_shape,
        specs,
        *args,
        after=(),
        through=(),
        limit=8,
        scratch=(),
        in_hbm=0,
    ):
        many = isinstance(out_shape, list)
        specs = list(specs) + [vspec] * (len(args) - len(specs))
        inputs = len(args) + len(after) + len(through)
        outputs = len(out_shape) if many else 1

        def body(*refs):
            kernel(
                *refs[: len(args)],
                *refs[inputs : inputs + outputs],
                *refs[inputs + outputs + len(through) :],
            )

        out_specs = [aspec] * in_hbm + [vspec] * (outputs - in_hbm) + [aspec] * len(through)
        out_shapes = (out_shape if many else [out_shape]) + [
            jax.ShapeDtypeStruct(a.shape, a.dtype) for a in through
        ]
        single = not many and not through
        return pl.pallas_call(
            body,
            in_specs=specs + [aspec] * (len(after) + len(through)),
            out_specs=out_specs[0] if single else out_specs,
            out_shape=out_shapes[0] if single else out_shapes,
            input_output_aliases={
                len(args) + len(after) + i: outputs + i for i in range(len(through))
            },
            scratch_shapes=scratch,
            cost_estimate=pl.CostEstimate(
                flops=FLOPS.get(name, 10**8), bytes_accessed=2 * MIB, transcendentals=0
            ),
            compiler_params=pltpu.CompilerParams(vmem_limit_bytes=limit * MIB),
            name=name,
        )(*args, *after, *through)

    def within_half(rows_of):
        return [rows_of[0]] + [
            lax.ppermute(rows_of[s], "expert", [(i, i ^ s) for i in range(experts)])
            for s in range(half - 1, 0, -1)
        ]

    def to_mirror(x):
        return lax.ppermute(x, "expert", [(i, i ^ half) for i in range(experts)])

    def to_sibling(x):
        return lax.ppermute(x, "dp", [(0, 1), (1, 0)])

    far_tokens = to_mirror(tokens)
    own = weights[0].transpose(1, 0, 2)
    other = to_sibling(own)

    def forward(x_pieces, name, after=()):
        res = call(
            functools.partial(forward_kernel, half),
            name,
            pieces + [sent_x, acts, acts2, acts2],
            [],
            own,
            other,
            *x_pieces,
            after=after,
            limit=20,
        )
        return res[:half], res[half:]

    def backward(rg_pieces, fa, fb, name, after=(), through=()):
        res = call(
            functools.partial(backward_kernel, half),
            name,
            pieces + [sent_g, acts2],
            [],
            own,
            other,
            fa,
            fb,
            *rg_pieces,
            after=after,
            through=through,
            limit=20,
        )
        return res[:half], res[half:]

    res = call(
        pack_near_kernel,
        "pack_near",
        [jax.ShapeDtypeStruct((8, tok), F32), masks] + pieces,
        [],
        own,
        routes.T,
        gate_weights.T,
        tokens,
        limit=10,
    )
    meta, near_masks, x_near = res[0], res[1], within_half(res[2:])
    far_meta = to_mirror(meta)
    res = call(pack_far_kernel, "pack_far", [masks] + pieces, [], far_meta, far_tokens)
    far_masks, x_far = res[0], within_half(res[1:])

    out_near, (xn, hn, fan, fbn) = forward(x_near, "forward_near")
    got_near = within_half(out_near)
    out_far, (xf, hf, faf, fbf) = forward(x_far, "forward_far", after=[xn])
    rest_rows, *out_far = call(
        near_sum_kernel,
        "near_sum",
        dense,
        [],
        meta,
        near_masks,
        teacher,
        *got_near,
        through=out_far,
    )
    rest = to_mirror(rest_rows)
    xf_sib, xn_sib = to_sibling(xf), to_sibling(xn)
    out_far = call(order_kernel, "order_return", [], [], after=[xn_sib], through=out_far)
    (rest,) = call(order_kernel, "order_rest", [], [], after=out_far[:1], through=[rest])
    got_far = within_half(out_far)

    res = call(
        functools.partial(far_grad_kernel, half),
        "far_grad",
        [longer] + pieces,
        [],
        far_meta,
        far_masks,
        rest,
        *got_far,
        after=[xf_sib, xn_sib],
    )
    part, rg_far = to_mirror(res[0]), within_half(res[1:])
    grad_far, (gf, df) = backward(rg_far, faf, fbf, "backward_far")
    res = call(
        functools.partial(near_grad_kernel, half),
        "near_grad",
        [dense, pair] + pieces,
        [],
        meta,
        near_masks,
        teacher,
        part,
        *got_near,
        after=[df],
    )
    student, d_gates, rg_near = res[0], res[1], within_half(res[2:])

    back_far = within_half(grad_far)
    gf_sib = to_sibling(gf)
    part_rows = call(
        far_back_kernel, "far_back", dense, [], far_masks, *back_far, after=[rg_near[0]]
    )
    part = to_mirror(part_rows)
    far_weights, far_done = call(
        functools.partial(weight_far_kernel, across),
        "weight_far",
        [jax.ShapeDtypeStruct((3, units, width), BF16), tiny],
        [],
        *(xf, xf_sib, gf, gf_sib, df, hf),
        after=[part_rows],
        limit=16,
    )
    grad_near, (gn, dn) = backward(rg_near, fan, fbn, "backward_near", after=[part_rows, gf_sib, far_done])
    gn_sib = to_sibling(gn)
    back_near = within_half(grad_near)

    part, dn = call(order_kernel, "order_back", [], [], through=[part, dn])
    weight_grads, finished = call(
        functools.partial(weight_near_kernel, across),
        "weight_near",
        [jax.ShapeDtypeStruct((3, units, width), BF16), tiny],
        [],
        *(far_weights, xn, xn_sib, gn, gn_sib, dn, hn),
        limit=24,
        scratch=[
            pltpu.VMEM((3, units, width), BF16),
            pltpu.SemaphoreType.DMA((3, across)),
        ],
        in_hbm=1,
    )

    d_tokens = call(
        final_kernel,
        "combine_gradients",
        dense,
        [],
        near_masks,
        part,
        *back_near,
        after=[finished],
    )
    return (student, d_tokens, d_gates.T, weight_grads.transpose(1, 0, 2)[None])


def solution(mesh):
    rows = P(("groups", "expert", "dp"), None)
    return jax.shard_map(
        local,
        mesh=mesh,
        in_specs=(rows, rows, rows, rows, P("expert", "dp", None, None)),
        out_specs=(rows, rows, rows, P(("groups", "expert"), "dp", None, None)),
        check_vma=False,
    )
```

```python
import functools

import jax
import jax.numpy as jnp
from jax import lax
from jax.experimental import pallas as pl
from jax.experimental.pallas import tpu as pltpu
from jax.sharding import PartitionSpec as P

PLAIN = (((1,), (0,)), ((), ()))
LAST = (((1,), (1,)), ((), ()))
FIRST = (((0,), (0,)), ((), ()))
MIB = 1024 * 1024
F32 = jnp.float32
BF16 = jnp.bfloat16
FLOPS = {
    "pack_near": 30000000000,
    "pack_far": 30000000000,
    "forward_near": 100000000,
    "forward_far": 3000000000,
    "near_sum": 30000000000,
    "far_grad": 10000000000,
    "near_grad": 30000000000,
    "backward_far": 3000000000,
    "backward_near": 10000000000,
    "far_back": 10000000000,
    "weight_near": 30000000000,
    "combine_gradients": 30000000000,
    "order_rest": 30000000000,
    "order_back": 30000000000,
    "order_return": 0,
    "weight_far": 2400000000,
}


def dot(a, b, dims=PLAIN):
    return lax.dot_general(a, b, dims, preferred_element_type=F32)


def slot_masks(me, meta, pieces, capacity):
    tok = meta.shape[1]
    expert_of = (lax.broadcasted_iota(jnp.int32, (pieces, tok), 0) ^ me).astype(F32)
    first, second = meta[0:1, :] == expert_of, meta[1:2, :] == expert_of
    chosen = jnp.where(first | second, 1.0, 0.0).astype(BF16)
    before = lax.broadcasted_iota(jnp.int32, (tok, tok), 0) < lax.broadcasted_iota(
        jnp.int32, (tok, tok), 1
    )
    rank = dot(chosen, jnp.where(before, 1.0, 0.0).astype(BF16))
    rank0 = jnp.where(first, rank, -1.0)
    rank1 = jnp.where(second, rank, -1.0)
    place = lax.broadcasted_iota(jnp.int32, (capacity, tok), 0).astype(F32)

    def expand(ranks):
        return jnp.concatenate(
            [
                jnp.where(ranks[s : s + 1, :] == place, 1.0, 0.0).astype(BF16)
                for s in range(pieces)
            ],
            axis=0,
        )

    return expand(rank0), expand(rank1)


def put(refs, rows):
    capacity = refs[0].shape[0]
    for s, ref in enumerate(refs):
        ref[...] = rows[s * capacity : (s + 1) * capacity].astype(ref.dtype)


def put_columns(ref, rows):
    side = rows.shape[0]
    for i in range(rows.shape[1] // side):
        ref[i] = rows[:, i * side : (i + 1) * side]


def put_rows(ref, first, value):
    side = value.shape[1]
    for i in range(value.shape[0] // side):
        ref[first + i] = value[i * side : (i + 1) * side, :]


def get_columns(ref):
    return jnp.concatenate([ref[i] for i in range(ref.shape[0])], axis=1)


def get(refs):
    refs = refs[:1] + refs[:0:-1]
    return jnp.concatenate([ref[...] for ref in refs], axis=0)


def keep_masks(masks_ref, meta, refs):
    m0, m1 = slot_masks(lax.axis_index("expert"), meta, len(refs), refs[0].shape[0])
    masks_ref[0] = m0
    masks_ref[1] = m1
    return m0 + m1


def gate_columns(meta):
    columns = meta.T
    return columns[:, 2:3], columns[:, 3:4]


def route_sums(meta, masks_ref, refs):
    m0, m1 = masks_ref[0], masks_ref[1]
    got = get(refs)
    g0, g1 = gate_columns(meta)
    o0, o1 = dot(m0, got, FIRST), dot(m1, got, FIRST)
    return m0, m1, g0, g1, o0, o1, g0 * o0 + g1 * o1


def d_gates_of(diff, o0, o1):
    tok = diff.shape[0]
    lane = lax.broadcasted_iota(jnp.int32, (tok, 128), 1)
    d0 = jnp.sum(diff * o0, axis=1, keepdims=True)
    d1 = jnp.sum(diff * o1, axis=1, keepdims=True)
    return jnp.where(lane == 0, d0, jnp.where(lane == 1, d1, 0.0)).T[0:2, :]


def put_route_grads(refs, m0, m1, g0, g1, diff):
    grads = jnp.concatenate([(g0 * diff).astype(BF16), (g1 * diff).astype(BF16)], axis=0)
    put(refs, dot(jnp.concatenate([m0, m1], axis=1), grads))


def pack_near_kernel(
    routes_ref, gates_ref, tokens_ref, meta_ref, masks_ref, *rows_refs
):
    meta = jnp.concatenate(
        [
            routes_ref[...].astype(F32),
            gates_ref[...],
            jnp.zeros((4, routes_ref.shape[1]), F32),
        ],
        axis=0,
    )
    meta_ref[...] = meta
    put(rows_refs, dot(keep_masks(masks_ref, meta, rows_refs), tokens_ref[...]))


def pack_far_kernel(meta_ref, tokens_ref, masks_ref, *rows_refs):
    put(rows_refs, dot(keep_masks(masks_ref, meta_ref[...], rows_refs), tokens_ref[...]))


def forward_kernel(pieces, own_ref, other_ref, *refs):
    ins, outs, refs = refs[:pieces], refs[pieces : 2 * pieces], refs[2 * pieces :]
    sent_ref, hid_own_ref, fa_ref, fb_ref = refs
    x = get(ins)
    put_columns(sent_ref, x)
    units, width = other_ref.shape[1:]
    halves = ((own_ref, 0), (other_ref, units))
    products = [dot(w_ref[0:2].reshape(2 * units, width), x, LAST) for w_ref, _ in halves]
    total = None
    for (w_ref, first), both in zip(halves, products):
        gate, up = both[:units], both[units:]
        sig = 0.5 * jnp.tanh(0.5 * gate) + 0.5
        silu = gate * sig
        hidden = (silu * up).astype(BF16)
        fa_ref[first : first + units, :] = (up * (sig + silu * (1.0 - sig))).astype(BF16)
        fb_ref[first : first + units, :] = silu.astype(BF16)
        if w_ref is own_ref:
            hid_own_ref[...] = hidden
        else:
            put_rows(sent_ref, width // x.shape[0], hidden)
        out = dot(hidden, w_ref[2], FIRST)
        total = out if total is None else total + out
    put(outs, total)


def backward_kernel(pieces, own_ref, other_ref, fa_ref, fb_ref, *refs):
    ins, outs, refs = refs[:pieces], refs[pieces : 2 * pieces], refs[2 * pieces :]
    sent_ref, dgu_own_ref = refs
    rg = get(ins)
    put_columns(sent_ref, rg)
    units, width = own_ref.shape[1:]
    halves = ((own_ref, 0), (other_ref, units))
    products = [dot(w_ref[2], rg, LAST) for w_ref, _ in halves]
    total = None
    for (w_ref, first), dh in zip(halves, products):
        at = slice(first, first + units)
        dg = (dh * fa_ref[at, :].astype(F32)).astype(BF16)
        du = (dh * fb_ref[at, :].astype(F32)).astype(BF16)
        dgu = jnp.concatenate([dg, du], axis=0)
        if w_ref is own_ref:
            dgu_own_ref[...] = dgu
        else:
            put_rows(sent_ref, width // rg.shape[0], dgu)
        out = dot(dgu, w_ref[0:2].reshape(2 * units, width), FIRST)
        total = out if total is None else total + out
    put(outs, total)


def near_sum_kernel(meta_ref, masks_ref, teacher_ref, *refs):
    ins, out_ref = refs[:-1], refs[-1]
    total = route_sums(meta_ref[...], masks_ref, ins)[-1]
    out_ref[...] = (total - teacher_ref[...].astype(F32)).astype(BF16)


def far_grad_kernel(pieces, meta_ref, masks_ref, rest_ref, *refs):
    ins, part_ref, outs = refs[:pieces], refs[pieces], refs[pieces + 1 :]
    m0, m1, g0, g1, o0, o1, total = route_sums(meta_ref[...], masks_ref, ins)
    tok = total.shape[0]
    part_ref[:tok, :] = total.astype(BF16)
    diff = total + rest_ref[...].astype(F32)
    put_route_grads(outs, m0, m1, g0, g1, diff)
    value = d_gates_of(diff, o0, o1)
    high = value.astype(BF16)
    low = (value - high.astype(F32)).astype(BF16)
    rest = jnp.zeros((part_ref.shape[0] - tok - 4, tok), BF16)
    part_ref[tok:, :tok] = jnp.concatenate([high, low, rest], axis=0)
    part_ref[tok:, tok:] = jnp.zeros((part_ref.shape[0] - tok, part_ref.shape[1] - tok), BF16)


def near_grad_kernel(pieces, meta_ref, masks_ref, teacher_ref, part_ref, *refs):
    ins, student_ref, d_gates_ref, outs = (
        refs[:pieces],
        refs[pieces],
        refs[pieces + 1],
        refs[pieces + 2 :],
    )
    m0, m1, g0, g1, o0, o1, total = route_sums(meta_ref[...], masks_ref, ins)
    tok = total.shape[0]
    total = total + part_ref[:tok, :].astype(F32)
    student_ref[...] = total.astype(BF16)
    diff = total - teacher_ref[...].astype(F32)
    put_route_grads(outs, m0, m1, g0, g1, diff)
    far = part_ref[tok:, :tok].astype(F32)
    d_gates_ref[...] = d_gates_of(diff, o0, o1) + (far[0:2] + far[2:4])


def far_back_kernel(masks_ref, *refs):
    ins, out_ref = refs[:-1], refs[-1]
    out_ref[...] = dot(masks_ref[0] + masks_ref[1], get(ins), FIRST).astype(BF16)


def final_kernel(masks_ref, part_ref, *refs):
    ins, out_ref = refs[:-1], refs[-1]
    total = dot(masks_ref[0] + masks_ref[1], get(ins), FIRST) + part_ref[...].astype(F32)
    out_ref[...] = total.astype(BF16)


def weight_blocks(across, x, sent_x, g, sent_g, d, h):
    units, side = h.shape

    def acts(own, sent, first):
        blocks = range(across + first // side, across + (first + units) // side)
        theirs = jnp.concatenate([sent[i] for i in blocks], axis=0)
        return jnp.concatenate([own[first : first + units, :], theirs], axis=1)

    for row, own, sent, rows, first in (
        (2, h, sent_x, (g, sent_g), 0),
        (0, d, sent_g, (x, sent_x), 0),
        (1, d, sent_g, (x, sent_x), units),
    ):
        for i in range(across):
            column = jnp.concatenate([r[i] for r in rows], axis=0)
            yield row, i, dot(acts(own, sent, first), column)


def weight_far_kernel(across, x, sent_x, g, sent_g, d, h, out_ref, tiny_ref):
    tiny_ref[...] = jnp.zeros_like(tiny_ref)
    side = h.shape[1]
    for row, i, value in weight_blocks(across, x, sent_x, g, sent_g, d, h):
        out_ref[row, :, i * side : (i + 1) * side] = value.astype(BF16)


def weight_near_kernel(
    across, far_ref, x, sent_x, g, sent_g, d, h, out_hbm, tiny_ref, buf, sems
):
    tiny_ref[...] = jnp.zeros_like(tiny_ref)
    side = h.shape[1]
    copies = []
    for row, i, value in weight_blocks(across, x, sent_x, g, sent_g, d, h):
        at = pl.ds(i * side, side)
        buf[row, :, at] = (value + far_ref[row, :, at].astype(F32)).astype(BF16)
        copies.append(
            pltpu.make_async_copy(buf.at[row, :, at], out_hbm.at[row, :, at], sems.at[row, i])
        )
        copies[-1].start()
    for copy in copies:
        copy.wait()


def order_kernel():
    pass


def local(tokens, teacher, routes, gate_weights, weights):
    tok, width = tokens.shape
    experts = lax.axis_size("expert")
    half = experts // 2
    capacity = 4 * tok // experts
    rows = half * capacity
    units = weights.shape[1]

    pieces = [jax.ShapeDtypeStruct((capacity, width), BF16)] * half
    dense = jax.ShapeDtypeStruct((tok, width), BF16)
    longer = jax.ShapeDtypeStruct((tok + 16, width), BF16)
    pair = jax.ShapeDtypeStruct((2, tok), F32)
    acts = jax.ShapeDtypeStruct((units, rows), BF16)
    across, along = width // rows, units // rows
    sent_x = jax.ShapeDtypeStruct((across + along, rows, rows), BF16)
    sent_g = jax.ShapeDtypeStruct((across + 2 * along, rows, rows), BF16)
    acts2 = jax.ShapeDtypeStruct((2 * units, rows), BF16)
    tiny = jax.ShapeDtypeStruct((8, 128), F32)
    masks = jax.ShapeDtypeStruct((2, rows, tok), BF16)
    vspec = pl.BlockSpec(memory_space=pltpu.VMEM)
    aspec = pl.BlockSpec(memory_space=pl.ANY)

    def call(
        kernel,
        name,
        out_shape,
        specs,
        *args,
        after=(),
        through=(),
        limit=8,
        scratch=(),
        in_hbm=0,
    ):
        many = isinstance(out_shape, list)
        specs = list(specs) + [vspec] * (len(args) - len(specs))
        inputs = len(args) + len(after) + len(through)
        outputs = len(out_shape) if many else 1

        def body(*refs):
            kernel(
                *refs[: len(args)],
                *refs[inputs : inputs + outputs],
                *refs[inputs + outputs + len(through) :],
            )

        out_specs = [aspec] * in_hbm + [vspec] * (outputs - in_hbm) + [aspec] * len(through)
        out_shapes = (out_shape if many else [out_shape]) + [
            jax.ShapeDtypeStruct(a.shape, a.dtype) for a in through
        ]
        single = not many and not through
        return pl.pallas_call(
            body,
            in_specs=specs + [aspec] * (len(after) + len(through)),
            out_specs=out_specs[0] if single else out_specs,
            out_shape=out_shapes[0] if single else out_shapes,
            input_output_aliases={
                len(args) + len(after) + i: outputs + i for i in range(len(through))
            },
            scratch_shapes=scratch,
            cost_estimate=pl.CostEstimate(
                flops=FLOPS.get(name, 10**8), bytes_accessed=2 * MIB, transcendentals=0
            ),
            compiler_params=pltpu.CompilerParams(vmem_limit_bytes=limit * MIB),
            name=name,
        )(*args, *after, *through)

    def within_half(rows_of):
        return [rows_of[0]] + [
            lax.ppermute(rows_of[s], "expert", [(i, i ^ s) for i in range(experts)])
            for s in range(half - 1, 0, -1)
        ]

    def to_mirror(x):
        return lax.ppermute(x, "expert", [(i, i ^ half) for i in range(experts)])

    def to_sibling(x):
        return lax.ppermute(x, "dp", [(0, 1), (1, 0)])

    far_tokens = to_mirror(tokens)
    own = weights[0].transpose(1, 0, 2)
    other = to_sibling(own)

    def forward(x_pieces, name, after=()):
        res = call(
            functools.partial(forward_kernel, half),
            name,
            pieces + [sent_x, acts, acts2, acts2],
            [],
            own,
            other,
            *x_pieces,
            after=after,
            limit=20,
        )
        return res[:half], res[half:]

    def backward(rg_pieces, fa, fb, name, after=(), through=()):
        res = call(
            functools.partial(backward_kernel, half),
            name,
            pieces + [sent_g, acts2],
            [],
            own,
            other,
            fa,
            fb,
            *rg_pieces,
            after=after,
            through=through,
            limit=20,
        )
        return res[:half], res[half:]

    res = call(
        pack_near_kernel,
        "pack_near",
        [jax.ShapeDtypeStruct((8, tok), F32), masks] + pieces,
        [],
        routes.T,
        gate_weights.T,
        tokens,
        limit=10,
    )
    meta, near_masks, x_near = res[0], res[1], within_half(res[2:])
    far_meta = to_mirror(meta)
    res = call(pack_far_kernel, "pack_far", [masks] + pieces, [], far_meta, far_tokens)
    far_masks, x_far = res[0], within_half(res[1:])

    out_near, (xn, hn, fan, fbn) = forward(x_near, "forward_near")
    got_near = within_half(out_near)
    out_far, (xf, hf, faf, fbf) = forward(x_far, "forward_far", after=[xn])
    rest_rows, *out_far = call(
        near_sum_kernel,
        "near_sum",
        dense,
        [],
        meta,
        near_masks,
        teacher,
        *got_near,
        through=out_far,
    )
    rest = to_mirror(rest_rows)
    xf_sib, xn_sib = to_sibling(xf), to_sibling(xn)
    out_far = call(order_kernel, "order_return", [], [], after=[xn_sib], through=out_far)
    (rest,) = call(order_kernel, "order_rest", [], [], after=out_far[:1], through=[rest])
    got_far = within_half(out_far)

    res = call(
        functools.partial(far_grad_kernel, half),
        "far_grad",
        [longer] + pieces,
        [],
        far_meta,
        far_masks,
        rest,
        *got_far,
        after=[xf_sib, xn_sib],
    )
    part, rg_far = to_mirror(res[0]), within_half(res[1:])
    grad_far, (gf, df) = backward(rg_far, faf, fbf, "backward_far")
    res = call(
        functools.partial(near_grad_kernel, half),
        "near_grad",
        [dense, pair] + pieces,
        [],
        meta,
        near_masks,
        teacher,
        part,
        *got_near,
        after=[df],
    )
    student, d_gates, rg_near = res[0], res[1], within_half(res[2:])

    back_far = within_half(grad_far)
    gf_sib = to_sibling(gf)
    part_rows = call(
        far_back_kernel, "far_back", dense, [], far_masks, *back_far, after=[rg_near[0]]
    )
    part = to_mirror(part_rows)
    far_weights, far_done = call(
        functools.partial(weight_far_kernel, across),
        "weight_far",
        [jax.ShapeDtypeStruct((3, units, width), BF16), tiny],
        [],
        *(xf, xf_sib, gf, gf_sib, df, hf),
        after=[part_rows],
        limit=16,
    )
    grad_near, (gn, dn) = backward(rg_near, fan, fbn, "backward_near", after=[part_rows, gf_sib, far_done])
    gn_sib = to_sibling(gn)
    back_near = within_half(grad_near)

    part, dn = call(order_kernel, "order_back", [], [], through=[part, dn])
    weight_grads, finished = call(
        functools.partial(weight_near_kernel, across),
        "weight_near",
        [jax.ShapeDtypeStruct((3, units, width), BF16), tiny],
        [],
        *(far_weights, xn, xn_sib, gn, gn_sib, dn, hn),
        limit=24,
        scratch=[
            pltpu.VMEM((3, units, width), BF16),
            pltpu.SemaphoreType.DMA((3, across)),
        ],
        in_hbm=1,
    )

    d_tokens = call(
        final_kernel,
        "combine_gradients",
        dense,
        [],
        near_masks,
        part,
        *back_near,
        after=[finished],
    )
    return (student, d_tokens, d_gates.T, weight_grads.transpose(1, 0, 2)[None])


def solution(mesh):
    rows = P(("groups", "expert", "dp"), None)
    return jax.shard_map(
        local,
        mesh=mesh,
        in_specs=(rows, rows, rows, rows, P("expert", "dp", None, None)),
        out_specs=(rows, rows, rows, P(("groups", "expert"), "dp", None, None)),
        check_vma=False,
    )
```

```python
import functools

import jax
import jax.numpy as jnp
from jax import lax
from jax.experimental import pallas as pl
from jax.experimental.pallas import tpu as pltpu
from jax.sharding import PartitionSpec as P

PLAIN = (((1,), (0,)), ((), ()))
LAST = (((1,), (1,)), ((), ()))
FIRST = (((0,), (0,)), ((), ()))
MIB = 1024 * 1024
F32 = jnp.float32
BF16 = jnp.bfloat16
FLOPS = {
    "pack_near": 30000000000,
    "pack_far": 30000000000,
    "forward_near": 100000000,
    "forward_far": 3000000000,
    "near_sum": 30000000000,
    "far_grad": 10000000000,
    "near_grad": 30000000000,
    "backward_far": 3000000000,
    "backward_near": 10000000000,
    "far_back": 10000000000,
    "weight_near": 30000000000,
    "combine_gradients": 30000000000,
    "order_rest": 30000000000,
    "order_back": 30000000000,
    "order_return": 0,
    "weight_far": 2400000000,
}


def dot(a, b, dims=PLAIN):
    return lax.dot_general(a, b, dims, preferred_element_type=F32)


def slot_masks(me, meta, pieces, capacity):
    tok = meta.shape[1]
    expert_of = (lax.broadcasted_iota(jnp.int32, (pieces, tok), 0) ^ me).astype(F32)
    first, second = meta[0:1, :] == expert_of, meta[1:2, :] == expert_of
    chosen = jnp.where(first | second, 1.0, 0.0).astype(BF16)
    before = lax.broadcasted_iota(jnp.int32, (tok, tok), 0) < lax.broadcasted_iota(
        jnp.int32, (tok, tok), 1
    )
    rank = dot(chosen, jnp.where(before, 1.0, 0.0).astype(BF16))
    rank0 = jnp.where(first, rank, -1.0)
    rank1 = jnp.where(second, rank, -1.0)
    place = lax.broadcasted_iota(jnp.int32, (capacity, tok), 0).astype(F32)

    def expand(ranks):
        return jnp.concatenate(
            [
                jnp.where(ranks[s : s + 1, :] == place, 1.0, 0.0).astype(BF16)
                for s in range(pieces)
            ],
            axis=0,
        )

    return expand(rank0), expand(rank1)


def put(refs, rows):
    capacity = refs[0].shape[0]
    for s, ref in enumerate(refs):
        ref[...] = rows[s * capacity : (s + 1) * capacity].astype(ref.dtype)


def put_columns(ref, rows):
    side = rows.shape[0]
    for i in range(rows.shape[1] // side):
        ref[i] = rows[:, i * side : (i + 1) * side]


def put_rows(ref, first, value):
    side = value.shape[1]
    for i in range(value.shape[0] // side):
        ref[first + i] = value[i * side : (i + 1) * side, :]


def get_columns(ref):
    return jnp.concatenate([ref[i] for i in range(ref.shape[0])], axis=1)


def get(refs):
    refs = refs[:1] + refs[:0:-1]
    return jnp.concatenate([ref[...] for ref in refs], axis=0)


def keep_masks(masks_ref, meta, refs):
    m0, m1 = slot_masks(lax.axis_index("expert"), meta, len(refs), refs[0].shape[0])
    masks_ref[0] = m0
    masks_ref[1] = m1
    return m0 + m1


def gate_columns(meta):
    columns = meta.T
    return columns[:, 2:3], columns[:, 3:4]


def route_sums(meta, masks_ref, refs):
    m0, m1 = masks_ref[0], masks_ref[1]
    got = get(refs)
    g0, g1 = gate_columns(meta)
    o0, o1 = dot(m0, got, FIRST), dot(m1, got, FIRST)
    return m0, m1, g0, g1, o0, o1, g0 * o0 + g1 * o1


def d_gates_of(diff, o0, o1):
    tok = diff.shape[0]
    lane = lax.broadcasted_iota(jnp.int32, (tok, 128), 1)
    d0 = jnp.sum(diff * o0, axis=1, keepdims=True)
    d1 = jnp.sum(diff * o1, axis=1, keepdims=True)
    return jnp.where(lane == 0, d0, jnp.where(lane == 1, d1, 0.0)).T[0:2, :]


def put_route_grads(refs, m0, m1, g0, g1, diff):
    grads = jnp.concatenate([(g0 * diff).astype(BF16), (g1 * diff).astype(BF16)], axis=0)
    put(refs, dot(jnp.concatenate([m0, m1], axis=1), grads))


def pack_near_kernel(
    routes_ref, gates_ref, tokens_ref, meta_ref, masks_ref, *rows_refs
):
    meta = jnp.concatenate(
        [
            routes_ref[...].astype(F32),
            gates_ref[...],
            jnp.zeros((4, routes_ref.shape[1]), F32),
        ],
        axis=0,
    )
    meta_ref[...] = meta
    put(rows_refs, dot(keep_masks(masks_ref, meta, rows_refs), tokens_ref[...]))


def pack_far_kernel(meta_ref, tokens_ref, masks_ref, *rows_refs):
    put(rows_refs, dot(keep_masks(masks_ref, meta_ref[...], rows_refs), tokens_ref[...]))


def forward_kernel(pieces, own_ref, other_ref, *refs):
    ins, outs, refs = refs[:pieces], refs[pieces : 2 * pieces], refs[2 * pieces :]
    sent_ref, hid_own_ref, fa_ref, fb_ref = refs
    x = get(ins)
    put_columns(sent_ref, x)
    units, width = other_ref.shape[1:]
    halves = ((own_ref, 0), (other_ref, units))
    products = [dot(w_ref[0:2].reshape(2 * units, width), x, LAST) for w_ref, _ in halves]
    total = None
    for (w_ref, first), both in zip(halves, products):
        gate, up = both[:units], both[units:]
        sig = 0.5 * jnp.tanh(0.5 * gate) + 0.5
        silu = gate * sig
        hidden = (silu * up).astype(BF16)
        fa_ref[first : first + units, :] = (up * (sig + silu * (1.0 - sig))).astype(BF16)
        fb_ref[first : first + units, :] = silu.astype(BF16)
        if w_ref is own_ref:
            hid_own_ref[...] = hidden
        else:
            put_rows(sent_ref, width // x.shape[0], hidden)
        out = dot(hidden, w_ref[2], FIRST)
        total = out if total is None else total + out
    put(outs, total)


def backward_kernel(pieces, own_ref, other_ref, fa_ref, fb_ref, *refs):
    ins, outs, refs = refs[:pieces], refs[pieces : 2 * pieces], refs[2 * pieces :]
    sent_ref, dgu_own_ref = refs
    rg = get(ins)
    put_columns(sent_ref, rg)
    units, width = own_ref.shape[1:]
    halves = ((own_ref, 0), (other_ref, units))
    products = [dot(w_ref[2], rg, LAST) for w_ref, _ in halves]
    total = None
    for (w_ref, first), dh in zip(halves, products):
        at = slice(first, first + units)
        dg = (dh * fa_ref[at, :].astype(F32)).astype(BF16)
        du = (dh * fb_ref[at, :].astype(F32)).astype(BF16)
        dgu = jnp.concatenate([dg, du], axis=0)
        if w_ref is own_ref:
            dgu_own_ref[...] = dgu
        else:
            put_rows(sent_ref, width // rg.shape[0], dgu)
        out = dot(dgu, w_ref[0:2].reshape(2 * units, width), FIRST)
        total = out if total is None else total + out
    put(outs, total)


def near_sum_kernel(meta_ref, masks_ref, teacher_ref, *refs):
    ins, out_ref = refs[:-1], refs[-1]
    total = route_sums(meta_ref[...], masks_ref, ins)[-1]
    out_ref[...] = (total - teacher_ref[...].astype(F32)).astype(BF16)


def far_grad_kernel(pieces, meta_ref, masks_ref, rest_ref, *refs):
    ins, part_ref, outs = refs[:pieces], refs[pieces], refs[pieces + 1 :]
    m0, m1, g0, g1, o0, o1, total = route_sums(meta_ref[...], masks_ref, ins)
    tok = total.shape[0]
    part_ref[:tok, :] = total.astype(BF16)
    diff = total + rest_ref[...].astype(F32)
    put_route_grads(outs, m0, m1, g0, g1, diff)
    value = d_gates_of(diff, o0, o1)
    high = value.astype(BF16)
    low = (value - high.astype(F32)).astype(BF16)
    rest = jnp.zeros((part_ref.shape[0] - tok - 4, tok), BF16)
    part_ref[tok:, :tok] = jnp.concatenate([high, low, rest], axis=0)
    part_ref[tok:, tok:] = jnp.zeros((part_ref.shape[0] - tok, part_ref.shape[1] - tok), BF16)


def near_grad_kernel(pieces, meta_ref, masks_ref, teacher_ref, part_ref, *refs):
    ins, student_ref, d_gates_ref, outs = (
        refs[:pieces],
        refs[pieces],
        refs[pieces + 1],
        refs[pieces + 2 :],
    )
    m0, m1, g0, g1, o0, o1, total = route_sums(meta_ref[...], masks_ref, ins)
    tok = total.shape[0]
    total = total + part_ref[:tok, :].astype(F32)
    student_ref[...] = total.astype(BF16)
    diff = total - teacher_ref[...].astype(F32)
    put_route_grads(outs, m0, m1, g0, g1, diff)
    far = part_ref[tok:, :tok].astype(F32)
    d_gates_ref[...] = d_gates_of(diff, o0, o1) + (far[0:2] + far[2:4])


def far_back_kernel(masks_ref, *refs):
    ins, out_ref = refs[:-1], refs[-1]
    out_ref[...] = dot(masks_ref[0] + masks_ref[1], get(ins), FIRST).astype(BF16)


def final_kernel(masks_ref, part_ref, *refs):
    ins, out_ref = refs[:-1], refs[-1]
    got = jnp.concatenate([ref[...] for ref in ins], axis=0)
    total = dot(masks_ref[0] + masks_ref[1], got, FIRST) + part_ref[...].astype(F32)
    out_ref[...] = total.astype(BF16)


def weight_blocks(across, x, sent_x, g, sent_g, d, h):
    units, side = h.shape

    def acts(own, sent, first):
        blocks = range(across + first // side, across + (first + units) // side)
        theirs = jnp.concatenate([sent[i] for i in blocks], axis=0)
        return jnp.concatenate([own[first : first + units, :], theirs], axis=1)

    for row, own, sent, rows, first in (
        (2, h, sent_x, (g, sent_g), 0),
        (0, d, sent_g, (x, sent_x), 0),
        (1, d, sent_g, (x, sent_x), units),
    ):
        for i in range(across):
            column = jnp.concatenate([r[i] for r in rows], axis=0)
            yield row, i, dot(acts(own, sent, first), column)


def weight_far_kernel(across, x, sent_x, g, sent_g, d, h, out_ref, tiny_ref):
    tiny_ref[...] = jnp.zeros_like(tiny_ref)
    side = h.shape[1]
    for row, i, value in weight_blocks(across, x, sent_x, g, sent_g, d, h):
        out_ref[row, :, i * side : (i + 1) * side] = value.astype(BF16)


def weight_near_kernel(
    across, far_ref, x, sent_x, g, sent_g, d, h, out_hbm, tiny_ref, buf, sems
):
    tiny_ref[...] = jnp.zeros_like(tiny_ref)
    side = h.shape[1]
    copies = []
    for row, i, value in weight_blocks(across, x, sent_x, g, sent_g, d, h):
        at = pl.ds(i * side, side)
        buf[row, :, at] = (value + far_ref[row, :, at].astype(F32)).astype(BF16)
        copies.append(
            pltpu.make_async_copy(buf.at[row, :, at], out_hbm.at[row, :, at], sems.at[row, i])
        )
        copies[-1].start()
    for copy in copies:
        copy.wait()


def order_kernel():
    pass


def local(tokens, teacher, routes, gate_weights, weights):
    tok, width = tokens.shape
    experts = lax.axis_size("expert")
    half = experts // 2
    capacity = 4 * tok // experts
    rows = half * capacity
    units = weights.shape[1]

    pieces = [jax.ShapeDtypeStruct((capacity, width), BF16)] * half
    dense = jax.ShapeDtypeStruct((tok, width), BF16)
    longer = jax.ShapeDtypeStruct((tok + 16, width), BF16)
    pair = jax.ShapeDtypeStruct((2, tok), F32)
    acts = jax.ShapeDtypeStruct((units, rows), BF16)
    across, along = width // rows, units // rows
    sent_x = jax.ShapeDtypeStruct((across + along, rows, rows), BF16)
    sent_g = jax.ShapeDtypeStruct((across + 2 * along, rows, rows), BF16)
    acts2 = jax.ShapeDtypeStruct((2 * units, rows), BF16)
    tiny = jax.ShapeDtypeStruct((8, 128), F32)
    masks = jax.ShapeDtypeStruct((2, rows, tok), BF16)
    vspec = pl.BlockSpec(memory_space=pltpu.VMEM)
    aspec = pl.BlockSpec(memory_space=pl.ANY)

    def call(
        kernel,
        name,
        out_shape,
        specs,
        *args,
        after=(),
        through=(),
        limit=8,
        scratch=(),
        in_hbm=0,
    ):
        many = isinstance(out_shape, list)
        specs = list(specs) + [vspec] * (len(args) - len(specs))
        inputs = len(args) + len(after) + len(through)
        outputs = len(out_shape) if many else 1

        def body(*refs):
            kernel(
                *refs[: len(args)],
                *refs[inputs : inputs + outputs],
                *refs[inputs + outputs + len(through) :],
            )

        out_specs = [aspec] * in_hbm + [vspec] * (outputs - in_hbm) + [aspec] * len(through)
        out_shapes = (out_shape if many else [out_shape]) + [
            jax.ShapeDtypeStruct(a.shape, a.dtype) for a in through
        ]
        single = not many and not through
        return pl.pallas_call(
            body,
            in_specs=specs + [aspec] * (len(after) + len(through)),
            out_specs=out_specs[0] if single else out_specs,
            out_shape=out_shapes[0] if single else out_shapes,
            input_output_aliases={
                len(args) + len(after) + i: outputs + i for i in range(len(through))
            },
            scratch_shapes=scratch,
            cost_estimate=pl.CostEstimate(
                flops=FLOPS.get(name, 10**8), bytes_accessed=2 * MIB, transcendentals=0
            ),
            compiler_params=pltpu.CompilerParams(vmem_limit_bytes=limit * MIB),
            name=name,
        )(*args, *after, *through)

    def within_half(rows_of):
        return [rows_of[0]] + [
            lax.ppermute(rows_of[s], "expert", [(i, i ^ s) for i in range(experts)])
            for s in range(half - 1, 0, -1)
        ]

    def to_mirror(x):
        return lax.ppermute(x, "expert", [(i, i ^ half) for i in range(experts)])

    def to_sibling(x):
        return lax.ppermute(x, "dp", [(0, 1), (1, 0)])

    far_tokens = to_mirror(tokens)
    own = weights[0].transpose(1, 0, 2)
    other = to_sibling(own)

    def forward(x_pieces, name, after=()):
        res = call(
            functools.partial(forward_kernel, half),
            name,
            pieces + [sent_x, acts, acts2, acts2],
            [],
            own,
            other,
            *x_pieces,
            after=after,
            limit=20,
        )
        return res[:half], res[half:]

    def backward(rg_pieces, fa, fb, name, after=(), through=()):
        res = call(
            functools.partial(backward_kernel, half),
            name,
            pieces + [sent_g, acts2],
            [],
            own,
            other,
            fa,
            fb,
            *rg_pieces,
            after=after,
            through=through,
            limit=20,
        )
        return res[:half], res[half:]

    res = call(
        pack_near_kernel,
        "pack_near",
        [jax.ShapeDtypeStruct((8, tok), F32), masks] + pieces,
        [],
        routes.T,
        gate_weights.T,
        tokens,
        limit=10,
    )
    meta, near_masks, x_near = res[0], res[1], within_half(res[2:])
    far_meta = to_mirror(meta)
    res = call(pack_far_kernel, "pack_far", [masks] + pieces, [], far_meta, far_tokens)
    far_masks, x_far = res[0], within_half(res[1:])

    out_near, (xn, hn, fan, fbn) = forward(x_near, "forward_near")
    got_near = within_half(out_near)
    out_far, (xf, hf, faf, fbf) = forward(x_far, "forward_far", after=[xn])
    rest_rows, *out_far = call(
        near_sum_kernel,
        "near_sum",
        dense,
        [],
        meta,
        near_masks,
        teacher,
        *got_near,
        through=out_far,
    )
    rest = to_mirror(rest_rows)
    xf_sib, xn_sib = to_sibling(xf), to_sibling(xn)
    out_far = call(order_kernel, "order_return", [], [], after=[xn_sib], through=out_far)
    (rest,) = call(order_kernel, "order_rest", [], [], after=out_far[:1], through=[rest])
    got_far = within_half(out_far)

    res = call(
        functools.partial(far_grad_kernel, half),
        "far_grad",
        [longer] + pieces,
        [],
        far_meta,
        far_masks,
        rest,
        *got_far,
        after=[xf_sib, xn_sib],
    )
    part, rg_far = to_mirror(res[0]), within_half(res[1:])
    grad_far, (gf, df) = backward(rg_far, faf, fbf, "backward_far")
    res = call(
        functools.partial(near_grad_kernel, half),
        "near_grad",
        [dense, pair] + pieces,
        [],
        meta,
        near_masks,
        teacher,
        part,
        *got_near,
        after=[df],
    )
    student, d_gates, rg_near = res[0], res[1], within_half(res[2:])

    back_far = within_half(grad_far)
    gf_sib = to_sibling(gf)
    part_rows = call(
        far_back_kernel, "far_back", dense, [], far_masks, *back_far, after=[rg_near[0]]
    )
    part = to_mirror(part_rows)
    far_weights, far_done = call(
        functools.partial(weight_far_kernel, across),
        "weight_far",
        [jax.ShapeDtypeStruct((3, units, width), BF16), tiny],
        [],
        *(xf, xf_sib, gf, gf_sib, df, hf),
        after=[part_rows],
        limit=16,
    )
    grad_near, (gn, dn) = backward(rg_near, fan, fbn, "backward_near", after=[part_rows, gf_sib, far_done])
    gn_sib = to_sibling(gn)
    back_near = within_half(grad_near)

    part, dn = call(order_kernel, "order_back", [], [], through=[part, dn])
    weight_grads, finished = call(
        functools.partial(weight_near_kernel, across),
        "weight_near",
        [jax.ShapeDtypeStruct((3, units, width), BF16), tiny],
        [],
        *(far_weights, xn, xn_sib, gn, gn_sib, dn, hn),
        limit=24,
        scratch=[
            pltpu.VMEM((3, units, width), BF16),
            pltpu.SemaphoreType.DMA((3, across)),
        ],
        in_hbm=1,
    )

    d_tokens = call(
        final_kernel,
        "combine_gradients",
        dense,
        [],
        near_masks,
        part,
        *(back_near[:1] + back_near[:0:-1]),
        after=[finished],
    )
    return (student, d_tokens, d_gates.T, weight_grads.transpose(1, 0, 2)[None])


def solution(mesh):
    rows = P(("groups", "expert", "dp"), None)
    return jax.shard_map(
        local,
        mesh=mesh,
        in_specs=(rows, rows, rows, rows, P("expert", "dp", None, None)),
        out_specs=(rows, rows, rows, P(("groups", "expert"), "dp", None, None)),
        check_vma=False,
    )
```
